32 devices in a mesh: row: 16 (over z, y, core), col: 2 (over x).
Axes of the slice: x: 2, y: 2, z: 4, core: 2. Of those that a mesh axis runs over, the one named last changes fastest.
Arguments:
- positions: float32 [3, 16, 2, 128], P(None, 'row', 'col'), may hold values from 0 to 12
- species: int32 [16, 2, 128], P('row', 'col'), may hold values from 0 to 5
- counts: int32 [16, 2, 128], P('row', 'col'), may hold values from 32 to 64
- neighbours: int32 [16, 2, 64, 128], P('row', 'col'), may hold values from 0 to 1151
- ghost_index: int32 [16, 2, 8, 128], P('row', 'col'), may hold values from 0 to 127
- wave_numbers: int32 [3, 1000], replicated, may hold values from -6 to 6, as said below
- embedding: float32 [6, 128], replicated, may hold values from -6 to 6
- w_radial: float32 [16, 128], replicated, may hold values from -1.5 to 1.5
- w_mix: float32 [128, 128], replicated, may hold values from -0.5 to 0.5
- w_read: float32 [128, 128], replicated, may hold values from -0.5 to 0.5
- w_out: float32 [128], replicated, may hold values from -0.5 to 0.5
- amplitude: float32 [128], replicated, may hold values from 10 to 100
- kernel_width: float32 [128], replicated, may hold values from 0.5 to 4
- filter_gain: float32 [1000, 128], replicated, may hold values from 0.1 to 1.9
Outputs:
- forces: float32 [3, 16, 2, 128], P(None, 'row', 'col')
- virial: float32 [3, 3], replicated
The draws below stay inside these ranges and needn't reach their ends.
Inputs may be any that keep to these rules, and one draw needn't show every extreme that they name: `wave_numbers`: the first two rows lie in -6 to 6, the third in 1 to 6. `counts`: slots at or beyond an atom's count are padding. `neighbours`: indices into the extended table of step one. `ghost_index`: local atom indices; repeats are allowed.
All inputs are finite; a program needn't handle non-finite values.
Results may differ from the reference program's by a relative error of at most 0.0003.
Values sent between devices are 32-bit elements; how exact they have to be, the bound alone decides.
No kernel may reach another device: no remote copies, remote signals or barrier semaphores. Data moves between devices by JAX's collectives and lax.ppermute only.
A program may use at most 64 MiB of HBM per device.

```python
import math
import jax
import jax.numpy as jnp
from jax import lax

C = 128
K = 1000
NB = 64
NRB = 16
SPEC = 6
KMAX = 6
A_DEV = 128
G_DEV = 128
N_ROW = 16
N_COL = 2


def draw_wave_numbers(key, part):
    plane_numbers = jax.random.randint(jax.random.fold_in(key, 11), (2, K), -KMAX, KMAX + 1)
    height_numbers = jax.random.randint(jax.random.fold_in(key, 12), (1, K), 1, KMAX + 1)
    return jnp.concatenate([plane_numbers, height_numbers], axis=0).astype(jnp.int32)


def touch_ends(values, stream_key, smallest, largest):
    spot = [jax.random.randint(jax.random.fold_in(stream_key, axis), (), 0, length) for axis, length in enumerate(values.shape)]
    longest = values.shape.index(max(values.shape))
    neighbour = spot[:longest] + [(spot[longest] + 1) % values.shape[longest]] + spot[longest + 1:]
    return values.at[tuple(spot)].set(smallest).at[tuple(neighbour)].set(largest)


def shard_levels(key, shape, shards, least, largest):
    def one(dim, parts):
        heights = jax.random.uniform(jax.random.fold_in(jax.random.fold_in(key, 6), dim), (parts,), jnp.float32, least / len(shards), largest / len(shards))
        return jnp.repeat(jnp.exp(heights), shape[dim] // parts).reshape((-1,) + (1,) * (len(shape) - dim - 1))

    factor_of = one(*shards[0])
    for cut in shards[1:]:
        factor_of = factor_of * one(*cut)
    return factor_of


def normal_values(own_key, shape, scale, limit, held_as=jnp.bfloat16):
    values = jax.random.normal(own_key, shape, jnp.float32) * scale
    return jnp.minimum(jnp.maximum(values, -limit), limit).astype(held_as)


def setup_inputs(seed: int = 0) -> dict:
    keys = jax.random.split(jax.random.key(seed), 15)
    return {
        "positions": jnp.clip(12.0 * jax.random.uniform(keys[0], (3, N_ROW, N_COL, A_DEV), jnp.float32) ** shard_levels(keys[0], (3, N_ROW, N_COL, A_DEV), ((1, 16), (2, 2)), -0.2, 0.2), 0.0, 12.0),
        "species": touch_ends(jax.random.randint(keys[1], (N_ROW, N_COL, A_DEV), 0, SPEC), jax.random.fold_in(keys[1], 1), 0, SPEC - 1).astype(jnp.int32),
        "counts": touch_ends(jax.random.randint(keys[2], (N_ROW, N_COL, A_DEV), NB // 2, NB + 1), jax.random.fold_in(keys[2], 1), NB // 2, NB).astype(jnp.int32),
        "neighbours": touch_ends(jax.random.randint(keys[3], (N_ROW, N_COL, NB, A_DEV), 0, A_DEV + 8 * G_DEV), jax.random.fold_in(keys[3], 1), 0, (A_DEV + 8 * G_DEV) - 1).astype(jnp.int32),
        "ghost_index": touch_ends(jax.random.randint(keys[4], (N_ROW, N_COL, 8, G_DEV), 0, A_DEV), jax.random.fold_in(keys[4], 1), 0, A_DEV - 1).astype(jnp.int32),
        "wave_numbers": draw_wave_numbers(jax.random.fold_in(keys[14], 71), 0),
        "embedding": normal_values(keys[6], (SPEC, C), 1.0, 6.0, jnp.float32),
        "w_radial": normal_values(keys[7], (NRB, C), NRB ** -0.5, 1.5, jnp.float32),
        "w_mix": normal_values(keys[8], (C, C), C ** -0.5, 0.5, jnp.float32),
        "w_read": normal_values(keys[9], (C, C), C ** -0.5, 0.5, jnp.float32),
        "w_out": normal_values(keys[10], (C,), C ** -0.5, 0.5, jnp.float32),
        "amplitude": jnp.clip(jnp.exp(jax.random.uniform(keys[11], (C,), jnp.float32, math.log(10.0), math.log(100.0))), 10.0, 100.0),
        "kernel_width": jnp.clip(jnp.exp(jax.random.uniform(keys[12], (C,), jnp.float32, math.log(0.5), math.log(4.0))), 0.5, 4.0),
        "filter_gain": jnp.clip(1.0 + 0.18 * jax.random.normal(keys[13], (K, C), jnp.float32), 0.1, 1.9),
    }


CELL_EDGE = 12.0
HEIGHT = 36.0
EXACT = lax.Precision.HIGHEST
DIRECTIONS = ((-1, -1), (-1, 0), (-1, 1), (0, -1), (0, 1), (1, -1), (1, 0), (1, 1))

def radial_rates(count):
    return 0.003 * jnp.exp(math.log(1.6) * jnp.arange(count, dtype=jnp.int32).astype(jnp.float32))

def block_size(count):
    if count % 125 == 0 and count > 125:
        return 125
    return count

def short_range(edge_vectors, own_kinds, edge_kinds, edge_valid, embedding, w_radial, w_mix, w_read, w_out):
    slot_count, atom_count = edge_valid.shape
    species_count = embedding.shape[0]
    decay_rates = radial_rates(w_radial.shape[0])
    group_size = 4 if slot_count % 4 == 0 else 1
    groups = slot_count // group_size
    vector_groups = jnp.moveaxis(edge_vectors.reshape(3, groups, group_size, atom_count), 1, 0)
    kind_groups = edge_kinds.reshape(groups, group_size, atom_count)
    mask_groups = edge_valid.reshape(groups, group_size, atom_count)
    species_ids = jnp.arange(species_count, dtype=jnp.int32)

    def one_group(running, inputs):
        vectors, neighbour_kinds, edge_mask = inputs
        squared = lax.optimization_barrier(jnp.sum(vectors * vectors, axis=0))
        radial_basis = jnp.exp(-decay_rates[:, None, None] * squared[None])
        filters = jnp.einsum('rsa,rc->sac', radial_basis, w_radial, precision=EXACT)
        onehot = (neighbour_kinds[:, :, None] == species_ids[None, None, :]).astype(jnp.float32)
        features = jnp.einsum('sak,kc->sac', onehot, embedding, precision=EXACT)
        return (running + lax.optimization_barrier(jnp.sum(edge_mask[:, :, None] * filters * features, axis=0)), None)
    initial = jnp.zeros((atom_count, w_radial.shape[1]), jnp.float32)
    summed, _unused = lax.scan(jax.checkpoint(one_group), initial, (vector_groups, kind_groups, mask_groups))
    aggregate = summed / slot_count
    own_onehot = (own_kinds[:, None] == species_ids[None, :]).astype(jnp.float32)
    initial_features = jnp.dot(own_onehot, embedding, precision=EXACT)
    updated = initial_features + jax.nn.silu(jnp.dot(aggregate, w_mix, precision=EXACT))
    readout = jax.nn.silu(jnp.dot(updated, w_read, precision=EXACT))
    energy = jnp.sum(jnp.dot(readout, w_out, precision=EXACT))
    return (energy, updated)

def structure_factors(coords, features, wave_vectors):
    wave_count = wave_vectors.shape[1]
    block_width = block_size(wave_count)
    blocks = jnp.moveaxis(wave_vectors.reshape(3, wave_count // block_width, block_width), 1, 0)

    def one_block(wave_block):
        phases = jnp.einsum('xk,xn->kn', wave_block, coords, precision=EXACT)
        return jnp.stack([jnp.dot(jnp.cos(phases), features, precision=EXACT), jnp.dot(jnp.sin(phases), features, precision=EXACT)])
    pieces = lax.map(jax.checkpoint(one_block), blocks)
    return jnp.moveaxis(pieces, 1, 0).reshape(2, wave_count, features.shape[1])

def wave_vectors_of(wave_numbers, row_count, col_count):
    lengths = jnp.array([CELL_EDGE * row_count, CELL_EDGE * col_count, HEIGHT], jnp.float32)
    return 2.0 * math.pi * wave_numbers.astype(jnp.float32) / lengths[:, None]

def ghost_tables(positions, species, ghost_index):
    coord_list = [positions]
    kind_list = [species]
    for order_id, (row_step, col_step) in enumerate(DIRECTIONS):
        source_id = len(DIRECTIONS) - 1 - order_id
        moved_coords = jnp.roll(positions, (-row_step, -col_step), axis=(1, 2))
        moved_kinds = jnp.roll(species, (-row_step, -col_step), axis=(0, 1))
        moved_index = jnp.roll(ghost_index[:, :, source_id, :], (-row_step, -col_step), axis=(0, 1))
        wide_index = jnp.broadcast_to(moved_index[None], (3,) + moved_index.shape)
        picked = jnp.take_along_axis(moved_coords, wide_index, axis=3)
        offset_vec = jnp.array([row_step * CELL_EDGE, col_step * CELL_EDGE, 0.0], jnp.float32)
        coord_list.append(picked + offset_vec[:, None, None, None])
        kind_list.append(jnp.take_along_axis(moved_kinds, moved_index, axis=2))
    return (jnp.concatenate(coord_list, axis=3), jnp.concatenate(kind_list, axis=2))

def total_energy(positions, strain, species, counts, neighbours, ghost_index, wave_numbers, embedding, w_radial, w_mix, w_read, w_out, amplitude, kernel_width, filter_gain):
    ext_coords, ext_kinds = ghost_tables(positions, species, ghost_index)
    device_count = N_ROW * N_COL
    atom_count = positions.shape[3]
    coord_rows = jnp.moveaxis(ext_coords.reshape(3, device_count, -1), 1, 0)
    kind_rows = ext_kinds.reshape(device_count, -1)
    neighbour_rows = neighbours.reshape(device_count, NB, atom_count)
    count_rows = counts.reshape(device_count, atom_count)
    slot_ids = jnp.arange(NB, dtype=jnp.int32)

    def one_device(inputs):
        coords, kind_table, neighbour_ids, live_counts = inputs
        own_coords = coords[:, :atom_count]
        edge_vectors = coords[:, neighbour_ids] - own_coords[:, None, :]
        edge_vectors = edge_vectors + jnp.einsum('xy,ysa->xsa', strain, edge_vectors, precision=EXACT)
        edge_valid = (slot_ids[:, None] < live_counts[None, :]).astype(jnp.float32)
        return short_range(edge_vectors, kind_table[:atom_count], kind_table[neighbour_ids], edge_valid, embedding, w_radial, w_mix, w_read, w_out)
    energies, updated = lax.map(jax.checkpoint(one_device), (coord_rows, kind_rows, neighbour_rows, count_rows))
    row_shift = jnp.arange(N_ROW, dtype=jnp.int32).astype(jnp.float32) * CELL_EDGE
    col_shift = jnp.arange(N_COL, dtype=jnp.int32).astype(jnp.float32) * CELL_EDGE
    offsets = jnp.stack([jnp.broadcast_to(row_shift[:, None], (N_ROW, N_COL)), jnp.broadcast_to(col_shift[None, :], (N_ROW, N_COL)), jnp.zeros((N_ROW, N_COL), jnp.float32)])
    global_coords = positions + offsets[..., None]
    wave_vectors = wave_vectors_of(wave_numbers, N_ROW, N_COL)
    factors = structure_factors(global_coords.reshape(3, -1), updated.reshape(-1, updated.shape[2]), wave_vectors)
    squared_norm = lax.optimization_barrier(jnp.sum(wave_vectors * wave_vectors, axis=0)) - 2.0 * jnp.einsum('xk,xy,yk->k', wave_vectors, strain, wave_vectors, precision=EXACT)
    volume = CELL_EDGE * N_ROW * CELL_EDGE * N_COL * HEIGHT * (1.0 + jnp.trace(strain))
    weights = amplitude[None, :] * filter_gain * jnp.exp(-kernel_width[None, :] * squared_norm[:, None])
    kspace_energy = 0.5 / volume * jnp.sum(weights * (factors[0] * factors[0] + factors[1] * factors[1]))
    return jnp.sum(energies) + kspace_energy

def reference(positions, species, counts, neighbours, ghost_index, wave_numbers, embedding, w_radial, w_mix, w_read, w_out, amplitude, kernel_width, filter_gain):
    strain = jnp.zeros((3, 3), jnp.float32)
    position_grad, strain_grad = jax.grad(total_energy, argnums=(0, 1))(positions, strain, species, counts, neighbours, ghost_index, wave_numbers, embedding, w_radial, w_mix, w_read, w_out, amplitude, kernel_width, filter_gain)
    volume = CELL_EDGE * N_ROW * CELL_EDGE * N_COL * HEIGHT
    return (-position_grad, -strain_grad / volume)
```

```python
import functools
import math

import jax
import jax.numpy as jnp
from jax import lax
from jax.experimental import pallas as pl
from jax.experimental.pallas import tpu as pltpu
from jax.sharding import PartitionSpec as P

CELL_EDGE = 12.0
HEIGHT = 36.0
KMAX = 6
HARMONICS = 8
EXACT = lax.Precision.HIGHEST
GOOD = lax.Precision.HIGH
DIRECTIONS = ((-1, -1), (-1, 0), (-1, 1), (0, -1), (0, 1), (1, -1), (1, 0), (1, 1))
F32 = jnp.float32
BF16 = jnp.bfloat16
AXES = ("row", "col")


def radial_rate(order):
    return 0.003 * 1.6**order


def round_up(value, step):
    return -(-value // step) * step


def direction_slots(row_count, col_count):
    seen = {}
    slots = []
    for row_step, col_step in DIRECTIONS:
        key = (row_step % row_count, col_step % col_count)
        slots.append(seen.get(key, 0))
        seen[key] = slots[-1] + 1
    return slots, max(seen.values())


def dot(lhs, rhs, lhs_dim, rhs_dim, precision=None):
    return lax.dot_general(
        lhs,
        rhs,
        (((lhs_dim,), (rhs_dim,)), ((), ())),
        precision=precision,
        preferred_element_type=F32,
    )


def split(values):
    high = values.astype(BF16).astype(F32)
    return high, values - high


def gain_kernel(dims, gain_ref, waves_ref, amp_ref, width_ref, phi_ref, width_out_ref):
    device_count, channel_count, own_channels, lengths, volume = dims
    me = lax.axis_index("row") * lax.axis_size("col") + lax.axis_index("col")
    wave_count = gain_ref.shape[0]
    rows = (KMAX + 1) * HARMONICS
    lanes = own_channels * HARMONICS
    place = lax.broadcasted_iota(jnp.int32, (8, channel_count), 0) * device_count + me
    chosen = (lax.broadcasted_iota(jnp.int32, (8, channel_count), 1) == place).astype(F32)
    own_gain = dot(chosen, gain_ref[...], 1, 1, EXACT)
    first, second, third = waves_ref[0:1, :], waves_ref[1:2, :], waves_ref[2:3, :]
    sign = jnp.where(first < 0, 2, 0) + jnp.where(second < 0, 1, 0)
    key = sign * rows + jnp.abs(first) * HARMONICS + jnp.abs(second)
    spots = lax.broadcasted_iota(jnp.int32, (4 * rows, wave_count), 0) == key
    onehot = jnp.where(spots, 1.0, 0.0).astype(BF16)
    heights = lax.broadcasted_iota(jnp.int32, (HARMONICS, wave_count), 0) + 1 == third
    blocks = [
        jnp.where(heights, own_gain[q : q + 1, :], 0.0) for q in range(own_channels)
    ]
    wide = jnp.concatenate(blocks, axis=0)
    high = wide.astype(BF16)
    rest = wide - high.astype(F32)
    middle = rest.astype(BF16)
    low = (rest - middle.astype(F32)).astype(BF16)
    summed = dot(onehot, high, 1, 1) + (dot(onehot, middle, 1, 1) + dot(onehot, low, 1, 1))
    lane = lax.broadcasted_iota(jnp.int32, (8, channel_count), 1)
    wanted = jnp.minimum((lane // HARMONICS) * device_count + me, channel_count - 1)
    amp = jnp.take_along_axis(jnp.broadcast_to(amp_ref[...], (8, channel_count)), wanted, axis=1)
    width = jnp.take_along_axis(
        jnp.broadcast_to(width_ref[...], (8, channel_count)), wanted, axis=1
    )
    amp, width = amp[0:1, :lanes], width[0:1, :lanes]
    k1, k2, k3 = grid_numbers(rows, lanes, lengths)
    squared = k1 * k1 + k2 * k2 + k3 * k3
    base = amp * jnp.exp(-width * squared) * (1.0 / volume)
    for sign_id in range(4):
        phi_ref[sign_id] = base * summed[sign_id * rows : (sign_id + 1) * rows, :]
    width_out_ref[...] = jnp.broadcast_to(width, (8, lanes))


def grid_numbers(rows, lanes, lengths):
    row_id = lax.broadcasted_iota(jnp.int32, (rows, lanes), 0)
    lane_id = lax.broadcasted_iota(jnp.int32, (rows, lanes), 1)
    k1 = (row_id // HARMONICS).astype(F32) * (2.0 * math.pi / lengths[0])
    k2 = (row_id % HARMONICS).astype(F32) * (2.0 * math.pi / lengths[1])
    k3 = (lane_id % HARMONICS + 1).astype(F32) * (2.0 * math.pi / lengths[2])
    return k1, k2, k3


def short_forward_kernel(
    own_channels,
    own_ref,
    prev_ref,
    next_ref,
    left_ref,
    right_ref,
    counts_ref,
    ids_ref,
    radial_ref,
    embed_ref,
    mix_ref,
    read_ref,
    out_ref,
    send_ref,
    vec_ref,
    kind_ref,
    dupd_ref,
    slope_ref,
    table,
    base,
    pooled,
    weights,
    kinds8,
):
    slot_count, atom_count = ids_ref.shape
    species_count, channel_count = embed_ref.shape
    radial_count = radial_ref.shape[0]
    device_count = send_ref.shape[0]

    def cell(row_step, col_step):
        if col_step == 0:
            return {0: own_ref, -1: prev_ref, 1: next_ref}[row_step]
        side = left_ref if col_step < 0 else right_ref
        return side.at[{0: 0, -1: 1, 1: 2}[row_step]]

    for order, (row_step, col_step) in enumerate(DIRECTIONS):
        block = cell(row_step, col_step)
        source = len(DIRECTIONS) - 1 - order
        base[0, order : order + 1, :] = block[0:1, :] + row_step * CELL_EDGE
        base[1, order : order + 1, :] = block[1:2, :] + col_step * CELL_EDGE
        base[2, order : order + 1, :] = block[2:3, :]
        base[3, order : order + 1, :] = block[3:4, :]
        base[4, order : order + 1, :] = block[4 + source : 5 + source, :]
    picks = base[4].astype(jnp.int32)
    for part in range(4):
        table[part, 0:1, :] = own_ref[part : part + 1, :]
        table[part, 8:16, :] = jnp.take_along_axis(base[part], picks, axis=1)

    ids = ids_ref[...]
    lane = ids & (atom_count - 1)
    source = ids // atom_count
    gathered = []
    for part in range(4):
        wide = jnp.broadcast_to(table[part, 0:1, :], ids.shape)
        values = jnp.take_along_axis(wide, lane, axis=1)
        for order in range(len(DIRECTIONS)):
            wide = jnp.broadcast_to(table[part, 8 + order : 9 + order, :], ids.shape)
            values = jnp.where(
                source == order + 1, jnp.take_along_axis(wide, lane, axis=1), values
            )
        gathered.append(values)
    slot = lax.broadcasted_iota(jnp.int32, ids.shape, 0)
    kind = jnp.where(slot < counts_ref[...], gathered[3], -1.0)
    kind_ref[...] = kind
    squared = jnp.zeros(ids.shape, F32)
    for part in range(3):
        vector = gathered[part] - own_ref[part : part + 1, :]
        vec_ref[part] = vector
        squared = squared + vector * vector
    masks = [kind == float(k) for k in range(species_count)]
    for order in range(radial_count):
        basis = jnp.exp(squared * (-radial_rate(order)))
        for k in range(species_count):
            spot = k * radial_count + order
            pooled[spot : spot + 1, :] = jnp.sum(
                jnp.where(masks[k], basis, 0.0), axis=0, keepdims=True
            )
    for k in range(species_count):
        weights[k * radial_count : (k + 1) * radial_count, :] = (
            radial_ref[...] * embed_ref[k : k + 1, :]
        )
    aggregate = dot(weights[...], pooled[...], 0, 0, EXACT) * (1.0 / slot_count)
    kinds8[...] = jnp.zeros_like(kinds8)
    kinds8[0:species_count, :] = embed_ref[...]
    own_hot = (
        lax.broadcasted_iota(jnp.int32, kinds8.shape, 0).astype(F32) == own_ref[3:4, :]
    ).astype(F32)
    initial = dot(kinds8[...], own_hot, 0, 0, EXACT)
    before = dot(mix_ref[...], aggregate, 0, 0, EXACT)
    gate = 1.0 / (1.0 + jnp.exp(-before))
    updated = initial + before * gate
    slope_ref[...] = gate + before * gate * (1.0 - gate)
    for q in range(own_channels):
        low, high = q * device_count, min(channel_count, (q + 1) * device_count)
        send_ref[0 : high - low, q, :] = updated[low:high, :]
        if high - low < device_count:
            send_ref[high - low :, q, :] = jnp.zeros(
                (device_count - (high - low), atom_count), F32
            )
    for part in range(3):
        send_ref[:, own_channels + part, :] = jnp.broadcast_to(
            own_ref[part : part + 1, :], (device_count, atom_count)
        )
    readout = dot(read_ref[...], updated, 0, 0, EXACT)
    gate = 1.0 / (1.0 + jnp.exp(-readout))
    scale = jnp.broadcast_to(out_ref[...], (channel_count, channel_count)).T
    dread = scale[:, 0:atom_count] * (gate + readout * gate * (1.0 - gate))
    dupd_ref[...] = dot(read_ref[...], dread, 1, 0, EXACT)


def turn_tables(turns, multiples):
    angle = turns * multiples
    halves = jnp.floor(2.0 * angle + 0.5)
    rest = angle - 0.5 * halves
    sign = 1.0 - 2.0 * (halves - 2.0 * jnp.floor(0.5 * halves))
    square = rest * rest

    def series(first, last):
        terms = [
            (-1.0) ** (p // 2) * (2.0 * math.pi) ** p / math.factorial(p)
            for p in range(first, last + 1, 2)
        ]
        total = jnp.full_like(square, terms[-1])
        for term in reversed(terms[:-1]):
            total = total * square + term
        return total

    return sign * series(0, 12), sign * rest * series(1, 13)


def wave_kernel(
    dims, recv_ref, phi_ref, width_ref, send_ref, virial_ref, planes, lifted, heights
):
    own_channels, col_count, chunk, lengths = dims
    device_count, _, atom_count = recv_ref.shape
    rows = (KMAX + 1) * HARMONICS
    lanes = own_channels * HARMONICS
    chunk_count = device_count // chunk
    multiples = lax.broadcasted_iota(jnp.int32, (HARMONICS, atom_count), 0).astype(F32)

    def fill(chunk_id):
        def one(index, _):
            device = chunk_id * chunk + index
            spot = pl.ds(pl.multiple_of(index * atom_count, atom_count), atom_count)
            block = recv_ref[device]
            corner_row = (device // col_count).astype(F32) * CELL_EDGE
            corner_col = (device % col_count).astype(F32) * CELL_EDGE
            turns_x = (block[own_channels : own_channels + 1] + corner_row) * (1.0 / lengths[0])
            turns_y = (block[own_channels + 1 : own_channels + 2] + corner_col) * (1.0 / lengths[1])
            turns_z = block[own_channels + 2 : own_channels + 3] * (1.0 / lengths[2])
            cos_x, sin_x = turn_tables(turns_x, multiples)
            cos_y, sin_y = turn_tables(turns_y, multiples)
            cos_z, sin_z = turn_tables(turns_z, multiples + 1.0)
            for m in range(KMAX + 1):
                cos_row, sin_row = cos_x[m : m + 1, :], sin_x[m : m + 1, :]
                for p, (first, second) in enumerate(
                    ((cos_row, cos_y), (cos_row, sin_y), (sin_row, cos_y), (sin_row, sin_y))
                ):
                    low = p * rows + m * HARMONICS
                    planes[low : low + HARMONICS, spot] = first * second
            heights[0, :, spot] = cos_z
            heights[1, :, spot] = sin_z
            for q in range(own_channels):
                feature = block[q : q + 1, :]
                lifted[q * HARMONICS : (q + 1) * HARMONICS, spot] = feature * cos_z
                lifted[lanes + q * HARMONICS : lanes + (q + 1) * HARMONICS, spot] = feature * sin_z
            return 0

        lax.fori_loop(0, chunk, one, 0, unroll=2)

    def project(chunk_id):
        fill(chunk_id)
        return dot(planes[...], lifted[...], 1, 1, GOOD)

    if chunk_count == 1:
        sums = project(0)
    else:
        sums = lax.fori_loop(
            0,
            chunk_count,
            lambda c, total: total + project(c),
            jnp.zeros((4 * rows, 2 * lanes), F32),
        )
    cos_part, sin_part = sums[:, :lanes], sums[:, lanes:]
    blocks = [(cos_part[p * rows : (p + 1) * rows], sin_part[p * rows : (p + 1) * rows]) for p in range(4)]
    (cc_c, cc_s), (cs_c, cs_s), (sc_c, sc_s), (ss_c, ss_s) = blocks
    zero = jnp.zeros((rows, lanes), F32)
    d_cc_c = d_cc_s = d_cs_c = d_cs_s = d_sc_c = d_sc_s = d_ss_c = d_ss_s = zero
    total = even = first_odd = second_odd = both_odd = zero
    for sign_id, (s1, s2) in enumerate(((1.0, 1.0), (1.0, -1.0), (-1.0, 1.0), (-1.0, -1.0))):
        real = cc_c - s1 * s2 * ss_c - s1 * sc_s - s2 * cs_s
        imag = cc_s - s1 * s2 * ss_s + s1 * sc_c + s2 * cs_c
        phi = phi_ref[sign_id]
        dreal, dimag = phi * real, phi * imag
        power = dreal * real + dimag * imag
        d_cc_c, d_ss_c = d_cc_c + dreal, d_ss_c - s1 * s2 * dreal
        d_sc_s, d_cs_s = d_sc_s - s1 * dreal, d_cs_s - s2 * dreal
        d_cc_s, d_ss_s = d_cc_s + dimag, d_ss_s - s1 * s2 * dimag
        d_sc_c, d_cs_c = d_sc_c + s1 * dimag, d_cs_c + s2 * dimag
        even = even + power
        first_odd = first_odd + s1 * power
        second_odd = second_odd + s2 * power
        both_odd = both_odd + s1 * s2 * power
    width = width_ref[0:1, :]
    k1, k2, k3 = grid_numbers(rows, lanes, lengths)

    def total_of(values):
        return jnp.sum(jnp.sum(values, axis=0, keepdims=True), axis=1, keepdims=True)

    energy = 0.5 * total_of(even)
    scaled = width * even
    terms = {
        (0, 0): energy - total_of(k1 * k1 * scaled),
        (1, 1): energy - total_of(k2 * k2 * scaled),
        (2, 2): energy - total_of(k3 * k3 * scaled),
        (0, 1): -total_of(k1 * k2 * width * both_odd),
        (0, 2): -total_of(k1 * k3 * width * first_odd),
        (1, 2): -total_of(k2 * k3 * width * second_odd),
    }
    virial_ref[...] = virial_row(terms, virial_ref.shape)

    values = jnp.concatenate(
        [
            jnp.concatenate(pair, axis=1)
            for pair in ((d_cc_c, d_cc_s), (d_cs_c, d_cs_s), (d_sc_c, d_sc_s), (d_ss_c, d_ss_s))
        ],
        axis=0,
    )
    cc, cs, sc, ss = (values[p * rows : (p + 1) * rows] for p in range(4))
    row_id = lax.broadcasted_iota(jnp.int32, (rows, 2 * lanes), 0)
    m1 = (row_id // HARMONICS).astype(F32)
    m2 = (row_id % HARMONICS).astype(F32)
    along_x = jnp.concatenate([m1 * sc, m1 * ss, -m1 * cc, -m1 * cs], axis=0)
    along_y = jnp.concatenate([m2 * cs, -m2 * cc, m2 * ss, -m2 * sc], axis=0)
    stacked = jnp.concatenate([values, along_x, along_y], axis=1)

    numbers = multiples + 1.0

    def back(chunk_id):
        if chunk_count > 1:
            fill(chunk_id)
        result = dot(stacked, planes[...], 0, 0, GOOD)
        for index in range(chunk):
            low, high = index * atom_count, (index + 1) * atom_count
            device = chunk_id * chunk + index
            cos_z, sin_z = heights[0, :, low:high], heights[1, :, low:high]
            part = result[:, low:high]
            grad_x = jnp.zeros((HARMONICS, atom_count), F32)
            grad_y = grad_x
            grad_z = grad_x
            pieces = []
            for q in range(own_channels):
                a, b = q * HARMONICS, lanes + q * HARMONICS
                on_cos, on_sin = part[a : a + HARMONICS], part[b : b + HARMONICS]
                pieces.append(on_cos * cos_z + on_sin * sin_z)
                lift_cos = lifted[a : a + HARMONICS, low:high]
                lift_sin = lifted[b : b + HARMONICS, low:high]
                grad_z = grad_z + on_sin * lift_cos - on_cos * lift_sin
                a, b = a + 2 * lanes, b + 2 * lanes
                grad_x = grad_x + part[a : a + HARMONICS] * lift_cos + part[b : b + HARMONICS] * lift_sin
                a, b = a + 2 * lanes, b + 2 * lanes
                grad_y = grad_y + part[a : a + HARMONICS] * lift_cos + part[b : b + HARMONICS] * lift_sin
            pieces.append(grad_x * (2.0 * math.pi / lengths[0]))
            pieces.append(grad_y * (2.0 * math.pi / lengths[1]))
            pieces.append(grad_z * numbers * (2.0 * math.pi / lengths[2]))
            for spot, piece in enumerate(pieces):
                send_ref[device, spot : spot + 1, :] = jnp.sum(piece, axis=0, keepdims=True)

    if chunk_count == 1:
        back(0)
    else:

        def step(chunk_id, carry):
            back(chunk_id)
            return carry

        lax.fori_loop(0, chunk_count, step, 0)


def virial_row(terms, shape):
    lane = lax.broadcasted_iota(jnp.int32, shape, 1)
    row = jnp.zeros(shape, F32)
    for (i, j), value in terms.items():
        spots = (lane == 3 * i + j) | (lane == 3 * j + i)
        row = jnp.where(spots, value, row)
    return row


def short_back_kernel(
    dims,
    recv_ref,
    vec_ref,
    kind_ref,
    dupd_ref,
    slope_ref,
    ids_ref,
    radial_ref,
    embed_ref,
    mix_ref,
    wave_virial_ref,
    send_ref,
    own_ref,
    fgrad,
    weights,
    dpool,
    parts,
):
    own_channels, row_count, col_count = dims
    slot_count, atom_count = ids_ref.shape
    species_count, channel_count = embed_ref.shape
    radial_count = radial_ref.shape[0]
    device_count = send_ref.shape[0]
    table_rows = round_up(len(DIRECTIONS) + 1, 16)
    for q in range(own_channels):
        low, high = q * device_count, min(channel_count, (q + 1) * device_count)
        fgrad[low:high, :] = recv_ref[0 : high - low, q, :]
    total = jnp.sum(recv_ref[...], axis=0)
    dbefore = (fgrad[...] + dupd_ref[...]) * slope_ref[...]
    daggregate = dot(mix_ref[...], dbefore, 1, 0, EXACT)
    for k in range(species_count):
        weights[k * radial_count : (k + 1) * radial_count, :] = (
            radial_ref[...] * embed_ref[k : k + 1, :]
        )
    dpool[...] = dot(weights[...], daggregate, 1, 0, EXACT)
    vectors = [vec_ref[part] for part in range(3)]
    squared = vectors[0] * vectors[0] + vectors[1] * vectors[1] + vectors[2] * vectors[2]
    kind = kind_ref[...]
    sums = [jnp.zeros(kind.shape, F32) for _ in range(species_count)]
    for order in range(radial_count):
        rate = radial_rate(order)
        basis = jnp.exp(squared * (-rate)) * (-2.0 * rate / slot_count)
        for k in range(species_count):
            spot = k * radial_count + order
            sums[k] = sums[k] + basis * dpool[spot : spot + 1, :]
    slope = jnp.zeros(kind.shape, F32)
    for k in range(species_count):
        slope = jnp.where(kind == float(k), sums[k], slope)
    grads = [slope * vector for vector in vectors]

    def total_of(values):
        return jnp.sum(jnp.sum(values, axis=0, keepdims=True), axis=1, keepdims=True)

    terms = {
        (i, j): -total_of(grads[i] * vectors[j]) for i in range(3) for j in range(i, 3)
    }
    virial = virial_row(terms, (1, atom_count)) + wave_virial_ref[0:1, :]
    for part in range(3):
        parts[2 * part], parts[2 * part + 1] = split(grads[part])

    sublane = lax.broadcasted_iota(jnp.int32, (atom_count, atom_count), 0)
    table_id = lax.broadcasted_iota(jnp.int32, (table_rows, atom_count), 0)
    group = 8
    scattered = jnp.zeros((atom_count, 6 * table_rows), F32)
    for low in range(0, slot_count, group):
        hots, columns = [], []
        for s in range(low, low + group):
            ids = ids_ref[s : s + 1, :]
            hots.append(jnp.where(sublane == (ids & (atom_count - 1)), 1.0, 0.0).astype(BF16))
            mine = table_id == ids // atom_count
            columns.append(
                jnp.concatenate(
                    [
                        jnp.where(mine, parts[p, s : s + 1, :], 0.0).astype(BF16)
                        for p in range(6)
                    ],
                    axis=0,
                )
            )
        scattered = scattered + dot(
            jnp.concatenate(hots, axis=1), jnp.concatenate(columns, axis=1), 1, 1
        )
    rows = scattered.T
    me_row, me_col = lax.axis_index("row"), lax.axis_index("col")
    slots, _ = direction_slots(row_count, col_count)
    send_ref[...] = jnp.zeros_like(send_ref)
    send_ref[:, 0, :] = jnp.broadcast_to(virial, (device_count, atom_count))
    own_ref[...] = jnp.zeros_like(own_ref)
    for part in range(3):
        low = 2 * part * table_rows
        both = rows[low : low + table_rows] + rows[low + table_rows : low + 2 * table_rows]
        own_ref[part : part + 1, :] = (
            both[0:1, :]
            - jnp.sum(grads[part], axis=0, keepdims=True)
            + total[own_channels + part : own_channels + part + 1, :]
        )
        for order, (row_step, col_step) in enumerate(DIRECTIONS):
            target = lax.rem(me_row + row_step + row_count, row_count) * col_count + lax.rem(
                me_col + col_step + col_count, col_count
            )
            send_ref[target, 1 + 3 * slots[order] + part, :] = both[1 + order, :]


def final_kernel(dims, recv_ref, own_ref, ghost_ref, forces_ref, virial_ref, parts):
    row_count, col_count, volume = dims
    atom_count = own_ref.shape[1]
    slots, _ = direction_slots(row_count, col_count)
    me_row, me_col = lax.axis_index("row"), lax.axis_index("col")
    sublane = lax.broadcasted_iota(jnp.int32, (atom_count, ghost_ref.shape[1]), 0)
    hots = []
    parts[...] = jnp.zeros_like(parts)
    for order, (row_step, col_step) in enumerate(DIRECTIONS):
        source = lax.rem(me_row - row_step + row_count, row_count) * col_count + lax.rem(
            me_col - col_step + col_count, col_count
        )
        opposite = len(DIRECTIONS) - 1 - order
        hots.append(
            jnp.where(sublane == ghost_ref[opposite : opposite + 1, :], 1.0, 0.0).astype(BF16)
        )
        low, high = order * ghost_ref.shape[1], (order + 1) * ghost_ref.shape[1]
        for part in range(3):
            row = recv_ref[source, 1 + 3 * slots[order] + part, :].reshape(1, -1)
            parts[2 * part : 2 * part + 1, low:high], parts[2 * part + 1 : 2 * part + 2, low:high] = split(row)
    returned = dot(jnp.concatenate(hots, axis=1), parts[...].astype(BF16), 1, 1).T
    for part in range(3):
        forces_ref[part : part + 1, :] = -(
            own_ref[part : part + 1, :]
            + (returned[2 * part : 2 * part + 1, :] + returned[2 * part + 1 : 2 * part + 2, :])
        )
    virial = jnp.sum(recv_ref[:, 0, :], axis=0, keepdims=True) * (1.0 / volume)
    for i in range(3):
        virial_ref[i : i + 1, :] = virial[:, 3 * i : 3 * i + 3]


def sides(block, axis):
    count = lax.axis_size(axis)
    before = lax.ppermute(block, axis, [(i, (i + 1) % count) for i in range(count)])
    if count == 2:
        return before, before
    return before, lax.ppermute(block, axis, [((i + 1) % count, i) for i in range(count)])


def per_device(
    positions,
    species,
    counts,
    neighbours,
    ghost_index,
    wave_numbers,
    embedding,
    w_radial,
    w_mix,
    w_read,
    w_out,
    amplitude,
    kernel_width,
    filter_gain,
):
    row_count = lax.axis_size("row")
    col_count = lax.axis_size("col")
    device_count = row_count * col_count
    atom_count = positions.shape[3]
    slot_count = neighbours.shape[2]
    direction_count, ghost_count = ghost_index.shape[2:]
    species_count, channel_count = embedding.shape
    radial_count = w_radial.shape[0]
    own_channels = -(-channel_count // device_count)
    lengths = (CELL_EDGE * row_count, CELL_EDGE * col_count, HEIGHT)
    volume = lengths[0] * lengths[1] * lengths[2]
    rows = (KMAX + 1) * HARMONICS
    lanes = own_channels * HARMONICS
    slab = round_up(own_channels + 3, 8)
    _, shared = direction_slots(row_count, col_count)
    slab_back = round_up(1 + 3 * shared, 8)
    chunk = math.gcd(device_count, 32)

    def shape(*dims):
        return jax.ShapeDtypeStruct(dims, F32)

    def scratch(*dims):
        return pltpu.VMEM(dims, F32)

    ids = neighbours.reshape(slot_count, atom_count)
    ghosts = ghost_index.reshape(direction_count, ghost_count)
    raw = jnp.concatenate(
        [
            positions.reshape(3, atom_count),
            species.reshape(1, atom_count).astype(F32),
            ghosts.astype(F32),
        ],
        axis=0,
    )
    before, after = sides(raw, "row")
    column = jnp.stack([raw, before, after])
    left, right = sides(column, "col")

    phi, width = pl.pallas_call(
        functools.partial(
            gain_kernel, (device_count, channel_count, own_channels, lengths, volume)
        ),
        out_shape=(shape(4, rows, lanes), shape(8, lanes)),
        cost_estimate=pl.CostEstimate(
            flops=2 * 4 * rows * filter_gain.shape[0] * 3 * lanes,
            bytes_accessed=4 * filter_gain.size,
            transcendentals=0,
        ),
        name="wave_weights",
    )(filter_gain, wave_numbers, amplitude.reshape(1, -1), kernel_width.reshape(1, -1))

    send, vectors, kinds, dupd, slope = pl.pallas_call(
        functools.partial(short_forward_kernel, own_channels),
        out_shape=(
            shape(device_count, slab, atom_count),
            shape(3, slot_count, atom_count),
            shape(slot_count, atom_count),
            shape(channel_count, atom_count),
            shape(channel_count, atom_count),
        ),
        scratch_shapes=[
            scratch(4, 16, atom_count),
            scratch(5, direction_count, atom_count),
            scratch(species_count * radial_count, atom_count),
            scratch(species_count * radial_count, channel_count),
            scratch(round_up(species_count, 8), channel_count),
        ],
        name="short_forward",
    )(
        raw,
        before,
        after,
        left,
        right,
        counts.reshape(1, atom_count),
        ids,
        w_radial,
        embedding,
        w_mix,
        w_read,
        w_out.reshape(1, -1),
    )
    features = lax.all_to_all(send, AXES, 0, 0, tiled=True)

    send, wave_virial = pl.pallas_call(
        functools.partial(wave_kernel, (own_channels, col_count, chunk, lengths)),
        out_shape=(shape(device_count, slab, atom_count), shape(8, atom_count)),
        scratch_shapes=[
            scratch(4 * rows, chunk * atom_count),
            scratch(2 * lanes, chunk * atom_count),
            scratch(2, HARMONICS, chunk * atom_count),
        ],
        compiler_params=pltpu.CompilerParams(vmem_limit_bytes=40 * 1024 * 1024),
        name="waves",
    )(features, phi, width)
    gradients = lax.all_to_all(send, AXES, 0, 0, tiled=True)

    send, own = pl.pallas_call(
        functools.partial(short_back_kernel, (own_channels, row_count, col_count)),
        out_shape=(shape(device_count, slab_back, atom_count), shape(8, atom_count)),
        scratch_shapes=[
            scratch(channel_count, atom_count),
            scratch(species_count * radial_count, channel_count),
            scratch(species_count * radial_count, atom_count),
            scratch(6, slot_count, atom_count),
        ],
        name="short_back",
    )(gradients, vectors, kinds, dupd, slope, ids, w_radial, embedding, w_mix, wave_virial)
    returned = lax.all_to_all(send, AXES, 0, 0, tiled=True)

    forces, virial = pl.pallas_call(
        functools.partial(final_kernel, (row_count, col_count, volume)),
        out_shape=(shape(3, atom_count), shape(3, 3)),
        scratch_shapes=[scratch(16, direction_count * ghost_count)],
        name="returned_ghosts",
    )(returned, own, ghosts)
    return (forces[:, None, None, :], virial)


def solution(mesh):
    return jax.shard_map(
        per_device,
        mesh=mesh,
        in_specs=(
            P(None, "row", "col", None),
            P("row", "col", None),
            P("row", "col", None),
            P("row", "col", None, None),
            P("row", "col", None, None),
            P(),
            P(),
            P(),
            P(),
            P(),
            P(),
            P(),
            P(),
            P(),
        ),
        out_specs=(P(None, "row", "col", None), P()),
        check_vma=False,
    )
```

```python
import functools
import math

import jax
import jax.numpy as jnp
from jax import lax
from jax.experimental import pallas as pl
from jax.experimental.pallas import tpu as pltpu
from jax.sharding import PartitionSpec as P

CELL_EDGE = 12.0
HEIGHT = 36.0
KMAX = 6
HARMONICS = 8
SUBLANES = 8
EXACT = lax.Precision.HIGHEST
GOOD = lax.Precision.HIGH
DIRECTIONS = ((-1, -1), (-1, 0), (-1, 1), (0, -1), (0, 1), (1, -1), (1, 0), (1, 1))
F32 = jnp.float32
BF16 = jnp.bfloat16
AXES = ("row", "col")


def radial_rate(order):
    return 0.003 * 1.6**order


def round_up(value, step):
    return -(-value // step) * step


def direction_slots(row_count, col_count):
    seen = {}
    slots = []
    for row_step, col_step in DIRECTIONS:
        key = (row_step % row_count, col_step % col_count)
        slots.append(seen.get(key, 0))
        seen[key] = slots[-1] + 1
    return slots, max(seen.values())


def dot(lhs, rhs, lhs_dim, rhs_dim, precision=None):
    return lax.dot_general(
        lhs,
        rhs,
        (((lhs_dim,), (rhs_dim,)), ((), ())),
        precision=precision,
        preferred_element_type=F32,
    )


def split(values):
    high = values.astype(BF16).astype(F32)
    return high, values - high


def wave_weights(dims, gain_ref, waves_ref, amp_ref, width_ref, phi_ref, width_out_ref):
    device_count, channel_count, own_channels, lengths, volume = dims
    me = lax.axis_index("row") * lax.axis_size("col") + lax.axis_index("col")
    wave_count = gain_ref.shape[0]
    rows = (KMAX + 1) * HARMONICS
    lanes = own_channels * HARMONICS
    place = lax.broadcasted_iota(jnp.int32, (8, channel_count), 0) * device_count + me
    chosen = (lax.broadcasted_iota(jnp.int32, (8, channel_count), 1) == place).astype(F32)
    own_gain = dot(chosen, gain_ref[...], 1, 1, EXACT)
    first, second, third = waves_ref[0:1, :], waves_ref[1:2, :], waves_ref[2:3, :]
    sign = jnp.where(first < 0, 2, 0) + jnp.where(second < 0, 1, 0)
    key = sign * rows + jnp.abs(first) * HARMONICS + jnp.abs(second)
    spots = lax.broadcasted_iota(jnp.int32, (4 * rows, wave_count), 0) == key
    onehot = jnp.where(spots, 1.0, 0.0).astype(BF16)
    heights = lax.broadcasted_iota(jnp.int32, (HARMONICS, wave_count), 0) + 1 == third
    blocks = [
        jnp.where(heights, own_gain[q : q + 1, :], 0.0) for q in range(own_channels)
    ]
    wide = jnp.concatenate(blocks, axis=0)
    high = wide.astype(BF16)
    rest = wide - high.astype(F32)
    middle = rest.astype(BF16)
    low = (rest - middle.astype(F32)).astype(BF16)
    summed = dot(onehot, high, 1, 1) + (dot(onehot, middle, 1, 1) + dot(onehot, low, 1, 1))
    lane = lax.broadcasted_iota(jnp.int32, (8, channel_count), 1)
    wanted = jnp.minimum((lane // HARMONICS) * device_count + me, channel_count - 1)
    amp = jnp.take_along_axis(jnp.broadcast_to(amp_ref[...], (8, channel_count)), wanted, axis=1)
    width = jnp.take_along_axis(
        jnp.broadcast_to(width_ref[...], (8, channel_count)), wanted, axis=1
    )
    amp, width = amp[0:1, :lanes], width[0:1, :lanes]
    k1, k2, k3 = grid_numbers(rows, lanes, lengths)
    squared = k1 * k1 + k2 * k2 + k3 * k3
    base = amp * jnp.exp(-width * squared) * (1.0 / volume)
    for sign_id in range(4):
        phi_ref[sign_id] = base * summed[sign_id * rows : (sign_id + 1) * rows, :]
    width_out_ref[...] = jnp.broadcast_to(width, (8, lanes))


def grid_numbers(rows, lanes, lengths):
    row_id = lax.broadcasted_iota(jnp.int32, (rows, lanes), 0)
    lane_id = lax.broadcasted_iota(jnp.int32, (rows, lanes), 1)
    k1 = (row_id // HARMONICS).astype(F32) * (2.0 * math.pi / lengths[0])
    k2 = (row_id % HARMONICS).astype(F32) * (2.0 * math.pi / lengths[1])
    k3 = (lane_id % HARMONICS + 1).astype(F32) * (2.0 * math.pi / lengths[2])
    return k1, k2, k3


def neighbour_of(step, row_count, col_count):
    row = lax.rem(lax.axis_index("row") + step[0] + row_count, row_count)
    col = lax.rem(lax.axis_index("col") + step[1] + col_count, col_count)
    return row * col_count + col


def pack_kernel(counts, positions_ref, species_ref, ghosts_ref, send_ref, kinds_ref, positions, species, ghosts, sems):
    row_count, col_count = counts
    fetch(((positions_ref, positions), (species_ref, species), (ghosts_ref, ghosts)), sems)
    device_count, _, atom_count = send_ref.shape
    slots, _ = direction_slots(row_count, col_count)
    kinds = species[...].astype(F32)
    kinds_ref[...] = kinds
    for part in range(3):
        send_ref[:, part, :] = jnp.broadcast_to(positions[part], (device_count, atom_count))
    send_ref[:, 3, :] = jnp.broadcast_to(kinds, (device_count, atom_count))
    for order, step in enumerate(DIRECTIONS):
        target = neighbour_of(step, row_count, col_count)
        send_ref[target, 4 + slots[order], :] = ghosts[order, :].astype(F32)


def fetch(pairs, sems):
    copies = [
        pltpu.make_async_copy(source, target, sems.at[spot])
        for spot, (source, target) in enumerate(pairs)
    ]
    for copy in copies:
        copy.start()
    for copy in copies:
        copy.wait()


def prepare_kernel(dims, kinds_ref, *refs):
    copied = 7
    sources, refs = refs[: copied + 4], refs[copied + 4 :]
    counts_ref, ids_ref, radial_ref, embed_ref, mix_ref, read_ref, out_ref = refs[:copied]
    phi_ref, width_out_ref, pool_ref, back_ref, mix_turned_ref, initial_ref = refs[copied : copied + 6]
    gain, waves, amp, width, weights, kinds8, sems = refs[copied + 6 :]
    fetch(tuple(zip(sources, (*refs[:copied], gain, waves, amp, width))), sems)
    slot_count = ids_ref.shape[0]
    species_count, channel_count = embed_ref.shape
    radial_count = radial_ref.shape[0]
    atom_count = kinds_ref.shape[1]
    mix_turned_ref[...] = mix_ref[...].T
    kinds8[...] = jnp.zeros_like(kinds8)
    kinds8[0:species_count, :] = embed_ref[...]
    own_hot = (
        lax.broadcasted_iota(jnp.int32, (kinds8.shape[0], atom_count), 0).astype(F32) == kinds_ref[...]
    ).astype(F32)
    initial_ref[...] = dot(kinds8[...], own_hot, 0, 0, EXACT)
    rates = [radial_rate(order) for order in range(radial_count)]
    order_id = lax.broadcasted_iota(jnp.int32, (radial_count, channel_count), 0)
    factor = jnp.zeros((radial_count, channel_count), F32)
    for order, rate in enumerate(rates):
        factor = jnp.where(order_id == order, -2.0 * rate / slot_count, factor)
    weights[...] = jnp.zeros_like(weights)
    for k in range(species_count):
        block = radial_ref[...] * embed_ref[k : k + 1, :]
        weights[k * radial_count : (k + 1) * radial_count, :] = block * (1.0 / slot_count)
        back_ref[k * radial_count : (k + 1) * radial_count, :] = block * factor
    turned = weights[...].T
    lane = lax.broadcasted_iota(jnp.int32, turned.shape, 1)
    for tile in range(pool_ref.shape[1] // lane.shape[1]):
        picks = lane // SUBLANES + tile * (lane.shape[1] // SUBLANES)
        pool_ref[:, tile * lane.shape[1] : (tile + 1) * lane.shape[1]] = jnp.take_along_axis(
            turned, picks, axis=1
        )
    wave_weights(dims, gain, waves, amp, width, phi_ref, width_out_ref)


def short_forward_kernel(
    dims,
    cells_ref,
    counts_ref,
    ids_ref,
    pool_ref,
    mix_ref,
    initial_ref,
    send_ref,
    vec_ref,
    kind_ref,
    upd_ref,
    slope_ref,
    table,
    base,
    pooled,
):
    own_channels, row_count, col_count = dims[:3]
    slot_count, atom_count = ids_ref.shape
    species_count, radial_count = dims[3:]
    channel_count = mix_ref.shape[0]
    device_count = send_ref.shape[0]
    slots, _ = direction_slots(row_count, col_count)
    own = cells_ref[neighbour_of((0, 0), row_count, col_count)]
    for order, step in enumerate(DIRECTIONS):
        source = neighbour_of(step, row_count, col_count)
        list_row = 4 + slots[len(DIRECTIONS) - 1 - order]
        block = cells_ref[source]
        base[0, order : order + 1, :] = block[0:1] + step[0] * CELL_EDGE
        base[1, order : order + 1, :] = block[1:2] + step[1] * CELL_EDGE
        base[2, order : order + 1, :] = block[2:3]
        base[3, order : order + 1, :] = block[3:4]
        base[4, order : order + 1, :] = block[list_row : list_row + 1]
    picks = base[4].astype(jnp.int32)
    for part in range(4):
        table[part, 0:1, :] = own[part : part + 1]
        table[part, 8:16, :] = jnp.take_along_axis(base[part], picks, axis=1)

    ids = ids_ref[...]
    lane = ids & (atom_count - 1)
    source = ids // atom_count
    gathered = []
    for part in range(4):
        wide = jnp.broadcast_to(table[part, 0:1, :], ids.shape)
        values = jnp.take_along_axis(wide, lane, axis=1)
        for order in range(len(DIRECTIONS)):
            wide = jnp.broadcast_to(table[part, 8 + order : 9 + order, :], ids.shape)
            values = jnp.where(
                source == order + 1, jnp.take_along_axis(wide, lane, axis=1), values
            )
        gathered.append(values)
    slot = lax.broadcasted_iota(jnp.int32, ids.shape, 0)
    kind = jnp.where(slot < counts_ref[...], gathered[3], -1.0)
    kind_ref[...] = kind
    squared = jnp.zeros(ids.shape, F32)
    for part in range(3):
        vector = gathered[part] - own[part : part + 1]
        vec_ref[part] = vector
        squared = squared + vector * vector
    masks = [kind == float(k) for k in range(species_count)]
    for order in range(radial_count):
        basis = jnp.exp(squared * (-radial_rate(order)))
        for k in range(species_count):
            spot = (k * radial_count + order) * SUBLANES
            chosen = jnp.where(masks[k], basis, 0.0)
            pooled[spot : spot + SUBLANES, :] = jnp.sum(
                chosen.reshape(slot_count // SUBLANES, SUBLANES, atom_count), axis=0
            )
    aggregate = dot(pool_ref[...], pooled[...], 1, 0, GOOD)
    before = dot(mix_ref[...], aggregate, 1, 0, GOOD)
    gate = 1.0 / (1.0 + jnp.exp(-before))
    updated = initial_ref[...] + before * gate
    slope_ref[...] = gate + before * gate * (1.0 - gate)
    for q in range(own_channels):
        low, high = q * device_count, min(channel_count, (q + 1) * device_count)
        send_ref[0 : high - low, q, :] = updated[low:high, :]
        if high - low < device_count:
            send_ref[high - low :, q, :] = jnp.zeros(
                (device_count - (high - low), atom_count), F32
            )
    upd_ref[...] = updated


def readout_kernel(upd_ref, read_ref, out_ref, dupd_ref):
    channel_count, atom_count = upd_ref.shape
    readout = dot(read_ref[...], upd_ref[...], 0, 0, GOOD)
    gate = 1.0 / (1.0 + jnp.exp(-readout))
    scale = jnp.broadcast_to(out_ref[...], (channel_count, channel_count)).T
    dread = scale[:, 0:atom_count] * (gate + readout * gate * (1.0 - gate))
    dupd_ref[...] = dot(read_ref[...], dread, 1, 0, GOOD)


def turn_tables(turns, multiples):
    angle = turns * multiples
    halves = jnp.floor(2.0 * angle + 0.5)
    rest = angle - 0.5 * halves
    sign = 1.0 - 2.0 * (halves - 2.0 * jnp.floor(0.5 * halves))
    square = rest * rest

    def series(first, last):
        terms = [
            (-1.0) ** (p // 2) * (2.0 * math.pi) ** p / math.factorial(p)
            for p in range(first, last + 1, 2)
        ]
        total = jnp.full_like(square, terms[-1])
        for term in reversed(terms[:-1]):
            total = total * square + term
        return total

    return sign * series(0, 12), sign * rest * series(1, 13)


def table_kernel(dims, cells_ref, axes_ref):
    col_count, chunk_count, lengths = dims
    chunk, _, atom_count = cells_ref.shape
    first_device = pl.program_id(0) * chunk if chunk_count > 1 else 0
    multiples = lax.broadcasted_iota(jnp.int32, (HARMONICS, atom_count), 0).astype(F32)

    def one(index, _):
        device = first_device + index
        spot = pl.ds(pl.multiple_of(index * atom_count, atom_count), atom_count)
        block = cells_ref[index]
        corner_row = (device // col_count).astype(F32) * CELL_EDGE
        corner_col = (device % col_count).astype(F32) * CELL_EDGE
        turns = (
            (block[0:1] + corner_row) * (1.0 / lengths[0]),
            (block[1:2] + corner_col) * (1.0 / lengths[1]),
            block[2:3] * (1.0 / lengths[2]),
        )
        for axis in range(3):
            numbers = multiples + 1.0 if axis == 2 else multiples
            cos, sin = turn_tables(turns[axis], numbers)
            axes_ref[2 * axis, :, spot] = cos
            axes_ref[2 * axis + 1, :, spot] = sin
        return 0

    lax.fori_loop(0, chunk, one, 0, unroll=4)


def wave_kernel(
    dims,
    recv_ref,
    axes_ref,
    phi_ref,
    width_ref,
    send_ref,
    virial_ref,
    high,
    low,
    lifted,
    sums,
    coefficients,
):
    own_channels, chunk_count, lengths = dims
    planes = (high, low, axes_ref, lifted)
    if chunk_count == 1:
        sums[...] = wave_sums(own_channels, recv_ref, *planes)
        wave_coefficients(lengths, sums, phi_ref, width_ref, virial_ref, coefficients)
        wave_back(own_channels, lengths, *planes, coefficients, send_ref)
        return
    phase, chunk_id = pl.program_id(0), pl.program_id(1)

    @pl.when((phase == 0) & (chunk_id == 0))
    def _():
        sums[...] = jnp.zeros_like(sums)

    part = wave_sums(own_channels, recv_ref, *planes)

    @pl.when(phase == 0)
    def _():
        sums[...] += part

    @pl.when((phase == 1) & (chunk_id == 0))
    def _():
        wave_coefficients(lengths, sums, phi_ref, width_ref, virial_ref, coefficients)

    @pl.when(phase == 1)
    def _():
        wave_back(own_channels, lengths, *planes, coefficients, send_ref)


def wave_sums(own_channels, recv_ref, high_ref, low_ref, axes_ref, lifted):
    chunk, _, atom_count = recv_ref.shape
    lanes = own_channels * HARMONICS
    group = math.gcd(chunk, 8)
    total = 0.0
    for first in range(0, chunk, group):
        for index in range(first, first + group):
            spot = slice(index * atom_count, (index + 1) * atom_count)
            for q in range(own_channels):
                feature = recv_ref[index, q : q + 1, :]
                for part in range(2):
                    row = part * lanes + q * HARMONICS
                    lifted[row : row + HARMONICS, spot] = feature * axes_ref[4 + part, :, spot]
            products = [
                axes_ref[first_axis, m : m + 1, spot] * axes_ref[second_axis, :, spot]
                for first_axis, second_axis in ((0, 2), (0, 3), (1, 2), (1, 3))
                for m in range(KMAX + 1)
            ]
            for pair in range(len(products) // 2):
                both = jnp.concatenate(products[2 * pair : 2 * pair + 2], axis=0)
                high = both.astype(BF16)
                rows = slice(2 * HARMONICS * pair, 2 * HARMONICS * (pair + 1))
                high_ref[rows, spot] = high
                low_ref[rows, spot] = (both - high.astype(F32)).astype(BF16)
        spot = slice(first * atom_count, (first + group) * atom_count)
        values = lifted[:, spot]
        high = values.astype(BF16)
        low = (values - high.astype(F32)).astype(BF16)
        main = dot(high_ref[:, spot], jnp.concatenate([high, low], axis=0), 1, 1)
        total = total + main[:, : 2 * lanes] + (main[:, 2 * lanes :] + dot(low_ref[:, spot], high, 1, 1))
    return total


def wave_coefficients(lengths, sums_ref, phi_ref, width_ref, virial_ref, coefficients_ref):
    _, rows, lanes = phi_ref.shape
    sums = sums_ref[...]
    cos_part, sin_part = sums[:, :lanes], sums[:, lanes:]
    blocks = [(cos_part[p * rows : (p + 1) * rows], sin_part[p * rows : (p + 1) * rows]) for p in range(4)]
    (cc_c, cc_s), (cs_c, cs_s), (sc_c, sc_s), (ss_c, ss_s) = blocks
    zero = jnp.zeros((rows, lanes), F32)
    d_cc_c = d_cc_s = d_cs_c = d_cs_s = d_sc_c = d_sc_s = d_ss_c = d_ss_s = zero
    total = even = first_odd = second_odd = both_odd = zero
    for sign_id, (s1, s2) in enumerate(((1.0, 1.0), (1.0, -1.0), (-1.0, 1.0), (-1.0, -1.0))):
        real = cc_c - s1 * s2 * ss_c - s1 * sc_s - s2 * cs_s
        imag = cc_s - s1 * s2 * ss_s + s1 * sc_c + s2 * cs_c
        phi = phi_ref[sign_id]
        dreal, dimag = phi * real, phi * imag
        power = dreal * real + dimag * imag
        d_cc_c, d_ss_c = d_cc_c + dreal, d_ss_c - s1 * s2 * dreal
        d_sc_s, d_cs_s = d_sc_s - s1 * dreal, d_cs_s - s2 * dreal
        d_cc_s, d_ss_s = d_cc_s + dimag, d_ss_s - s1 * s2 * dimag
        d_sc_c, d_cs_c = d_sc_c + s1 * dimag, d_cs_c + s2 * dimag
        even = even + power
        first_odd = first_odd + s1 * power
        second_odd = second_odd + s2 * power
        both_odd = both_odd + s1 * s2 * power
    width = width_ref[0:1, :]
    k1, k2, k3 = grid_numbers(rows, lanes, lengths)

    def total_of(values):
        return jnp.sum(jnp.sum(values, axis=0, keepdims=True), axis=1, keepdims=True)

    energy = 0.5 * total_of(even)
    scaled = width * even
    terms = {
        (0, 0): energy - total_of(k1 * k1 * scaled),
        (1, 1): energy - total_of(k2 * k2 * scaled),
        (2, 2): energy - total_of(k3 * k3 * scaled),
        (0, 1): -total_of(k1 * k2 * width * both_odd),
        (0, 2): -total_of(k1 * k3 * width * first_odd),
        (1, 2): -total_of(k2 * k3 * width * second_odd),
    }
    virial_ref[...] = virial_row(terms, virial_ref.shape)

    values = jnp.concatenate(
        [
            jnp.concatenate(pair, axis=1)
            for pair in ((d_cc_c, d_cc_s), (d_cs_c, d_cs_s), (d_sc_c, d_sc_s), (d_ss_c, d_ss_s))
        ],
        axis=0,
    )
    cc, cs, sc, ss = (values[p * rows : (p + 1) * rows] for p in range(4))
    row_id = lax.broadcasted_iota(jnp.int32, (rows, 2 * lanes), 0)
    m1 = (row_id // HARMONICS).astype(F32)
    m2 = (row_id % HARMONICS).astype(F32)
    along_x = jnp.concatenate([m1 * sc, m1 * ss, -m1 * cc, -m1 * cs], axis=0)
    along_y = jnp.concatenate([m2 * cs, -m2 * cc, m2 * ss, -m2 * sc], axis=0)
    stacked = jnp.concatenate([values, along_x, along_y], axis=1).T
    high = stacked.astype(BF16)
    coefficients_ref[0 : 6 * lanes, :] = high
    coefficients_ref[6 * lanes :, :] = (stacked - high.astype(F32)).astype(BF16)


def wave_back(own_channels, lengths, high_ref, low_ref, axes_ref, lifted, coefficients, send_ref):
    chunk, _, atom_count = send_ref.shape
    lanes = own_channels * HARMONICS
    numbers = lax.broadcasted_iota(jnp.int32, (HARMONICS, atom_count), 0).astype(F32) + 1.0
    values = coefficients[...]
    main = dot(values, high_ref[...], 1, 0)
    result = main[: 6 * lanes] + (main[6 * lanes :] + dot(values[: 6 * lanes], low_ref[...], 1, 0))
    for index in range(chunk):
        low, high = index * atom_count, (index + 1) * atom_count
        cos_z, sin_z = axes_ref[4, :, low:high], axes_ref[5, :, low:high]
        part = result[:, low:high]
        grad_x = jnp.zeros((HARMONICS, atom_count), F32)
        grad_y = grad_x
        grad_z = grad_x
        pieces = []
        for q in range(own_channels):
            a, b = q * HARMONICS, lanes + q * HARMONICS
            on_cos, on_sin = part[a : a + HARMONICS], part[b : b + HARMONICS]
            pieces.append(on_cos * cos_z + on_sin * sin_z)
            lift_cos = lifted[a : a + HARMONICS, low:high]
            lift_sin = lifted[b : b + HARMONICS, low:high]
            grad_z = grad_z + on_sin * lift_cos - on_cos * lift_sin
            a, b = a + 2 * lanes, b + 2 * lanes
            grad_x = grad_x + part[a : a + HARMONICS] * lift_cos + part[b : b + HARMONICS] * lift_sin
            a, b = a + 2 * lanes, b + 2 * lanes
            grad_y = grad_y + part[a : a + HARMONICS] * lift_cos + part[b : b + HARMONICS] * lift_sin
        pieces.append(grad_x * (2.0 * math.pi / lengths[0]))
        pieces.append(grad_y * (2.0 * math.pi / lengths[1]))
        pieces.append(grad_z * numbers * (2.0 * math.pi / lengths[2]))
        for spot, piece in enumerate(pieces):
            send_ref[index, spot : spot + 1, :] = jnp.sum(piece, axis=0, keepdims=True)


def virial_row(terms, shape):
    lane = lax.broadcasted_iota(jnp.int32, shape, 1)
    row = jnp.zeros(shape, F32)
    for (i, j), value in terms.items():
        spots = (lane == 3 * i + j) | (lane == 3 * j + i)
        row = jnp.where(spots, value, row)
    return row


def short_back_kernel(
    dims,
    recv_ref,
    vec_ref,
    kind_ref,
    dupd_ref,
    slope_ref,
    ids_ref,
    back_ref,
    mix_ref,
    wave_virial_ref,
    send_ref,
    own_ref,
    fgrad,
    dpool,
    parts,
):
    own_channels, row_count, col_count, species_count, radial_count = dims
    slot_count, atom_count = ids_ref.shape
    channel_count = mix_ref.shape[0]
    device_count = send_ref.shape[0]
    table_rows = round_up(len(DIRECTIONS) + 1, 16)
    for q in range(own_channels):
        low, high = q * device_count, min(channel_count, (q + 1) * device_count)
        fgrad[low:high, :] = recv_ref[0 : high - low, q, :]
    total = jnp.sum(recv_ref[...], axis=0)
    dbefore = (fgrad[...] + dupd_ref[...]) * slope_ref[...]
    daggregate = dot(mix_ref[...], dbefore, 1, 0, GOOD)
    dpool[...] = dot(back_ref[...], daggregate, 1, 0, GOOD)
    vectors = [vec_ref[part] for part in range(3)]
    squared = vectors[0] * vectors[0] + vectors[1] * vectors[1] + vectors[2] * vectors[2]
    kind = kind_ref[...]
    sums = [jnp.zeros(kind.shape, F32) for _ in range(species_count)]
    for order in range(radial_count):
        basis = jnp.exp(squared * (-radial_rate(order)))
        for k in range(species_count):
            spot = k * radial_count + order
            sums[k] = sums[k] + basis * dpool[spot : spot + 1, :]
    slope = jnp.zeros(kind.shape, F32)
    for k in range(species_count):
        slope = jnp.where(kind == float(k), sums[k], slope)
    grads = [slope * vector for vector in vectors]

    def total_of(values):
        return jnp.sum(jnp.sum(values, axis=0, keepdims=True), axis=1, keepdims=True)

    terms = {
        (i, j): -total_of(grads[i] * vectors[j]) for i in range(3) for j in range(i, 3)
    }
    virial = virial_row(terms, (1, atom_count)) + wave_virial_ref[0:1, :]
    for part in range(3):
        parts[2 * part], parts[2 * part + 1] = split(grads[part])

    sublane = lax.broadcasted_iota(jnp.int32, (atom_count, atom_count), 0)
    table_id = lax.broadcasted_iota(jnp.int32, (table_rows, atom_count), 0)
    group = 8
    scattered = jnp.zeros((atom_count, 6 * table_rows), F32)
    for low in range(0, slot_count, group):
        hots, columns = [], []
        for s in range(low, low + group):
            ids = ids_ref[s : s + 1, :]
            hots.append(jnp.where(sublane == (ids & (atom_count - 1)), 1.0, 0.0).astype(BF16))
            mine = table_id == ids // atom_count
            columns.append(
                jnp.concatenate(
                    [
                        jnp.where(mine, parts[p, s : s + 1, :], 0.0).astype(BF16)
                        for p in range(6)
                    ],
                    axis=0,
                )
            )
        scattered = scattered + dot(
            jnp.concatenate(hots, axis=1), jnp.concatenate(columns, axis=1), 1, 1
        )
    rows = scattered.T
    slots, _ = direction_slots(row_count, col_count)
    send_ref[...] = jnp.zeros_like(send_ref)
    send_ref[:, 0, :] = jnp.broadcast_to(virial, (device_count, atom_count))
    own_ref[...] = jnp.zeros_like(own_ref)
    for part in range(3):
        low = 2 * part * table_rows
        both = rows[low : low + table_rows] + rows[low + table_rows : low + 2 * table_rows]
        own_ref[part : part + 1, :] = (
            both[0:1, :]
            - jnp.sum(grads[part], axis=0, keepdims=True)
            + total[own_channels + part : own_channels + part + 1, :]
        )
        for order, step in enumerate(DIRECTIONS):
            target = neighbour_of(step, row_count, col_count)
            send_ref[target, 1 + 3 * slots[order] + part, :] = both[1 + order, :]


def final_kernel(dims, recv_ref, own_ref, ghost_ref, forces_ref, virial_ref, parts):
    row_count, col_count, volume = dims
    atom_count = own_ref.shape[1]
    slots, _ = direction_slots(row_count, col_count)
    sublane = lax.broadcasted_iota(jnp.int32, (atom_count, ghost_ref.shape[1]), 0)
    hots = []
    parts[...] = jnp.zeros_like(parts)
    for order, step in enumerate(DIRECTIONS):
        source = neighbour_of((-step[0], -step[1]), row_count, col_count)
        opposite = len(DIRECTIONS) - 1 - order
        hots.append(
            jnp.where(sublane == ghost_ref[opposite : opposite + 1, :], 1.0, 0.0).astype(BF16)
        )
        low, high = order * ghost_ref.shape[1], (order + 1) * ghost_ref.shape[1]
        for part in range(3):
            row = recv_ref[source, 1 + 3 * slots[order] + part, :].reshape(1, -1)
            parts[2 * part : 2 * part + 1, low:high], parts[2 * part + 1 : 2 * part + 2, low:high] = split(row)
    returned = dot(jnp.concatenate(hots, axis=1), parts[...].astype(BF16), 1, 1).T
    for part in range(3):
        forces_ref[part] = -(
            own_ref[part : part + 1, :]
            + (returned[2 * part : 2 * part + 1, :] + returned[2 * part + 1 : 2 * part + 2, :])
        )
    virial = jnp.sum(recv_ref[:, 0, :], axis=0, keepdims=True) * (1.0 / volume)
    for i in range(3):
        virial_ref[i : i + 1, :] = virial[:, 3 * i : 3 * i + 3]


def per_device(
    positions,
    species,
    counts,
    neighbours,
    ghost_index,
    wave_numbers,
    embedding,
    w_radial,
    w_mix,
    w_read,
    w_out,
    amplitude,
    kernel_width,
    filter_gain,
):
    row_count = lax.axis_size("row")
    col_count = lax.axis_size("col")
    device_count = row_count * col_count
    atom_count = positions.shape[3]
    slot_count = neighbours.shape[2]
    direction_count, ghost_count = ghost_index.shape[2:]
    species_count, channel_count = embedding.shape
    radial_count = w_radial.shape[0]
    own_channels = -(-channel_count // device_count)
    lengths = (CELL_EDGE * row_count, CELL_EDGE * col_count, HEIGHT)
    volume = lengths[0] * lengths[1] * lengths[2]
    rows = (KMAX + 1) * HARMONICS
    lanes = own_channels * HARMONICS
    slab = round_up(own_channels + 3, 8)
    _, shared = direction_slots(row_count, col_count)
    slab_back = round_up(1 + 3 * shared, 8)
    slab_first = round_up(4 + shared, 8)
    slab_features = round_up(own_channels, 4)
    chunk = math.gcd(device_count, 32)
    chunk_count = device_count // chunk

    def exchange(slabs):
        return lax.all_to_all(slabs, AXES, 0, 0, tiled=True)

    def shape(*dims):
        return jax.ShapeDtypeStruct(dims, F32)

    def scratch(*dims):
        return pltpu.VMEM(dims, F32)

    def call(kernel, out_shape, vmem=16, **options):
        return pl.pallas_call(
            kernel,
            out_shape=out_shape,
            compiler_params=pltpu.CompilerParams(vmem_limit_bytes=vmem * 1024 * 1024),
            **options,
        )

    ids = neighbours.reshape(slot_count, atom_count)
    ghosts = ghost_index.reshape(direction_count, ghost_count)
    mesh_counts = (row_count, col_count)
    def fetched(*arrays):
        return [pltpu.with_memory_space_constraint(x, pltpu.HBM) for x in arrays]

    kept = pl.BlockSpec(memory_space=pltpu.HBM)
    near = pl.BlockSpec(memory_space=pltpu.VMEM)
    send, own_kinds = call(
        functools.partial(pack_kernel, mesh_counts),
        (shape(device_count, slab_first, atom_count), shape(1, atom_count)),
        in_specs=[kept] * 3,
        scratch_shapes=[
            scratch(3, 1, atom_count),
            pltpu.VMEM((1, atom_count), jnp.int32),
            pltpu.VMEM(ghosts.shape, jnp.int32),
            pltpu.SemaphoreType.DMA((3,)),
        ],
        name="pack",
    )(*fetched(positions.reshape(3, 1, atom_count), species.reshape(1, atom_count), ghosts))
    cells = exchange(send)

    short_inputs = (
        counts.reshape(1, atom_count),
        ids,
        w_radial,
        embedding,
        w_mix,
        w_read,
        w_out.reshape(1, -1),
    )
    wave_inputs = (filter_gain, wave_numbers, amplitude.reshape(1, -1), kernel_width.reshape(1, -1))
    pooled_rows = species_count * radial_count
    live, ids, _, _, w_mix, w_read, w_out, phi, width, pool, back, mix_turned, initial = call(
        functools.partial(
            prepare_kernel, (device_count, channel_count, own_channels, lengths, volume)
        ),
        tuple(jax.ShapeDtypeStruct(x.shape, x.dtype) for x in short_inputs)
        + (
            shape(4, rows, lanes),
            shape(8, lanes),
            shape(channel_count, round_up(pooled_rows * SUBLANES, channel_count)),
            shape(pooled_rows, channel_count),
            shape(channel_count, channel_count),
            shape(channel_count, atom_count),
        ),
        in_specs=[near] + [kept] * (len(short_inputs) + len(wave_inputs)),
        scratch_shapes=[pltpu.VMEM(x.shape, x.dtype) for x in wave_inputs]
        + [
            scratch(round_up(pooled_rows, 128), channel_count),
            scratch(round_up(species_count, 8), channel_count),
            pltpu.SemaphoreType.DMA((len(short_inputs) + len(wave_inputs),)),
        ],
        cost_estimate=pl.CostEstimate(
            flops=2 * 4 * rows * filter_gain.shape[0] * 3 * lanes,
            bytes_accessed=4 * filter_gain.size,
            transcendentals=0,
        ),
        name="prepare",
    )(own_kinds, *fetched(*short_inputs, *wave_inputs))

    send, vectors, kinds, updated, slope = call(
        functools.partial(
            short_forward_kernel, (own_channels,) + mesh_counts + (species_count, radial_count)
        ),
        (
            shape(device_count, slab_features, atom_count),
            shape(3, slot_count, atom_count),
            shape(slot_count, atom_count),
            shape(channel_count, atom_count),
            shape(channel_count, atom_count),
        ),
        scratch_shapes=[
            scratch(4, 16, atom_count),
            scratch(5, direction_count, atom_count),
            scratch(pooled_rows * SUBLANES, atom_count),
        ],
        name="short_forward",
    )(cells, live, ids, pool, mix_turned, initial)
    send, cells, updated = lax.optimization_barrier((send, cells, updated))
    features = exchange(send)

    axes_block = (6, HARMONICS, chunk * atom_count)
    if chunk_count == 1:
        table_options = {}
    else:
        table_options = dict(
            grid=(chunk_count,),
            in_specs=[pl.BlockSpec((chunk, slab_first, atom_count), lambda i: (i, 0, 0))],
            out_specs=pl.BlockSpec(axes_block, lambda i: (0, 0, i)),
        )
    axes = call(
        functools.partial(table_kernel, (col_count, chunk_count, lengths)),
        shape(6, HARMONICS, device_count * atom_count),
        cost_estimate=pl.CostEstimate(
            flops=2000 * device_count * atom_count, bytes_accessed=200 * device_count * atom_count, transcendentals=0
        ),
        name="tables",
        **table_options,
    )(cells)
    dupd = call(readout_kernel, shape(channel_count, atom_count), name="readout")(
        updated, w_read, w_out
    )

    wave = functools.partial(wave_kernel, (own_channels, chunk_count, lengths))
    wave_shapes = (shape(device_count, slab, atom_count), shape(8, atom_count))
    wave_scratch = [
        pltpu.VMEM((4 * rows, chunk * atom_count), BF16),
        pltpu.VMEM((4 * rows, chunk * atom_count), BF16),
        scratch(2 * lanes, chunk * atom_count),
        scratch(4 * rows, 2 * lanes),
        pltpu.VMEM((12 * lanes, 4 * rows), BF16),
    ]
    if chunk_count == 1:
        wave_options = {}
    else:
        wave_options = dict(
            grid=(2, chunk_count),
            in_specs=[
                pl.BlockSpec((chunk, slab_features, atom_count), lambda p, i: (i, 0, 0)),
                pl.BlockSpec(axes_block, lambda p, i: (0, 0, i)),
                pl.BlockSpec((4, rows, lanes), lambda p, i: (0, 0, 0)),
                pl.BlockSpec((8, lanes), lambda p, i: (0, 0)),
            ],
            out_specs=(
                pl.BlockSpec((chunk, slab, atom_count), lambda p, i: (i * p, 0, 0)),
                pl.BlockSpec((8, atom_count), lambda p, i: (0, 0)),
            ),
        )
    send, wave_virial = call(
        wave, wave_shapes, vmem=20, scratch_shapes=wave_scratch, name="waves", **wave_options
    )(features, axes, phi, width)
    gradients = exchange(send)

    send, own = call(
        functools.partial(
            short_back_kernel, (own_channels,) + mesh_counts + (species_count, radial_count)
        ),
        out_shape=(shape(device_count, slab_back, atom_count), shape(8, atom_count)),
        scratch_shapes=[
            scratch(channel_count, atom_count),
            scratch(pooled_rows, atom_count),
            scratch(6, slot_count, atom_count),
        ],
        name="short_back",
    )(gradients, vectors, kinds, dupd, slope, ids, back, w_mix, wave_virial)
    returned = exchange(send)

    forces, virial = call(
        functools.partial(final_kernel, (row_count, col_count, volume)),
        out_shape=(shape(3, 1, atom_count), shape(3, 3)),
        scratch_shapes=[scratch(16, direction_count * ghost_count)],
        name="returned_ghosts",
    )(returned, own, ghosts)
    return (forces[:, None], virial)


def solution(mesh):
    return jax.shard_map(
        per_device,
        mesh=mesh,
        in_specs=(
            P(None, "row", "col", None),
            P("row", "col", None),
            P("row", "col", None),
            P("row", "col", None, None),
            P("row", "col", None, None),
            P(),
            P(),
            P(),
            P(),
            P(),
            P(),
            P(),
            P(),
            P(),
        ),
        out_specs=(P(None, "row", "col", None), P()),
        check_vma=False,
    )
```

```python
import functools
import math

import jax
import jax.numpy as jnp
from jax import lax
from jax.experimental import pallas as pl
from jax.experimental.pallas import tpu as pltpu
from jax.sharding import PartitionSpec as P

CELL_EDGE = 12.0
HEIGHT = 36.0
KMAX = 6
HARMONICS = 8
SUBLANES = 8
EXACT = lax.Precision.HIGHEST
GOOD = lax.Precision.HIGH
DIRECTIONS = ((-1, -1), (-1, 0), (-1, 1), (0, -1), (0, 1), (1, -1), (1, 0), (1, 1))
F32 = jnp.float32
BF16 = jnp.bfloat16
AXES = ("row", "col")


def radial_rate(order):
    return 0.003 * 1.6**order


def round_up(value, step):
    return -(-value // step) * step


def direction_slots(row_count, col_count):
    seen = {}
    slots = []
    for row_step, col_step in DIRECTIONS:
        key = (row_step % row_count, col_step % col_count)
        slots.append(seen.get(key, 0))
        seen[key] = slots[-1] + 1
    return slots, max(seen.values())


def dot(lhs, rhs, lhs_dim, rhs_dim, precision=None):
    return lax.dot_general(
        lhs,
        rhs,
        (((lhs_dim,), (rhs_dim,)), ((), ())),
        precision=precision,
        preferred_element_type=F32,
    )


def split(values):
    high = values.astype(BF16).astype(F32)
    return high, values - high


def wave_weights(dims, gain_ref, waves_ref, amp_ref, width_ref, phi_ref, width_out_ref):
    device_count, channel_count, own_channels, lengths, volume = dims
    me = lax.axis_index("row") * lax.axis_size("col") + lax.axis_index("col")
    wave_count = gain_ref.shape[0]
    rows = (KMAX + 1) * HARMONICS
    lanes = own_channels * HARMONICS
    place = lax.broadcasted_iota(jnp.int32, (8, channel_count), 0) * device_count + me
    chosen = (lax.broadcasted_iota(jnp.int32, (8, channel_count), 1) == place).astype(F32)
    own_gain = dot(chosen, gain_ref[...], 1, 1, EXACT)
    first, second, third = waves_ref[0:1, :], waves_ref[1:2, :], waves_ref[2:3, :]
    sign = jnp.where(first < 0, 2, 0) + jnp.where(second < 0, 1, 0)
    key = sign * rows + jnp.abs(first) * HARMONICS + jnp.abs(second)
    spots = lax.broadcasted_iota(jnp.int32, (4 * rows, wave_count), 0) == key
    onehot = jnp.where(spots, 1.0, 0.0).astype(BF16)
    heights = lax.broadcasted_iota(jnp.int32, (HARMONICS, wave_count), 0) + 1 == third
    blocks = [
        jnp.where(heights, own_gain[q : q + 1, :], 0.0) for q in range(own_channels)
    ]
    wide = jnp.concatenate(blocks, axis=0)
    high = wide.astype(BF16)
    rest = wide - high.astype(F32)
    middle = rest.astype(BF16)
    low = (rest - middle.astype(F32)).astype(BF16)
    summed = dot(onehot, high, 1, 1) + (dot(onehot, middle, 1, 1) + dot(onehot, low, 1, 1))
    lane = lax.broadcasted_iota(jnp.int32, (8, channel_count), 1)
    wanted = jnp.minimum((lane // HARMONICS) * device_count + me, channel_count - 1)
    amp = jnp.take_along_axis(jnp.broadcast_to(amp_ref[...], (8, channel_count)), wanted, axis=1)
    width = jnp.take_along_axis(
        jnp.broadcast_to(width_ref[...], (8, channel_count)), wanted, axis=1
    )
    amp, width = amp[0:1, :lanes], width[0:1, :lanes]
    k1, k2, k3 = grid_numbers(rows, lanes, lengths)
    squared = k1 * k1 + k2 * k2 + k3 * k3
    base = amp * jnp.exp(-width * squared) * (1.0 / volume)
    for sign_id in range(4):
        phi_ref[sign_id] = base * summed[sign_id * rows : (sign_id + 1) * rows, :]
    width_out_ref[...] = jnp.broadcast_to(width, (8, lanes))


def grid_numbers(rows, lanes, lengths):
    row_id = lax.broadcasted_iota(jnp.int32, (rows, lanes), 0)
    lane_id = lax.broadcasted_iota(jnp.int32, (rows, lanes), 1)
    k1 = (row_id // HARMONICS).astype(F32) * (2.0 * math.pi / lengths[0])
    k2 = (row_id % HARMONICS).astype(F32) * (2.0 * math.pi / lengths[1])
    k3 = (lane_id % HARMONICS + 1).astype(F32) * (2.0 * math.pi / lengths[2])
    return k1, k2, k3


def neighbour_of(step, row_count, col_count):
    row = lax.rem(lax.axis_index("row") + step[0] + row_count, row_count)
    col = lax.rem(lax.axis_index("col") + step[1] + col_count, col_count)
    return row * col_count + col


def pack_kernel(counts, positions_ref, species_ref, ghosts_ref, send_ref, kinds_ref, positions, species, ghosts, sems):
    row_count, col_count = counts
    fetch(((positions_ref, positions), (species_ref, species), (ghosts_ref, ghosts)), sems)
    device_count, _, atom_count = send_ref.shape
    slots, _ = direction_slots(row_count, col_count)
    kinds = species[...].astype(F32)
    kinds_ref[...] = kinds
    for part in range(3):
        send_ref[:, part, :] = jnp.broadcast_to(positions[part], (device_count, atom_count))
    send_ref[:, 3, :] = jnp.broadcast_to(kinds, (device_count, atom_count))
    for order, step in enumerate(DIRECTIONS):
        target = neighbour_of(step, row_count, col_count)
        send_ref[target, 4 + slots[order], :] = ghosts[order, :].astype(F32)


def fetch(pairs, sems):
    copies = [
        pltpu.make_async_copy(source, target, sems.at[spot])
        for spot, (source, target) in enumerate(pairs)
    ]
    for copy in copies:
        copy.start()
    for copy in copies:
        copy.wait()


def prepare_kernel(dims, kinds_ref, *refs):
    copied = 7
    sources, refs = refs[: copied + 4], refs[copied + 4 :]
    counts_ref, ids_ref, radial_ref, embed_ref, mix_ref, read_ref, out_ref = refs[:copied]
    phi_ref, width_out_ref, pool_ref, back_ref, mix_turned_ref, initial_ref = refs[copied : copied + 6]
    gain, waves, amp, width, weights, kinds8, sems = refs[copied + 6 :]
    fetch(tuple(zip(sources, (*refs[:copied], gain, waves, amp, width))), sems)
    slot_count = ids_ref.shape[0]
    species_count, channel_count = embed_ref.shape
    radial_count = radial_ref.shape[0]
    atom_count = kinds_ref.shape[1]
    mix_turned_ref[...] = mix_ref[...].T
    kinds8[...] = jnp.zeros_like(kinds8)
    kinds8[0:species_count, :] = embed_ref[...]
    own_hot = (
        lax.broadcasted_iota(jnp.int32, (kinds8.shape[0], atom_count), 0).astype(F32) == kinds_ref[...]
    ).astype(F32)
    initial_ref[...] = dot(kinds8[...], own_hot, 0, 0, EXACT)
    rates = [radial_rate(order) for order in range(radial_count)]
    order_id = lax.broadcasted_iota(jnp.int32, (radial_count, channel_count), 0)
    factor = jnp.zeros((radial_count, channel_count), F32)
    for order, rate in enumerate(rates):
        factor = jnp.where(order_id == order, -2.0 * rate / slot_count, factor)
    weights[...] = jnp.zeros_like(weights)
    for k in range(species_count):
        block = radial_ref[...] * embed_ref[k : k + 1, :]
        weights[k * radial_count : (k + 1) * radial_count, :] = block * (1.0 / slot_count)
        back_ref[k * radial_count : (k + 1) * radial_count, :] = block * factor
    turned = weights[...].T
    lane = lax.broadcasted_iota(jnp.int32, turned.shape, 1)
    for tile in range(pool_ref.shape[1] // lane.shape[1]):
        picks = lane // SUBLANES + tile * (lane.shape[1] // SUBLANES)
        pool_ref[:, tile * lane.shape[1] : (tile + 1) * lane.shape[1]] = jnp.take_along_axis(
            turned, picks, axis=1
        )
    wave_weights(dims, gain, waves, amp, width, phi_ref, width_out_ref)


def short_forward_kernel(
    dims,
    cells_ref,
    counts_ref,
    ids_ref,
    pool_ref,
    mix_ref,
    initial_ref,
    send_ref,
    vec_ref,
    kind_ref,
    owner_ref,
    upd_ref,
    slope_ref,
    table,
    lists,
    pooled,
):
    own_channels, row_count, col_count = dims[:3]
    slot_count, atom_count = ids_ref.shape
    species_count, radial_count = dims[3:]
    channel_count = mix_ref.shape[0]
    device_count = send_ref.shape[0]
    slots, _ = direction_slots(row_count, col_count)
    own = cells_ref[neighbour_of((0, 0), row_count, col_count)]
    for part in range(4):
        table[part, 0:1, :] = own[part : part + 1]
    for order, step in enumerate(DIRECTIONS):
        source = neighbour_of(step, row_count, col_count)
        list_row = 4 + slots[len(DIRECTIONS) - 1 - order]
        block = cells_ref[source]
        row = 8 + order
        table[0, row : row + 1, :] = block[0:1] + step[0] * CELL_EDGE
        table[1, row : row + 1, :] = block[1:2] + step[1] * CELL_EDGE
        table[2, row : row + 1, :] = block[2:3]
        table[3, row : row + 1, :] = block[3:4]
        lists[order : order + 1, :] = block[list_row : list_row + 1].astype(jnp.int32)

    ids = ids_ref[...]
    lane = ids & (atom_count - 1)
    source = ids // atom_count
    here = [source == order + 1 for order in range(len(DIRECTIONS))]

    def picked(ref, first, places, start):
        values = start
        for order in range(len(DIRECTIONS)):
            wide = jnp.broadcast_to(ref[first + order : first + order + 1, :], ids.shape)
            values = jnp.where(here[order], jnp.take_along_axis(wide, places, axis=1), values)
        return values

    owner = picked(lists, 0, lane, lane)
    owner_ref[...] = owner + source * atom_count
    gathered = []
    for part in range(4):
        wide = jnp.broadcast_to(table[part, 0:1, :], ids.shape)
        first = jnp.take_along_axis(wide, owner, axis=1)
        gathered.append(picked(table.at[part], 8, owner, first))
    slot = lax.broadcasted_iota(jnp.int32, ids.shape, 0)
    kind = jnp.where(slot < counts_ref[...], gathered[3], -1.0)
    kind_ref[...] = kind
    squared = jnp.zeros(ids.shape, F32)
    for part in range(3):
        vector = gathered[part] - own[part : part + 1]
        vec_ref[part] = vector
        squared = squared + vector * vector
    masks = [kind == float(k) for k in range(species_count)]
    for order in range(radial_count):
        basis = jnp.exp(squared * (-radial_rate(order)))
        for k in range(species_count):
            spot = (k * radial_count + order) * SUBLANES
            chosen = jnp.where(masks[k], basis, 0.0)
            pooled[spot : spot + SUBLANES, :] = jnp.sum(
                chosen.reshape(slot_count // SUBLANES, SUBLANES, atom_count), axis=0
            )
    aggregate = dot(pool_ref[...], pooled[...], 1, 0, GOOD)
    before = dot(mix_ref[...], aggregate, 1, 0, GOOD)
    gate = 1.0 / (1.0 + jnp.exp(-before))
    updated = initial_ref[...] + before * gate
    slope_ref[...] = gate + before * gate * (1.0 - gate)
    for q in range(own_channels):
        low, high = q * device_count, min(channel_count, (q + 1) * device_count)
        send_ref[0 : high - low, q, :] = updated[low:high, :]
        if high - low < device_count:
            send_ref[high - low :, q, :] = jnp.zeros(
                (device_count - (high - low), atom_count), F32
            )
    upd_ref[...] = updated


def readout_kernel(upd_ref, read_ref, out_ref, dupd_ref):
    channel_count, atom_count = upd_ref.shape
    readout = dot(read_ref[...], upd_ref[...], 0, 0, GOOD)
    gate = 1.0 / (1.0 + jnp.exp(-readout))
    scale = jnp.broadcast_to(out_ref[...], (channel_count, channel_count)).T
    dread = scale[:, 0:atom_count] * (gate + readout * gate * (1.0 - gate))
    dupd_ref[...] = dot(read_ref[...], dread, 1, 0, GOOD)


def turn_tables(turns, multiples):
    angle = turns * multiples
    halves = jnp.floor(2.0 * angle + 0.5)
    rest = angle - 0.5 * halves
    sign = 1.0 - 2.0 * (halves - 2.0 * jnp.floor(0.5 * halves))
    square = rest * rest

    def series(first, last):
        terms = [
            (-1.0) ** (p // 2) * (2.0 * math.pi) ** p / math.factorial(p)
            for p in range(first, last + 1, 2)
        ]
        total = jnp.full_like(square, terms[-1])
        for term in reversed(terms[:-1]):
            total = total * square + term
        return total

    return sign * series(0, 12), sign * rest * series(1, 13)


def table_kernel(dims, cells_ref, axes_ref):
    col_count, chunk_count, lengths = dims
    chunk, _, atom_count = cells_ref.shape
    first_device = pl.program_id(0) * chunk if chunk_count > 1 else 0
    multiples = lax.broadcasted_iota(jnp.int32, (HARMONICS, atom_count), 0).astype(F32)

    def one(index, _):
        device = first_device + index
        spot = pl.ds(pl.multiple_of(index * atom_count, atom_count), atom_count)
        block = cells_ref[index]
        corner_row = (device // col_count).astype(F32) * CELL_EDGE
        corner_col = (device % col_count).astype(F32) * CELL_EDGE
        turns = (
            (block[0:1] + corner_row) * (1.0 / lengths[0]),
            (block[1:2] + corner_col) * (1.0 / lengths[1]),
            block[2:3] * (1.0 / lengths[2]),
        )
        for axis in range(3):
            numbers = multiples + 1.0 if axis == 2 else multiples
            cos, sin = turn_tables(turns[axis], numbers)
            axes_ref[2 * axis, :, spot] = cos
            axes_ref[2 * axis + 1, :, spot] = sin
        return 0

    lax.fori_loop(0, chunk, one, 0, unroll=4)


def wave_kernel(dims, recv_ref, axes_ref, phi_ref, send_ref, sums, high, low, lifted, coefficients):
    own_channels, chunk_count, lengths = dims
    planes = (high, low, axes_ref, lifted)
    if chunk_count == 1:
        sums[...] = wave_sums(own_channels, recv_ref, *planes)
        wave_coefficients(sums, phi_ref, coefficients)
        wave_features(own_channels, *planes, coefficients, send_ref)
        return
    phase, chunk_id = pl.program_id(0), pl.program_id(1)

    @pl.when((phase == 0) & (chunk_id == 0))
    def _():
        sums[...] = jnp.zeros_like(sums)

    part = wave_sums(own_channels, recv_ref, *planes)

    @pl.when(phase == 0)
    def _():
        sums[...] += part

    @pl.when((phase == 1) & (chunk_id == 0))
    def _():
        wave_coefficients(sums, phi_ref, coefficients)

    @pl.when(phase == 1)
    def _():
        wave_features(own_channels, *planes, coefficients, send_ref)


def wave_force_kernel(
    dims, recv_ref, axes_ref, phi_ref, width_ref, sums, push_ref, high, low, lifted, coefficients
):
    own_channels, chunk_count, lengths = dims
    planes = (high, low, axes_ref, lifted)
    wave_planes(own_channels, recv_ref, *planes)
    if chunk_count == 1:
        wave_coefficients(sums, phi_ref, coefficients, True)
    else:

        @pl.when(pl.program_id(0) == 0)
        def _():
            wave_coefficients(sums, phi_ref, coefficients, True)

    wave_back(own_channels, lengths, *planes, coefficients, push_ref)
    virial = wave_virial(lengths, sums, phi_ref, width_ref, (1, push_ref.shape[2]))
    push_ref[:, 3, :] = jnp.broadcast_to(virial, (push_ref.shape[0], push_ref.shape[2]))


def wave_planes(own_channels, recv_ref, high_ref, low_ref, axes_ref, lifted, devices=None):
    chunk, _, atom_count = recv_ref.shape
    lanes = own_channels * HARMONICS
    for index in devices or range(chunk):
        spot = slice(index * atom_count, (index + 1) * atom_count)
        for q in range(own_channels):
            feature = recv_ref[index, q : q + 1, :]
            for part in range(2):
                row = part * lanes + q * HARMONICS
                lifted[row : row + HARMONICS, spot] = feature * axes_ref[4 + part, :, spot]
        products = [
            axes_ref[first_axis, m : m + 1, spot] * axes_ref[second_axis, :, spot]
            for first_axis, second_axis in ((0, 2), (0, 3), (1, 2), (1, 3))
            for m in range(KMAX + 1)
        ]
        for pair in range(len(products) // 2):
            both = jnp.concatenate(products[2 * pair : 2 * pair + 2], axis=0)
            high = both.astype(BF16)
            rows = slice(2 * HARMONICS * pair, 2 * HARMONICS * (pair + 1))
            high_ref[rows, spot] = high
            low_ref[rows, spot] = (both - high.astype(F32)).astype(BF16)


def wave_sums(own_channels, recv_ref, high_ref, low_ref, axes_ref, lifted):
    chunk, _, atom_count = recv_ref.shape
    lanes = own_channels * HARMONICS
    group = math.gcd(chunk, 8)
    total = 0.0
    for first in range(0, chunk, group):
        devices = range(first, first + group)
        wave_planes(own_channels, recv_ref, high_ref, low_ref, axes_ref, lifted, devices)
        spot = slice(first * atom_count, (first + group) * atom_count)
        values = lifted[:, spot]
        high = values.astype(BF16)
        low = (values - high.astype(F32)).astype(BF16)
        main = dot(high_ref[:, spot], jnp.concatenate([high, low], axis=0), 1, 1)
        total = total + main[:, : 2 * lanes] + (main[:, 2 * lanes :] + dot(low_ref[:, spot], high, 1, 1))
    return total


SIGNS = ((1.0, 1.0), (1.0, -1.0), (-1.0, 1.0), (-1.0, -1.0))


def wave_blocks(sums_ref, phi_ref):
    _, rows, lanes = phi_ref.shape
    sums = sums_ref[...]
    cos_part, sin_part = sums[:, :lanes], sums[:, lanes:]
    cc_c, cs_c, sc_c, ss_c = (cos_part[p * rows : (p + 1) * rows] for p in range(4))
    cc_s, cs_s, sc_s, ss_s = (sin_part[p * rows : (p + 1) * rows] for p in range(4))
    for sign_id, (s1, s2) in enumerate(SIGNS):
        real = cc_c - s1 * s2 * ss_c - s1 * sc_s - s2 * cs_s
        imag = cc_s - s1 * s2 * ss_s + s1 * sc_c + s2 * cs_c
        phi = phi_ref[sign_id]
        yield s1, s2, phi * real, phi * imag, real, imag


def wave_virial(lengths, sums_ref, phi_ref, width_ref, shape):
    _, rows, lanes = phi_ref.shape
    even = first_odd = second_odd = both_odd = jnp.zeros((rows, lanes), F32)
    for s1, s2, dreal, dimag, real, imag in wave_blocks(sums_ref, phi_ref):
        power = dreal * real + dimag * imag
        even = even + power
        first_odd = first_odd + s1 * power
        second_odd = second_odd + s2 * power
        both_odd = both_odd + s1 * s2 * power
    width = width_ref[0:1, :]
    k1, k2, k3 = grid_numbers(rows, lanes, lengths)

    def total_of(values):
        return jnp.sum(jnp.sum(values, axis=0, keepdims=True), axis=1, keepdims=True)

    energy = 0.5 * total_of(even)
    scaled = width * even
    terms = {
        (0, 0): energy - total_of(k1 * k1 * scaled),
        (1, 1): energy - total_of(k2 * k2 * scaled),
        (2, 2): energy - total_of(k3 * k3 * scaled),
        (0, 1): -total_of(k1 * k2 * width * both_odd),
        (0, 2): -total_of(k1 * k3 * width * first_odd),
        (1, 2): -total_of(k2 * k3 * width * second_odd),
    }
    return virial_row(terms, shape)


def wave_coefficients(sums_ref, phi_ref, coefficients_ref, gradients=False):
    _, rows, lanes = phi_ref.shape
    zero = jnp.zeros((rows, lanes), F32)
    d_cc_c = d_cc_s = d_cs_c = d_cs_s = d_sc_c = d_sc_s = d_ss_c = d_ss_s = zero
    for s1, s2, dreal, dimag, _, _ in wave_blocks(sums_ref, phi_ref):
        d_cc_c, d_ss_c = d_cc_c + dreal, d_ss_c - s1 * s2 * dreal
        d_sc_s, d_cs_s = d_sc_s - s1 * dreal, d_cs_s - s2 * dreal
        d_cc_s, d_ss_s = d_cc_s + dimag, d_ss_s - s1 * s2 * dimag
        d_sc_c, d_cs_c = d_sc_c + s1 * dimag, d_cs_c + s2 * dimag
    values = jnp.concatenate(
        [
            jnp.concatenate(pair, axis=1)
            for pair in ((d_cc_c, d_cc_s), (d_cs_c, d_cs_s), (d_sc_c, d_sc_s), (d_ss_c, d_ss_s))
        ],
        axis=0,
    )
    if gradients:
        cc, cs, sc, ss = (values[p * rows : (p + 1) * rows] for p in range(4))
        row_id = lax.broadcasted_iota(jnp.int32, (rows, 2 * lanes), 0)
        m1 = (row_id // HARMONICS).astype(F32)
        m2 = (row_id % HARMONICS).astype(F32)
        along_x = jnp.concatenate([m1 * sc, m1 * ss, -m1 * cc, -m1 * cs], axis=0)
        along_y = jnp.concatenate([m2 * cs, -m2 * cc, m2 * ss, -m2 * sc], axis=0)
        values = jnp.concatenate([values, along_x, along_y], axis=1)
    turned = values.T
    high = turned.astype(BF16)
    count = turned.shape[0]
    coefficients_ref[0:count, :] = high
    coefficients_ref[count:, :] = (turned - high.astype(F32)).astype(BF16)


def wave_spread(high_ref, low_ref, coefficients):
    values = coefficients[...]
    count = values.shape[0] // 2
    main = dot(values, high_ref[...], 1, 0)
    return main[:count] + (main[count:] + dot(values[:count], low_ref[...], 1, 0))


def wave_features(own_channels, high_ref, low_ref, axes_ref, lifted, coefficients, send_ref):
    chunk, _, atom_count = send_ref.shape
    lanes = own_channels * HARMONICS
    result = wave_spread(high_ref, low_ref, coefficients)
    for index in range(chunk):
        spot = slice(index * atom_count, (index + 1) * atom_count)
        cos_z, sin_z = axes_ref[4, :, spot], axes_ref[5, :, spot]
        for q in range(own_channels):
            a, b = q * HARMONICS, lanes + q * HARMONICS
            piece = result[a : a + HARMONICS, spot] * cos_z + result[b : b + HARMONICS, spot] * sin_z
            send_ref[index, q : q + 1, :] = jnp.sum(piece, axis=0, keepdims=True)


def wave_back(own_channels, lengths, high_ref, low_ref, axes_ref, lifted, coefficients, push_ref):
    chunk, _, atom_count = push_ref.shape
    lanes = own_channels * HARMONICS
    numbers = lax.broadcasted_iota(jnp.int32, (HARMONICS, atom_count), 0).astype(F32) + 1.0
    result = wave_spread(high_ref, low_ref, coefficients)
    for index in range(chunk):
        spot = slice(index * atom_count, (index + 1) * atom_count)
        part = result[:, spot]
        grad_x = jnp.zeros((HARMONICS, atom_count), F32)
        grad_y = grad_x
        grad_z = grad_x
        for q in range(own_channels):
            a, b = q * HARMONICS, lanes + q * HARMONICS
            lift_cos = lifted[a : a + HARMONICS, spot]
            lift_sin = lifted[b : b + HARMONICS, spot]
            grad_z = grad_z + part[b : b + HARMONICS] * lift_cos - part[a : a + HARMONICS] * lift_sin
            a, b = a + 2 * lanes, b + 2 * lanes
            grad_x = grad_x + part[a : a + HARMONICS] * lift_cos + part[b : b + HARMONICS] * lift_sin
            a, b = a + 2 * lanes, b + 2 * lanes
            grad_y = grad_y + part[a : a + HARMONICS] * lift_cos + part[b : b + HARMONICS] * lift_sin
        pieces = (
            grad_x * (2.0 * math.pi / lengths[0]),
            grad_y * (2.0 * math.pi / lengths[1]),
            grad_z * numbers * (2.0 * math.pi / lengths[2]),
        )
        for row, piece in enumerate(pieces):
            push_ref[index, row : row + 1, :] = jnp.sum(piece, axis=0, keepdims=True)


def virial_row(terms, shape):
    lane = lax.broadcasted_iota(jnp.int32, shape, 1)
    row = jnp.zeros(shape, F32)
    for (i, j), value in terms.items():
        spots = (lane == 3 * i + j) | (lane == 3 * j + i)
        row = jnp.where(spots, value, row)
    return row


def short_back_kernel(
    dims,
    recv_ref,
    vec_ref,
    kind_ref,
    dupd_ref,
    slope_ref,
    owner_ref,
    back_ref,
    mix_ref,
    push_ref,
    send_ref,
    fgrad,
    dpool,
    parts,
):
    own_channels, row_count, col_count, species_count, radial_count = dims
    slot_count, atom_count = owner_ref.shape
    channel_count = mix_ref.shape[0]
    device_count = send_ref.shape[0]
    table_rows = round_up(len(DIRECTIONS) + 1, 16)
    for q in range(own_channels):
        low, high = q * device_count, min(channel_count, (q + 1) * device_count)
        fgrad[low:high, :] = recv_ref[0 : high - low, q, :]
    dbefore = (fgrad[...] + dupd_ref[...]) * slope_ref[...]
    daggregate = dot(mix_ref[...], dbefore, 1, 0, GOOD)
    dpool[...] = dot(back_ref[...], daggregate, 1, 0, GOOD)
    vectors = [vec_ref[part] for part in range(3)]
    squared = vectors[0] * vectors[0] + vectors[1] * vectors[1] + vectors[2] * vectors[2]
    kind = kind_ref[...]
    sums = [jnp.zeros(kind.shape, F32) for _ in range(species_count)]
    for order in range(radial_count):
        basis = jnp.exp(squared * (-radial_rate(order)))
        for k in range(species_count):
            spot = k * radial_count + order
            sums[k] = sums[k] + basis * dpool[spot : spot + 1, :]
    slope = jnp.zeros(kind.shape, F32)
    for k in range(species_count):
        slope = jnp.where(kind == float(k), sums[k], slope)
    grads = [slope * vector for vector in vectors]

    def total_of(values):
        return jnp.sum(jnp.sum(values, axis=0, keepdims=True), axis=1, keepdims=True)

    terms = {
        (i, j): -total_of(grads[i] * vectors[j]) for i in range(3) for j in range(i, 3)
    }
    virial = virial_row(terms, (1, atom_count))
    for part in range(3):
        parts[2 * part], parts[2 * part + 1] = split(grads[part])

    sublane = lax.broadcasted_iota(jnp.int32, (atom_count, atom_count), 0)
    table_id = lax.broadcasted_iota(jnp.int32, (table_rows, atom_count), 0)
    group = 8
    scattered = jnp.zeros((atom_count, 6 * table_rows), F32)
    for low in range(0, slot_count, group):
        hots, columns = [], []
        for s in range(low, low + group):
            ids = owner_ref[s : s + 1, :]
            hots.append(jnp.where(sublane == (ids & (atom_count - 1)), 1.0, 0.0).astype(BF16))
            mine = table_id == ids // atom_count
            columns.append(
                jnp.concatenate(
                    [
                        jnp.where(mine, parts[p, s : s + 1, :], 0.0).astype(BF16)
                        for p in range(6)
                    ],
                    axis=0,
                )
            )
        scattered = scattered + dot(
            jnp.concatenate(hots, axis=1), jnp.concatenate(columns, axis=1), 1, 1
        )
    rows = scattered.T
    send_ref[...] = push_ref[...]
    send_ref[:, 3, :] += jnp.broadcast_to(virial, (device_count, atom_count))
    me = neighbour_of((0, 0), row_count, col_count)
    for part in range(3):
        low = 2 * part * table_rows
        both = rows[low : low + table_rows] + rows[low + table_rows : low + 2 * table_rows]
        send_ref[me, part, :] += both[0, :] - jnp.sum(grads[part], axis=0)
        for order, step in enumerate(DIRECTIONS):
            target = neighbour_of(step, row_count, col_count)
            send_ref[target, part, :] += both[1 + order, :]


def final_kernel(volume, recv_ref, forces_ref, virial_ref):
    total = jnp.sum(recv_ref[...], axis=0)
    for part in range(3):
        forces_ref[part] = -total[part : part + 1, :]
    virial = total[3:4, :] * (1.0 / volume)
    for i in range(3):
        virial_ref[i : i + 1, :] = virial[:, 3 * i : 3 * i + 3]


def per_device(
    positions,
    species,
    counts,
    neighbours,
    ghost_index,
    wave_numbers,
    embedding,
    w_radial,
    w_mix,
    w_read,
    w_out,
    amplitude,
    kernel_width,
    filter_gain,
):
    row_count = lax.axis_size("row")
    col_count = lax.axis_size("col")
    device_count = row_count * col_count
    atom_count = positions.shape[3]
    slot_count = neighbours.shape[2]
    direction_count, ghost_count = ghost_index.shape[2:]
    species_count, channel_count = embedding.shape
    radial_count = w_radial.shape[0]
    own_channels = -(-channel_count // device_count)
    lengths = (CELL_EDGE * row_count, CELL_EDGE * col_count, HEIGHT)
    volume = lengths[0] * lengths[1] * lengths[2]
    rows = (KMAX + 1) * HARMONICS
    lanes = own_channels * HARMONICS
    _, shared = direction_slots(row_count, col_count)
    slab_first = round_up(4 + shared, 8)
    slab_features = round_up(own_channels, 4)
    chunk = math.gcd(device_count, 32)
    chunk_count = device_count // chunk

    def exchange(slabs):
        return lax.all_to_all(slabs, AXES, 0, 0, tiled=True)

    def shape(*dims):
        return jax.ShapeDtypeStruct(dims, F32)

    def scratch(*dims):
        return pltpu.VMEM(dims, F32)

    def call(kernel, out_shape, vmem=16, **options):
        return pl.pallas_call(
            kernel,
            out_shape=out_shape,
            compiler_params=pltpu.CompilerParams(vmem_limit_bytes=vmem * 1024 * 1024),
            **options,
        )

    ids = neighbours.reshape(slot_count, atom_count)
    ghosts = ghost_index.reshape(direction_count, ghost_count)
    mesh_counts = (row_count, col_count)
    def fetched(*arrays):
        return [pltpu.with_memory_space_constraint(x, pltpu.HBM) for x in arrays]

    kept = pl.BlockSpec(memory_space=pltpu.HBM)
    near = pl.BlockSpec(memory_space=pltpu.VMEM)
    send, own_kinds = call(
        functools.partial(pack_kernel, mesh_counts),
        (shape(device_count, slab_first, atom_count), shape(1, atom_count)),
        in_specs=[kept] * 3,
        scratch_shapes=[
            scratch(3, 1, atom_count),
            pltpu.VMEM((1, atom_count), jnp.int32),
            pltpu.VMEM(ghosts.shape, jnp.int32),
            pltpu.SemaphoreType.DMA((3,)),
        ],
        name="pack",
    )(*fetched(positions.reshape(3, 1, atom_count), species.reshape(1, atom_count), ghosts))
    cells = exchange(send)

    short_inputs = (
        counts.reshape(1, atom_count),
        ids,
        w_radial,
        embedding,
        w_mix,
        w_read,
        w_out.reshape(1, -1),
    )
    wave_inputs = (filter_gain, wave_numbers, amplitude.reshape(1, -1), kernel_width.reshape(1, -1))
    pooled_rows = species_count * radial_count
    live, ids, _, _, w_mix, w_read, w_out, phi, width, pool, back, mix_turned, initial = call(
        functools.partial(
            prepare_kernel, (device_count, channel_count, own_channels, lengths, volume)
        ),
        tuple(jax.ShapeDtypeStruct(x.shape, x.dtype) for x in short_inputs)
        + (
            shape(4, rows, lanes),
            shape(8, lanes),
            shape(channel_count, round_up(pooled_rows * SUBLANES, channel_count)),
            shape(pooled_rows, channel_count),
            shape(channel_count, channel_count),
            shape(channel_count, atom_count),
        ),
        in_specs=[near] + [kept] * (len(short_inputs) + len(wave_inputs)),
        scratch_shapes=[pltpu.VMEM(x.shape, x.dtype) for x in wave_inputs]
        + [
            scratch(round_up(pooled_rows, 128), channel_count),
            scratch(round_up(species_count, 8), channel_count),
            pltpu.SemaphoreType.DMA((len(short_inputs) + len(wave_inputs),)),
        ],
        cost_estimate=pl.CostEstimate(
            flops=2 * 4 * rows * filter_gain.shape[0] * 3 * lanes,
            bytes_accessed=4 * filter_gain.size,
            transcendentals=0,
        ),
        name="prepare",
    )(own_kinds, *fetched(*short_inputs, *wave_inputs))

    send, vectors, kinds, owners, updated, slope = call(
        functools.partial(
            short_forward_kernel, (own_channels,) + mesh_counts + (species_count, radial_count)
        ),
        (
            shape(device_count, slab_features, atom_count),
            shape(3, slot_count, atom_count),
            shape(slot_count, atom_count),
            jax.ShapeDtypeStruct((slot_count, atom_count), jnp.int32),
            shape(channel_count, atom_count),
            shape(channel_count, atom_count),
        ),
        scratch_shapes=[
            scratch(4, 16, atom_count),
            pltpu.VMEM((direction_count, atom_count), jnp.int32),
            scratch(pooled_rows * SUBLANES, atom_count),
        ],
        name="short_forward",
    )(cells, live, ids, pool, mix_turned, initial)
    send, cells, updated = lax.optimization_barrier((send, cells, updated))
    features = exchange(send)

    axes_block = (6, HARMONICS, chunk * atom_count)
    if chunk_count == 1:
        table_options = {}
    else:
        table_options = dict(
            grid=(chunk_count,),
            in_specs=[pl.BlockSpec((chunk, slab_first, atom_count), lambda i: (i, 0, 0))],
            out_specs=pl.BlockSpec(axes_block, lambda i: (0, 0, i)),
        )
    axes = call(
        functools.partial(table_kernel, (col_count, chunk_count, lengths)),
        shape(6, HARMONICS, device_count * atom_count),
        cost_estimate=pl.CostEstimate(
            flops=2000 * device_count * atom_count, bytes_accessed=200 * device_count * atom_count, transcendentals=0
        ),
        name="tables",
        **table_options,
    )(cells)
    dupd = call(readout_kernel, shape(channel_count, atom_count), name="readout")(
        updated, w_read, w_out
    )

    features, dupd = lax.optimization_barrier((features, dupd))

    plane = pltpu.VMEM((4 * rows, chunk * atom_count), BF16)
    wave_scratch = [plane, plane, scratch(2 * lanes, chunk * atom_count)]
    sums_shape = (4 * rows, 2 * lanes)
    features_block = (chunk, slab_features, atom_count)
    wave_options, force_options = {}, {}
    if chunk_count > 1:
        wave_options = dict(
            grid=(2, chunk_count),
            in_specs=[
                pl.BlockSpec(features_block, lambda p, i: (i, 0, 0)),
                pl.BlockSpec(axes_block, lambda p, i: (0, 0, i)),
                pl.BlockSpec((4, rows, lanes), lambda p, i: (0, 0, 0)),
            ],
            out_specs=(
                pl.BlockSpec(features_block, lambda p, i: (i * p, 0, 0)),
                pl.BlockSpec(sums_shape, lambda p, i: (0, 0)),
            ),
        )
        force_options = dict(
            grid=(chunk_count,),
            in_specs=[
                pl.BlockSpec(features_block, lambda i: (i, 0, 0)),
                pl.BlockSpec(axes_block, lambda i: (0, 0, i)),
                pl.BlockSpec((4, rows, lanes), lambda i: (0, 0, 0)),
                pl.BlockSpec((8, lanes), lambda i: (0, 0)),
                pl.BlockSpec(sums_shape, lambda i: (0, 0)),
            ],
            out_specs=pl.BlockSpec((chunk, 4, atom_count), lambda i: (i, 0, 0)),
        )
    wave_dims = (own_channels, chunk_count, lengths)
    send, sums = call(
        functools.partial(wave_kernel, wave_dims),
        (shape(device_count, slab_features, atom_count), shape(*sums_shape)),
        vmem=20,
        scratch_shapes=wave_scratch + [pltpu.VMEM((4 * lanes, 4 * rows), BF16)],
        name="waves",
        **wave_options,
    )(features, axes, phi)
    gradients = exchange(send)

    push = call(
        functools.partial(wave_force_kernel, wave_dims),
        shape(device_count, 4, atom_count),
        vmem=32,
        scratch_shapes=wave_scratch + [pltpu.VMEM((12 * lanes, 4 * rows), BF16)],
        cost_estimate=pl.CostEstimate(
            flops=24 * lanes * 4 * rows * device_count * atom_count,
            bytes_accessed=200 * device_count * atom_count,
            transcendentals=0,
        ),
        name="wave_forces",
        **force_options,
    )(features, axes, phi, width, sums)

    send = call(
        functools.partial(
            short_back_kernel, (own_channels,) + mesh_counts + (species_count, radial_count)
        ),
        shape(device_count, 4, atom_count),
        scratch_shapes=[
            scratch(channel_count, atom_count),
            scratch(pooled_rows, atom_count),
            scratch(6, slot_count, atom_count),
        ],
        name="short_back",
    )(gradients, vectors, kinds, dupd, slope, owners, back, w_mix, push)
    returned = exchange(send)

    forces, virial = call(
        functools.partial(final_kernel, volume),
        (shape(3, 1, atom_count), shape(3, 3)),
        name="total",
    )(returned)
    return (forces[:, None], virial)


def solution(mesh):
    return jax.shard_map(
        per_device,
        mesh=mesh,
        in_specs=(
            P(None, "row", "col", None),
            P("row", "col", None),
            P("row", "col", None),
            P("row", "col", None, None),
            P("row", "col", None, None),
            P(),
            P(),
            P(),
            P(),
            P(),
            P(),
            P(),
            P(),
            P(),
        ),
        out_specs=(P(None, "row", "col", None), P()),
        check_vma=False,
    )
```

```python
import functools
import math

import jax
import jax.numpy as jnp
from jax import lax
from jax.experimental import pallas as pl
from jax.experimental.pallas import tpu as pltpu
from jax.sharding import PartitionSpec as P

CELL_EDGE = 12.0
HEIGHT = 36.0
KMAX = 6
HARMONICS = 8
EXACT = lax.Precision.HIGHEST
GOOD = lax.Precision.HIGH
DIRECTIONS = ((-1, -1), (-1, 0), (-1, 1), (0, -1), (0, 1), (1, -1), (1, 0), (1, 1))
F32 = jnp.float32
BF16 = jnp.bfloat16
AXES = ("row", "col")


def radial_rate(order):
    return 0.003 * 1.6**order


def round_up(value, step):
    return -(-value // step) * step


def direction_slots(row_count, col_count):
    seen = {}
    slots = []
    for row_step, col_step in DIRECTIONS:
        key = (row_step % row_count, col_step % col_count)
        slots.append(seen.get(key, 0))
        seen[key] = slots[-1] + 1
    return slots, max(seen.values())


def dot(lhs, rhs, lhs_dim, rhs_dim, precision=None):
    return lax.dot_general(
        lhs,
        rhs,
        (((lhs_dim,), (rhs_dim,)), ((), ())),
        precision=precision,
        preferred_element_type=F32,
    )


def split(values):
    high = values.astype(BF16).astype(F32)
    return high, values - high


def wave_weights(dims, gain_ref, waves_ref, amp_ref, width_ref, phi_ref, width_out_ref):
    device_count, channel_count, own_channels, lengths, volume = dims
    me = lax.axis_index("row") * lax.axis_size("col") + lax.axis_index("col")
    wave_count = gain_ref.shape[0]
    rows = (KMAX + 1) * HARMONICS
    lanes = own_channels * HARMONICS
    place = lax.broadcasted_iota(jnp.int32, (8, channel_count), 0) * device_count + me
    chosen = (lax.broadcasted_iota(jnp.int32, (8, channel_count), 1) == place).astype(F32)
    own_gain = dot(chosen, gain_ref[...], 1, 1, EXACT)
    first, second, third = waves_ref[0:1, :], waves_ref[1:2, :], waves_ref[2:3, :]
    sign = jnp.where(first < 0, 2, 0) + jnp.where(second < 0, 1, 0)
    key = sign * rows + jnp.abs(first) * HARMONICS + jnp.abs(second)
    spots = lax.broadcasted_iota(jnp.int32, (4 * rows, wave_count), 0) == key
    onehot = jnp.where(spots, 1.0, 0.0).astype(BF16)
    heights = lax.broadcasted_iota(jnp.int32, (HARMONICS, wave_count), 0) + 1 == third
    blocks = [
        jnp.where(heights, own_gain[q : q + 1, :], 0.0) for q in range(own_channels)
    ]
    wide = jnp.concatenate(blocks, axis=0)
    high = wide.astype(BF16)
    rest = wide - high.astype(F32)
    middle = rest.astype(BF16)
    low = (rest - middle.astype(F32)).astype(BF16)
    summed = dot(onehot, high, 1, 1) + (dot(onehot, middle, 1, 1) + dot(onehot, low, 1, 1))
    lane = lax.broadcasted_iota(jnp.int32, (8, channel_count), 1)
    wanted = jnp.minimum((lane // HARMONICS) * device_count + me, channel_count - 1)
    amp = jnp.take_along_axis(jnp.broadcast_to(amp_ref[...], (8, channel_count)), wanted, axis=1)
    width = jnp.take_along_axis(
        jnp.broadcast_to(width_ref[...], (8, channel_count)), wanted, axis=1
    )
    amp, width = amp[0:1, :lanes], width[0:1, :lanes]
    k1, k2, k3 = grid_numbers(rows, lanes, lengths)
    squared = k1 * k1 + k2 * k2 + k3 * k3
    base = amp * jnp.exp(-width * squared) * (1.0 / volume)
    for sign_id in range(4):
        phi_ref[sign_id] = base * summed[sign_id * rows : (sign_id + 1) * rows, :]
    width_out_ref[...] = jnp.broadcast_to(width, (8, lanes))


def grid_numbers(rows, lanes, lengths):
    row_id = lax.broadcasted_iota(jnp.int32, (rows, lanes), 0)
    lane_id = lax.broadcasted_iota(jnp.int32, (rows, lanes), 1)
    k1 = (row_id // HARMONICS).astype(F32) * (2.0 * math.pi / lengths[0])
    k2 = (row_id % HARMONICS).astype(F32) * (2.0 * math.pi / lengths[1])
    k3 = (lane_id % HARMONICS + 1).astype(F32) * (2.0 * math.pi / lengths[2])
    return k1, k2, k3


def neighbour_of(step, row_count, col_count):
    row = lax.rem(lax.axis_index("row") + step[0] + row_count, row_count)
    col = lax.rem(lax.axis_index("col") + step[1] + col_count, col_count)
    return row * col_count + col


def slab_rows(slab, rows, atom_count):
    width = slab.shape[-1] // atom_count
    return [
        slab[row // width : row // width + 1, row % width * atom_count : (row % width + 1) * atom_count]
        for row in rows
    ]


def pack_kernel(counts, copied, positions_ref, species_ref, ghosts_ref, *refs):
    row_count, col_count = counts
    sources, (send_ref, *targets) = refs[:copied], refs[copied : 2 * copied + 1]
    positions, species, ghosts, first_sems, sems = refs[2 * copied + 1 :]
    firsts = ((positions_ref, positions), (species_ref, species), (ghosts_ref, ghosts))
    firsts = start_copies(firsts, first_sems)
    others = start_copies(tuple(zip(sources, targets)), sems)
    device_count = send_ref.shape[0]
    atom_count = species.shape[1]
    width = send_ref.shape[2] // atom_count
    slots, _ = direction_slots(row_count, col_count)
    for copy in firsts:
        copy.wait()
    rows = [positions[0], positions[1], positions[2], species[...].astype(F32)]
    for row, values in enumerate(rows):
        low = row % width * atom_count
        send_ref[:, row // width, low : low + atom_count] = jnp.broadcast_to(
            values, (device_count, atom_count)
        )
    for order, step in enumerate(DIRECTIONS):
        target = neighbour_of(step, row_count, col_count)
        row = 4 + slots[order]
        low = row % width * atom_count
        send_ref[target, row // width, low : low + atom_count] = ghosts[order, :].astype(F32)
    for copy in others:
        copy.wait()


def start_copies(pairs, sems):
    copies = [
        pltpu.make_async_copy(source, target, sems.at[spot])
        for spot, (source, target) in enumerate(pairs)
    ]
    for copy in copies:
        copy.start()
    return copies


def weights_kernel(
    dims, slot_count, gain_ref, waves_ref, amp_ref, width_ref, radial_ref, embed_ref, phi_ref, width_out_ref, back_ref
):
    species_count, channel_count = embed_ref.shape
    radial_count = radial_ref.shape[0]
    order_id = lax.broadcasted_iota(jnp.int32, (radial_count, channel_count), 0)
    factor = jnp.zeros((radial_count, channel_count), F32)
    for order in range(radial_count):
        factor = jnp.where(order_id == order, -2.0 * radial_rate(order) / slot_count, factor)
    for k in range(species_count):
        back_ref[k * radial_count : (k + 1) * radial_count, :] = (
            radial_ref[...] * embed_ref[k : k + 1, :] * factor
        )
    wave_weights(dims, gain_ref, waves_ref, amp_ref, width_ref, phi_ref, width_out_ref)


def short_forward_kernel(
    dims,
    cells_ref,
    counts_ref,
    ids_ref,
    radial_ref,
    embed_ref,
    mix_ref,
    send_ref,
    vec_ref,
    kind_ref,
    owner_ref,
    upd_ref,
    slope_ref,
    table,
    lists,
    codes,
    pooled,
    weights,
    kinds8,
):
    own_channels, row_count, col_count = dims
    slot_count, atom_count = ids_ref.shape
    species_count, channel_count = embed_ref.shape
    radial_count = radial_ref.shape[0]
    device_count = send_ref.shape[0]
    slots, _ = direction_slots(row_count, col_count)
    own = slab_rows(cells_ref[neighbour_of((0, 0), row_count, col_count)], range(4), atom_count)
    for part in range(4):
        table[part, 0:1, :] = own[part]
    for order, step in enumerate(DIRECTIONS):
        source = neighbour_of(step, row_count, col_count)
        list_row = 4 + slots[len(DIRECTIONS) - 1 - order]
        block = slab_rows(cells_ref[source], (0, 1, 2, 3, list_row), atom_count)
        row = slice(8 + order, 9 + order)
        table[0, row, :] = block[0] + step[0] * CELL_EDGE
        table[1, row, :] = block[1] + step[1] * CELL_EDGE
        table[2, row, :] = block[2]
        table[3, row, :] = block[3]
        lists[order : order + 1, :] = block[4].astype(jnp.int32)
    picks = lists[...]
    for part in range(4):
        table[part, 8:16, :] = jnp.take_along_axis(table[part, 8:16, :], picks, axis=1)
    codes[8:16, :] = picks + atom_count * table[3, 8:16, :].astype(jnp.int32)
    codes[0:1, :] = lax.broadcasted_iota(
        jnp.int32, (1, atom_count), 1
    ) + atom_count * own[3].astype(jnp.int32)

    ids = ids_ref[...]
    lane = ids & (atom_count - 1)
    source = ids // atom_count
    here = [source == order + 1 for order in range(len(DIRECTIONS))]

    def picked(ref):
        values = jnp.take_along_axis(jnp.broadcast_to(ref[0:1, :], ids.shape), lane, axis=1)
        for order in range(len(DIRECTIONS)):
            wide = jnp.broadcast_to(ref[8 + order : 9 + order, :], ids.shape)
            values = jnp.where(here[order], jnp.take_along_axis(wide, lane, axis=1), values)
        return values

    gathered = [picked(table.at[part]) for part in range(3)]
    code = picked(codes)
    owner_ref[...] = (code & (atom_count - 1)) + source * atom_count
    gathered.append((code // atom_count).astype(F32))
    slot = lax.broadcasted_iota(jnp.int32, ids.shape, 0)
    kind = jnp.where(slot < counts_ref[...], gathered[3], -1.0)
    kind_ref[...] = kind
    squared = jnp.zeros(ids.shape, F32)
    for part in range(3):
        vector = gathered[part] - own[part]
        vec_ref[part] = vector
        squared = squared + vector * vector
    masks = [kind == float(k) for k in range(species_count)]
    for order in range(radial_count):
        basis = jnp.exp(squared * (-radial_rate(order)))
        for k in range(species_count):
            spot = k * radial_count + order
            pooled[spot : spot + 1, :] = jnp.sum(
                jnp.where(masks[k], basis, 0.0), axis=0, keepdims=True
            )
    for k in range(species_count):
        weights[k * radial_count : (k + 1) * radial_count, :] = (
            radial_ref[...] * embed_ref[k : k + 1, :] * (1.0 / slot_count)
        )
    kinds8[...] = jnp.zeros_like(kinds8)
    kinds8[0:species_count, :] = embed_ref[...]
    own_hot = (
        lax.broadcasted_iota(jnp.int32, (kinds8.shape[0], atom_count), 0).astype(F32) == own[3]
    ).astype(F32)
    initial = dot(kinds8[...], own_hot, 0, 0, EXACT)
    aggregate = dot(weights[...], pooled[...], 0, 0, GOOD)
    before = dot(mix_ref[...], aggregate, 0, 0, GOOD)
    gate = 1.0 / (1.0 + jnp.exp(-before))
    updated = initial + before * gate
    slope_ref[...] = gate + before * gate * (1.0 - gate)
    for q in range(own_channels):
        low, high = q * device_count, min(channel_count, (q + 1) * device_count)
        send_ref[0 : high - low, q, :] = updated[low:high, :]
        if high - low < device_count:
            send_ref[high - low :, q, :] = jnp.zeros(
                (device_count - (high - low), atom_count), F32
            )
    upd_ref[...] = updated


def readout_kernel(upd_ref, read_ref, out_ref, dupd_ref):
    channel_count, atom_count = upd_ref.shape
    readout = dot(read_ref[...], upd_ref[...], 0, 0, GOOD)
    gate = 1.0 / (1.0 + jnp.exp(-readout))
    scale = jnp.broadcast_to(out_ref[...], (channel_count, channel_count)).T
    dread = scale[:, 0:atom_count] * (gate + readout * gate * (1.0 - gate))
    dupd_ref[...] = dot(read_ref[...], dread, 1, 0, GOOD)


def turn_tables(turns, multiples):
    angle = turns * multiples
    halves = jnp.floor(2.0 * angle + 0.5)
    rest = angle - 0.5 * halves
    sign = 1.0 - 2.0 * (halves - 2.0 * jnp.floor(0.5 * halves))
    square = rest * rest

    def series(first, last):
        terms = [
            (-1.0) ** (p // 2) * (2.0 * math.pi) ** p / math.factorial(p)
            for p in range(first, last + 1, 2)
        ]
        total = jnp.full_like(square, terms[-1])
        for term in reversed(terms[:-1]):
            total = total * square + term
        return total

    return sign * series(0, 12), sign * rest * series(1, 13)


def table_kernel(dims, cells_ref, axes_ref):
    col_count, chunk_count, lengths = dims
    chunk = cells_ref.shape[0]
    atom_count = axes_ref.shape[2] // chunk
    first_device = pl.program_id(0) * chunk if chunk_count > 1 else 0
    multiples = lax.broadcasted_iota(jnp.int32, (HARMONICS, atom_count), 0).astype(F32)

    def one(index, _):
        device = first_device + index
        spot = pl.ds(pl.multiple_of(index * atom_count, atom_count), atom_count)
        block = slab_rows(cells_ref[index], range(3), atom_count)
        corner_row = (device // col_count).astype(F32) * CELL_EDGE
        corner_col = (device % col_count).astype(F32) * CELL_EDGE
        turns = (
            (block[0] + corner_row) * (1.0 / lengths[0]),
            (block[1] + corner_col) * (1.0 / lengths[1]),
            block[2] * (1.0 / lengths[2]),
        )
        for axis in range(3):
            numbers = multiples + 1.0 if axis == 2 else multiples
            cos, sin = turn_tables(turns[axis], numbers)
            axes_ref[2 * axis, :, spot] = cos
            axes_ref[2 * axis + 1, :, spot] = sin
        return 0

    lax.fori_loop(0, chunk, one, 0, unroll=4)


def wave_kernel(dims, recv_ref, axes_ref, phi_ref, send_ref, sums, high, low, lifted, coefficients):
    own_channels, chunk_count, lengths = dims
    planes = (high, low, axes_ref, lifted)
    if chunk_count == 1:
        sums[...] = wave_sums(own_channels, recv_ref, *planes)
        wave_coefficients(sums, phi_ref, coefficients)
        wave_features(own_channels, *planes, coefficients, send_ref)
        return
    phase, chunk_id = pl.program_id(0), pl.program_id(1)

    @pl.when((phase == 0) & (chunk_id == 0))
    def _():
        sums[...] = jnp.zeros_like(sums)

    part = wave_sums(own_channels, recv_ref, *planes)

    @pl.when(phase == 0)
    def _():
        sums[...] += part

    @pl.when((phase == 1) & (chunk_id == 0))
    def _():
        wave_coefficients(sums, phi_ref, coefficients)

    @pl.when(phase == 1)
    def _():
        wave_features(own_channels, *planes, coefficients, send_ref)


def wave_force_kernel(
    dims, recv_ref, axes_ref, phi_ref, width_ref, sums, push_ref, high, low, lifted, coefficients
):
    own_channels, chunk_count, lengths = dims
    planes = (high, low, axes_ref, lifted)
    wave_planes(own_channels, recv_ref, *planes)
    if chunk_count == 1:
        wave_coefficients(sums, phi_ref, coefficients, True)
    else:

        @pl.when(pl.program_id(0) == 0)
        def _():
            wave_coefficients(sums, phi_ref, coefficients, True)

    wave_back(own_channels, lengths, *planes, coefficients, push_ref)
    virial = wave_virial(lengths, sums, phi_ref, width_ref, (1, push_ref.shape[2]))
    push_ref[:, 3, :] = jnp.broadcast_to(virial, (push_ref.shape[0], push_ref.shape[2]))


def wave_planes(own_channels, recv_ref, high_ref, low_ref, axes_ref, lifted, devices=None):
    chunk, _, atom_count = recv_ref.shape
    lanes = own_channels * HARMONICS
    for index in devices or range(chunk):
        spot = slice(index * atom_count, (index + 1) * atom_count)
        for q in range(own_channels):
            feature = recv_ref[index, q : q + 1, :]
            for part in range(2):
                row = part * lanes + q * HARMONICS
                lifted[row : row + HARMONICS, spot] = feature * axes_ref[4 + part, :, spot]
        products = [
            axes_ref[first_axis, m : m + 1, spot] * axes_ref[second_axis, :, spot]
            for first_axis, second_axis in ((0, 2), (0, 3), (1, 2), (1, 3))
            for m in range(KMAX + 1)
        ]
        for pair in range(len(products) // 2):
            both = jnp.concatenate(products[2 * pair : 2 * pair + 2], axis=0)
            high = both.astype(BF16)
            rows = slice(2 * HARMONICS * pair, 2 * HARMONICS * (pair + 1))
            high_ref[rows, spot] = high
            low_ref[rows, spot] = (both - high.astype(F32)).astype(BF16)


def wave_sums(own_channels, recv_ref, high_ref, low_ref, axes_ref, lifted):
    chunk, _, atom_count = recv_ref.shape
    lanes = own_channels * HARMONICS
    group = math.gcd(chunk, 16)
    total = 0.0
    for first in range(0, chunk, group):
        devices = range(first, first + group)
        wave_planes(own_channels, recv_ref, high_ref, low_ref, axes_ref, lifted, devices)
        spot = slice(first * atom_count, (first + group) * atom_count)
        values = lifted[:, spot]
        high = values.astype(BF16)
        low = (values - high.astype(F32)).astype(BF16)
        main = dot(high_ref[:, spot], jnp.concatenate([high, low], axis=0), 1, 1)
        total = total + main[:, : 2 * lanes] + (main[:, 2 * lanes :] + dot(low_ref[:, spot], high, 1, 1))
    return total


SIGNS = ((1.0, 1.0), (1.0, -1.0), (-1.0, 1.0), (-1.0, -1.0))


def wave_blocks(sums_ref, phi_ref):
    _, rows, lanes = phi_ref.shape
    sums = sums_ref[...]
    cos_part, sin_part = sums[:, :lanes], sums[:, lanes:]
    cc_c, cs_c, sc_c, ss_c = (cos_part[p * rows : (p + 1) * rows] for p in range(4))
    cc_s, cs_s, sc_s, ss_s = (sin_part[p * rows : (p + 1) * rows] for p in range(4))
    for sign_id, (s1, s2) in enumerate(SIGNS):
        real = cc_c - s1 * s2 * ss_c - s1 * sc_s - s2 * cs_s
        imag = cc_s - s1 * s2 * ss_s + s1 * sc_c + s2 * cs_c
        phi = phi_ref[sign_id]
        yield s1, s2, phi * real, phi * imag, real, imag


def wave_virial(lengths, sums_ref, phi_ref, width_ref, shape):
    _, rows, lanes = phi_ref.shape
    even = first_odd = second_odd = both_odd = jnp.zeros((rows, lanes), F32)
    for s1, s2, dreal, dimag, real, imag in wave_blocks(sums_ref, phi_ref):
        power = dreal * real + dimag * imag
        even = even + power
        first_odd = first_odd + s1 * power
        second_odd = second_odd + s2 * power
        both_odd = both_odd + s1 * s2 * power
    width = width_ref[0:1, :]
    k1, k2, k3 = grid_numbers(rows, lanes, lengths)

    def total_of(values):
        return jnp.sum(jnp.sum(values, axis=0, keepdims=True), axis=1, keepdims=True)

    energy = 0.5 * total_of(even)
    scaled = width * even
    terms = {
        (0, 0): energy - total_of(k1 * k1 * scaled),
        (1, 1): energy - total_of(k2 * k2 * scaled),
        (2, 2): energy - total_of(k3 * k3 * scaled),
        (0, 1): -total_of(k1 * k2 * width * both_odd),
        (0, 2): -total_of(k1 * k3 * width * first_odd),
        (1, 2): -total_of(k2 * k3 * width * second_odd),
    }
    return virial_row(terms, shape)


def wave_coefficients(sums_ref, phi_ref, coefficients_ref, gradients=False):
    _, rows, lanes = phi_ref.shape
    zero = jnp.zeros((rows, lanes), F32)
    d_cc_c = d_cc_s = d_cs_c = d_cs_s = d_sc_c = d_sc_s = d_ss_c = d_ss_s = zero
    for s1, s2, dreal, dimag, _, _ in wave_blocks(sums_ref, phi_ref):
        d_cc_c, d_ss_c = d_cc_c + dreal, d_ss_c - s1 * s2 * dreal
        d_sc_s, d_cs_s = d_sc_s - s1 * dreal, d_cs_s - s2 * dreal
        d_cc_s, d_ss_s = d_cc_s + dimag, d_ss_s - s1 * s2 * dimag
        d_sc_c, d_cs_c = d_sc_c + s1 * dimag, d_cs_c + s2 * dimag
    values = jnp.concatenate(
        [
            jnp.concatenate(pair, axis=1)
            for pair in ((d_cc_c, d_cc_s), (d_cs_c, d_cs_s), (d_sc_c, d_sc_s), (d_ss_c, d_ss_s))
        ],
        axis=0,
    )
    if gradients:
        cc, cs, sc, ss = (values[p * rows : (p + 1) * rows] for p in range(4))
        row_id = lax.broadcasted_iota(jnp.int32, (rows, 2 * lanes), 0)
        m1 = (row_id // HARMONICS).astype(F32)
        m2 = (row_id % HARMONICS).astype(F32)
        along_x = jnp.concatenate([m1 * sc, m1 * ss, -m1 * cc, -m1 * cs], axis=0)
        along_y = jnp.concatenate([m2 * cs, -m2 * cc, m2 * ss, -m2 * sc], axis=0)
        values = jnp.concatenate([values, along_x, along_y], axis=1)
    turned = values.T
    high = turned.astype(BF16)
    count = turned.shape[0]
    coefficients_ref[0:count, :] = high
    coefficients_ref[count:, :] = (turned - high.astype(F32)).astype(BF16)


def wave_spread(high_ref, low_ref, coefficients):
    values = coefficients[...]
    count = values.shape[0] // 2
    main = dot(values, high_ref[...], 1, 0)
    return main[:count] + (main[count:] + dot(values[:count], low_ref[...], 1, 0))


def wave_features(own_channels, high_ref, low_ref, axes_ref, lifted, coefficients, send_ref):
    chunk, _, atom_count = send_ref.shape
    lanes = own_channels * HARMONICS
    result = wave_spread(high_ref, low_ref, coefficients)
    for index in range(chunk):
        spot = slice(index * atom_count, (index + 1) * atom_count)
        cos_z, sin_z = axes_ref[4, :, spot], axes_ref[5, :, spot]
        for q in range(own_channels):
            a, b = q * HARMONICS, lanes + q * HARMONICS
            piece = result[a : a + HARMONICS, spot] * cos_z + result[b : b + HARMONICS, spot] * sin_z
            send_ref[index, q : q + 1, :] = jnp.sum(piece, axis=0, keepdims=True)


def wave_back(own_channels, lengths, high_ref, low_ref, axes_ref, lifted, coefficients, push_ref):
    chunk, _, atom_count = push_ref.shape
    lanes = own_channels * HARMONICS
    numbers = lax.broadcasted_iota(jnp.int32, (HARMONICS, atom_count), 0).astype(F32) + 1.0
    result = wave_spread(high_ref, low_ref, coefficients)
    for index in range(chunk):
        spot = slice(index * atom_count, (index + 1) * atom_count)
        part = result[:, spot]
        grad_x = jnp.zeros((HARMONICS, atom_count), F32)
        grad_y = grad_x
        grad_z = grad_x
        for q in range(own_channels):
            a, b = q * HARMONICS, lanes + q * HARMONICS
            lift_cos = lifted[a : a + HARMONICS, spot]
            lift_sin = lifted[b : b + HARMONICS, spot]
            grad_z = grad_z + part[b : b + HARMONICS] * lift_cos - part[a : a + HARMONICS] * lift_sin
            a, b = a + 2 * lanes, b + 2 * lanes
            grad_x = grad_x + part[a : a + HARMONICS] * lift_cos + part[b : b + HARMONICS] * lift_sin
            a, b = a + 2 * lanes, b + 2 * lanes
            grad_y = grad_y + part[a : a + HARMONICS] * lift_cos + part[b : b + HARMONICS] * lift_sin
        pieces = (
            grad_x * (2.0 * math.pi / lengths[0]),
            grad_y * (2.0 * math.pi / lengths[1]),
            grad_z * numbers * (2.0 * math.pi / lengths[2]),
        )
        for row, piece in enumerate(pieces):
            push_ref[index, row : row + 1, :] = jnp.sum(piece, axis=0, keepdims=True)


def virial_row(terms, shape):
    lane = lax.broadcasted_iota(jnp.int32, shape, 1)
    row = jnp.zeros(shape, F32)
    for (i, j), value in terms.items():
        spots = (lane == 3 * i + j) | (lane == 3 * j + i)
        row = jnp.where(spots, value, row)
    return row


def short_back_kernel(
    dims,
    recv_ref,
    vec_ref,
    kind_ref,
    dupd_ref,
    slope_ref,
    owner_ref,
    back_ref,
    mix_ref,
    push_ref,
    send_ref,
    fgrad,
    dpool,
    parts,
):
    own_channels, row_count, col_count, species_count, radial_count = dims
    slot_count, atom_count = owner_ref.shape
    channel_count = mix_ref.shape[0]
    device_count = send_ref.shape[0]
    table_rows = round_up(len(DIRECTIONS) + 1, 16)
    for q in range(own_channels):
        low, high = q * device_count, min(channel_count, (q + 1) * device_count)
        fgrad[low:high, :] = recv_ref[0 : high - low, q, :]
    dbefore = (fgrad[...] + dupd_ref[...]) * slope_ref[...]
    daggregate = dot(mix_ref[...], dbefore, 1, 0, GOOD)
    dpool[...] = dot(back_ref[...], daggregate, 1, 0, GOOD)
    vectors = [vec_ref[part] for part in range(3)]
    squared = vectors[0] * vectors[0] + vectors[1] * vectors[1] + vectors[2] * vectors[2]
    kind = kind_ref[...]
    sums = [jnp.zeros(kind.shape, F32) for _ in range(species_count)]
    for order in range(radial_count):
        basis = jnp.exp(squared * (-radial_rate(order)))
        for k in range(species_count):
            spot = k * radial_count + order
            sums[k] = sums[k] + basis * dpool[spot : spot + 1, :]
    slope = jnp.zeros(kind.shape, F32)
    for k in range(species_count):
        slope = jnp.where(kind == float(k), sums[k], slope)
    grads = [slope * vector for vector in vectors]

    def total_of(values):
        return jnp.sum(jnp.sum(values, axis=0, keepdims=True), axis=1, keepdims=True)

    terms = {
        (i, j): -total_of(grads[i] * vectors[j]) for i in range(3) for j in range(i, 3)
    }
    virial = virial_row(terms, (1, atom_count))
    for part in range(3):
        parts[2 * part], parts[2 * part + 1] = split(grads[part])

    sublane = lax.broadcasted_iota(jnp.int32, (atom_count, atom_count), 0)
    table_id = lax.broadcasted_iota(jnp.int32, (table_rows, atom_count), 0)
    group = 8
    scattered = jnp.zeros((atom_count, 6 * table_rows), F32)
    for low in range(0, slot_count, group):
        hots, columns = [], []
        for s in range(low, low + group):
            ids = owner_ref[s : s + 1, :]
            hots.append(jnp.where(sublane == (ids & (atom_count - 1)), 1.0, 0.0).astype(BF16))
            mine = table_id == ids // atom_count
            columns.append(
                jnp.concatenate(
                    [
                        jnp.where(mine, parts[p, s : s + 1, :], 0.0).astype(BF16)
                        for p in range(6)
                    ],
                    axis=0,
                )
            )
        scattered = scattered + dot(
            jnp.concatenate(hots, axis=1), jnp.concatenate(columns, axis=1), 1, 1
        )
    rows = scattered.T
    send_ref[...] = push_ref[...]
    send_ref[:, 3, :] += jnp.broadcast_to(virial, (device_count, atom_count))
    me = neighbour_of((0, 0), row_count, col_count)
    for part in range(3):
        low = 2 * part * table_rows
        both = rows[low : low + table_rows] + rows[low + table_rows : low + 2 * table_rows]
        send_ref[me, part, :] += both[0, :] - jnp.sum(grads[part], axis=0)
        for order, step in enumerate(DIRECTIONS):
            target = neighbour_of(step, row_count, col_count)
            send_ref[target, part, :] += both[1 + order, :]


def final_kernel(volume, recv_ref, forces_ref, virial_ref):
    total = jnp.sum(recv_ref[...], axis=0)
    for part in range(3):
        forces_ref[part] = -total[part : part + 1, :]
    virial = total[3:4, :] * (1.0 / volume)
    for i in range(3):
        virial_ref[i : i + 1, :] = virial[:, 3 * i : 3 * i + 3]


def per_device(
    positions,
    species,
    counts,
    neighbours,
    ghost_index,
    wave_numbers,
    embedding,
    w_radial,
    w_mix,
    w_read,
    w_out,
    amplitude,
    kernel_width,
    filter_gain,
):
    row_count = lax.axis_size("row")
    col_count = lax.axis_size("col")
    device_count = row_count * col_count
    atom_count = positions.shape[3]
    slot_count = neighbours.shape[2]
    direction_count, ghost_count = ghost_index.shape[2:]
    species_count, channel_count = embedding.shape
    radial_count = w_radial.shape[0]
    own_channels = -(-channel_count // device_count)
    lengths = (CELL_EDGE * row_count, CELL_EDGE * col_count, HEIGHT)
    volume = lengths[0] * lengths[1] * lengths[2]
    rows = (KMAX + 1) * HARMONICS
    lanes = own_channels * HARMONICS
    _, shared = direction_slots(row_count, col_count)
    slab_first = round_up(4 + shared, 2) // 2 * atom_count
    slab_features = round_up(own_channels, 4)
    chunk = math.gcd(device_count, 32)
    chunk_count = device_count // chunk

    def exchange(slabs):
        return lax.all_to_all(slabs, AXES, 0, 0, tiled=True)

    def shape(*dims):
        return jax.ShapeDtypeStruct(dims, F32)

    def scratch(*dims):
        return pltpu.VMEM(dims, F32)

    def call(kernel, out_shape, vmem=16, **options):
        return pl.pallas_call(
            kernel,
            out_shape=out_shape,
            compiler_params=pltpu.CompilerParams(vmem_limit_bytes=vmem * 1024 * 1024),
            **options,
        )

    ids = neighbours.reshape(slot_count, atom_count)
    ghosts = ghost_index.reshape(direction_count, ghost_count)
    mesh_counts = (row_count, col_count)
    inputs = (
        counts.reshape(1, atom_count),
        ids,
        w_radial,
        embedding,
        w_mix,
        w_read,
        w_out.reshape(1, -1),
        filter_gain,
        wave_numbers,
        amplitude.reshape(1, -1),
        kernel_width.reshape(1, -1),
    )
    send, *inputs = call(
        functools.partial(pack_kernel, mesh_counts, len(inputs)),
        (shape(device_count, 2, slab_first),)
        + tuple(jax.ShapeDtypeStruct(x.shape, x.dtype) for x in inputs),
        in_specs=[pl.BlockSpec(memory_space=pltpu.HBM)] * (3 + len(inputs)),
        scratch_shapes=[
            scratch(3, 1, atom_count),
            pltpu.VMEM((1, atom_count), jnp.int32),
            pltpu.VMEM(ghosts.shape, jnp.int32),
            pltpu.SemaphoreType.DMA((3,)),
            pltpu.SemaphoreType.DMA((len(inputs),)),
        ],
        name="pack",
    )(
        *[
            pltpu.with_memory_space_constraint(x, pltpu.HBM)
            for x in (positions.reshape(3, 1, atom_count), species.reshape(1, atom_count), ghosts, *inputs)
        ]
    )
    live, ids, w_radial, embedding, w_mix, w_read, w_out, *wave_inputs = inputs
    cells = exchange(send)

    pooled_rows = species_count * radial_count
    send, vectors, kinds, owners, updated, slope = call(
        functools.partial(short_forward_kernel, (own_channels,) + mesh_counts),
        (
            shape(device_count, slab_features, atom_count),
            shape(3, slot_count, atom_count),
            shape(slot_count, atom_count),
            jax.ShapeDtypeStruct((slot_count, atom_count), jnp.int32),
            shape(channel_count, atom_count),
            shape(channel_count, atom_count),
        ),
        scratch_shapes=[
            scratch(4, 16, atom_count),
            pltpu.VMEM((direction_count, atom_count), jnp.int32),
            pltpu.VMEM((16, atom_count), jnp.int32),
            scratch(pooled_rows, atom_count),
            scratch(pooled_rows, channel_count),
            scratch(round_up(species_count, 8), channel_count),
        ],
        name="short_forward",
    )(cells, live, ids, w_radial, embedding, w_mix)
    send, cells, updated, *wave_inputs = lax.optimization_barrier((send, cells, updated, *wave_inputs))
    features = exchange(send)

    phi, width, back = call(
        functools.partial(
            weights_kernel, (device_count, channel_count, own_channels, lengths, volume), slot_count
        ),
        (shape(4, rows, lanes), shape(8, lanes), shape(pooled_rows, channel_count)),
        cost_estimate=pl.CostEstimate(
            flops=2 * 4 * rows * filter_gain.shape[0] * 3 * lanes,
            bytes_accessed=4 * filter_gain.size,
            transcendentals=0,
        ),
        name="weights",
    )(*wave_inputs, w_radial, embedding)

    axes_block = (6, HARMONICS, chunk * atom_count)
    if chunk_count == 1:
        table_options = {}
    else:
        table_options = dict(
            grid=(chunk_count,),
            in_specs=[pl.BlockSpec((chunk, 2, slab_first), lambda i: (i, 0, 0))],
            out_specs=pl.BlockSpec(axes_block, lambda i: (0, 0, i)),
        )
    axes = call(
        functools.partial(table_kernel, (col_count, chunk_count, lengths)),
        shape(6, HARMONICS, device_count * atom_count),
        cost_estimate=pl.CostEstimate(
            flops=2000 * device_count * atom_count, bytes_accessed=200 * device_count * atom_count, transcendentals=0
        ),
        name="tables",
        **table_options,
    )(cells)
    dupd = call(readout_kernel, shape(channel_count, atom_count), name="readout")(
        updated, w_read, w_out
    )

    features, dupd, phi = lax.optimization_barrier((features, dupd, phi))

    plane = pltpu.VMEM((4 * rows, chunk * atom_count), BF16)
    wave_scratch = [plane, plane, scratch(2 * lanes, chunk * atom_count)]
    sums_shape = (4 * rows, 2 * lanes)
    features_block = (chunk, slab_features, atom_count)
    wave_options, force_options = {}, {}
    if chunk_count > 1:
        wave_options = dict(
            grid=(2, chunk_count),
            in_specs=[
                pl.BlockSpec(features_block, lambda p, i: (i, 0, 0)),
                pl.BlockSpec(axes_block, lambda p, i: (0, 0, i)),
                pl.BlockSpec((4, rows, lanes), lambda p, i: (0, 0, 0)),
            ],
            out_specs=(
                pl.BlockSpec(features_block, lambda p, i: (i * p, 0, 0)),
                pl.BlockSpec(sums_shape, lambda p, i: (0, 0)),
            ),
        )
        force_options = dict(
            grid=(chunk_count,),
            in_specs=[
                pl.BlockSpec(features_block, lambda i: (i, 0, 0)),
                pl.BlockSpec(axes_block, lambda i: (0, 0, i)),
                pl.BlockSpec((4, rows, lanes), lambda i: (0, 0, 0)),
                pl.BlockSpec((8, lanes), lambda i: (0, 0)),
                pl.BlockSpec(sums_shape, lambda i: (0, 0)),
            ],
            out_specs=pl.BlockSpec((chunk, 4, atom_count), lambda i: (i, 0, 0)),
        )
    wave_dims = (own_channels, chunk_count, lengths)
    send, sums = call(
        functools.partial(wave_kernel, wave_dims),
        (shape(device_count, slab_features, atom_count), shape(*sums_shape)),
        vmem=20,
        scratch_shapes=wave_scratch + [pltpu.VMEM((4 * lanes, 4 * rows), BF16)],
        name="waves",
        **wave_options,
    )(features, axes, phi)
    gradients = exchange(send)

    push = call(
        functools.partial(wave_force_kernel, wave_dims),
        shape(device_count, 4, atom_count),
        vmem=32,
        scratch_shapes=wave_scratch + [pltpu.VMEM((12 * lanes, 4 * rows), BF16)],
        cost_estimate=pl.CostEstimate(
            flops=24 * lanes * 4 * rows * device_count * atom_count,
            bytes_accessed=200 * device_count * atom_count,
            transcendentals=0,
        ),
        name="wave_forces",
        **force_options,
    )(features, axes, phi, width, sums)

    send = call(
        functools.partial(
            short_back_kernel, (own_channels,) + mesh_counts + (species_count, radial_count)
        ),
        shape(device_count, 4, atom_count),
        scratch_shapes=[
            scratch(channel_count, atom_count),
            scratch(pooled_rows, atom_count),
            scratch(6, slot_count, atom_count),
        ],
        name="short_back",
    )(gradients, vectors, kinds, dupd, slope, owners, back, w_mix, push)
    returned = exchange(send)

    forces, virial = call(
        functools.partial(final_kernel, volume),
        (shape(3, 1, atom_count), shape(3, 3)),
        name="total",
    )(returned)
    return (forces[:, None], virial)


def solution(mesh):
    return jax.shard_map(
        per_device,
        mesh=mesh,
        in_specs=(
            P(None, "row", "col", None),
            P("row", "col", None),
            P("row", "col", None),
            P("row", "col", None, None),
            P("row", "col", None, None),
            P(),
            P(),
            P(),
            P(),
            P(),
            P(),
            P(),
            P(),
            P(),
        ),
        out_specs=(P(None, "row", "col", None), P()),
        check_vma=False,
    )
```

```python
import functools
import math

import jax
import jax.numpy as jnp
from jax import lax
from jax.experimental import pallas as pl
from jax.experimental.pallas import tpu as pltpu
from jax.sharding import PartitionSpec as P

CELL_EDGE = 12.0
HEIGHT = 36.0
KMAX = 6
HARMONICS = 8
EXACT = lax.Precision.HIGHEST
GOOD = lax.Precision.HIGH
DIRECTIONS = ((-1, -1), (-1, 0), (-1, 1), (0, -1), (0, 1), (1, -1), (1, 0), (1, 1))
F32 = jnp.float32
BF16 = jnp.bfloat16
AXES = ("row", "col")


def radial_rate(order):
    return 0.003 * 1.6**order


def round_up(value, step):
    return -(-value // step) * step


def direction_slots(row_count, col_count):
    seen = {}
    slots = []
    for row_step, col_step in DIRECTIONS:
        key = (row_step % row_count, col_step % col_count)
        slots.append(seen.get(key, 0))
        seen[key] = slots[-1] + 1
    return slots, max(seen.values())


def tile_layout(own_channels):
    shared = HARMONICS // own_channels
    return shared, -(-KMAX // shared)


def dot(lhs, rhs, lhs_dim, rhs_dim, precision=None):
    return lax.dot_general(
        lhs,
        rhs,
        (((lhs_dim,), (rhs_dim,)), ((), ())),
        precision=precision,
        preferred_element_type=F32,
    )


def split(values):
    high = values.astype(BF16).astype(F32)
    return high, values - high


def wave_weights(dims, gain_ref, waves_ref, amp_ref, width_ref, phi_ref, width_out_ref):
    device_count, channel_count, own_channels, lengths, volume = dims
    me = lax.axis_index("row") * lax.axis_size("col") + lax.axis_index("col")
    wave_count = gain_ref.shape[0]
    rows = (KMAX + 1) * HARMONICS
    together, tiles = tile_layout(own_channels)
    lanes = tiles * HARMONICS
    place = lax.broadcasted_iota(jnp.int32, (8, channel_count), 0) * device_count + me
    chosen = (lax.broadcasted_iota(jnp.int32, (8, channel_count), 1) == place).astype(F32)
    own_gain = dot(chosen, gain_ref[...], 1, 1, EXACT)
    first, second, third = waves_ref[0:1, :], waves_ref[1:2, :], waves_ref[2:3, :]
    sign = jnp.where(first < 0, 2, 0) + jnp.where(second < 0, 1, 0)
    key = sign * rows + jnp.abs(first) * HARMONICS + jnp.abs(second)
    spots = lax.broadcasted_iota(jnp.int32, (4 * rows, wave_count), 0) == key
    onehot = jnp.where(spots, 1.0, 0.0).astype(BF16)
    mine = jnp.concatenate([own_gain[:own_channels]] * together, axis=0)
    height = lax.broadcasted_iota(jnp.int32, (HARMONICS, wave_count), 0) // own_channels + 1
    blocks = [jnp.where(height + tile * together == third, mine, 0.0) for tile in range(tiles)]
    wide = jnp.concatenate(blocks, axis=0)
    high = wide.astype(BF16)
    rest = wide - high.astype(F32)
    middle = rest.astype(BF16)
    low = (rest - middle.astype(F32)).astype(BF16)
    summed = dot(onehot, high, 1, 1) + (dot(onehot, middle, 1, 1) + dot(onehot, low, 1, 1))
    lane = lax.broadcasted_iota(jnp.int32, (8, channel_count), 1)
    wanted = jnp.minimum(lane % own_channels * device_count + me, channel_count - 1)
    amp = jnp.take_along_axis(jnp.broadcast_to(amp_ref[...], (8, channel_count)), wanted, axis=1)
    width = jnp.take_along_axis(
        jnp.broadcast_to(width_ref[...], (8, channel_count)), wanted, axis=1
    )
    amp, width = amp[0:1, :lanes], width[0:1, :lanes]
    k1, k2, k3 = grid_numbers(rows, lanes, own_channels, lengths)
    squared = k1 * k1 + k2 * k2 + k3 * k3
    base = amp * jnp.exp(-width * squared) * (1.0 / volume)
    for sign_id in range(4):
        phi_ref[sign_id] = base * summed[sign_id * rows : (sign_id + 1) * rows, :]
    width_out_ref[...] = jnp.broadcast_to(width, (8, lanes))


def grid_numbers(rows, lanes, own_channels, lengths):
    row_id = lax.broadcasted_iota(jnp.int32, (rows, lanes), 0)
    lane_id = lax.broadcasted_iota(jnp.int32, (rows, lanes), 1)
    k1 = (row_id // HARMONICS).astype(F32) * (2.0 * math.pi / lengths[0])
    k2 = (row_id % HARMONICS).astype(F32) * (2.0 * math.pi / lengths[1])
    k3 = (lane_id // own_channels + 1).astype(F32) * (2.0 * math.pi / lengths[2])
    return k1, k2, k3


def neighbour_of(step, row_count, col_count):
    row = lax.rem(lax.axis_index("row") + step[0] + row_count, row_count)
    col = lax.rem(lax.axis_index("col") + step[1] + col_count, col_count)
    return row * col_count + col


def slab_rows(slab, rows, atom_count):
    width = slab.shape[-1] // atom_count
    return [
        slab[row // width : row // width + 1, row % width * atom_count : (row % width + 1) * atom_count]
        for row in rows
    ]


def pack_kernel(counts, copied, positions_ref, species_ref, ghosts_ref, *refs):
    row_count, col_count = counts
    sources, (send_ref, *targets) = refs[:copied], refs[copied : 2 * copied + 1]
    positions, species, ghosts, first_sems, sems = refs[2 * copied + 1 :]
    firsts = ((positions_ref, positions), (species_ref, species), (ghosts_ref, ghosts))
    firsts = start_copies(firsts, first_sems)
    others = start_copies(tuple(zip(sources, targets)), sems)
    device_count = send_ref.shape[0]
    atom_count = species.shape[1]
    width = send_ref.shape[2] // atom_count
    slots, _ = direction_slots(row_count, col_count)
    for copy in firsts:
        copy.wait()
    rows = [positions[0], positions[1], positions[2], species[...].astype(F32)]
    for row, values in enumerate(rows):
        low = row % width * atom_count
        send_ref[:, row // width, low : low + atom_count] = jnp.broadcast_to(
            values, (device_count, atom_count)
        )
    for order, step in enumerate(DIRECTIONS):
        target = neighbour_of(step, row_count, col_count)
        row = 4 + slots[order]
        low = row % width * atom_count
        send_ref[target, row // width, low : low + atom_count] = ghosts[order, :].astype(F32)
    for copy in others:
        copy.wait()


def start_copies(pairs, sems):
    copies = [
        pltpu.make_async_copy(source, target, sems.at[spot])
        for spot, (source, target) in enumerate(pairs)
    ]
    for copy in copies:
        copy.start()
    return copies


def weights_kernel(dims, slot_count, table_dims, upd_ref, read_ref, out_ref, radial_ref, embed_ref, *refs):
    cells, refs = refs[: len(refs) - 13 - bool(table_dims)], refs[len(refs) - 13 - bool(table_dims) :]
    sources, (dupd_ref, back_ref, phi_ref, width_out_ref), refs = refs[:4], refs[4:8], refs[8:]
    axes, targets, sems = refs[: len(refs) - 5], refs[-5:-1], refs[-1]
    copies = start_copies(tuple(zip(sources, targets)), sems)
    if table_dims:
        table_kernel(table_dims, *cells, *axes)
    readout_gradient(upd_ref, read_ref, out_ref, dupd_ref)
    species_count, channel_count = embed_ref.shape
    radial_count = radial_ref.shape[0]
    order_id = lax.broadcasted_iota(jnp.int32, (radial_count, channel_count), 0)
    factor = jnp.zeros((radial_count, channel_count), F32)
    for order in range(radial_count):
        factor = jnp.where(order_id == order, -2.0 * radial_rate(order) / slot_count, factor)
    for k in range(species_count):
        back_ref[k * radial_count : (k + 1) * radial_count, :] = (
            radial_ref[...] * embed_ref[k : k + 1, :] * factor
        )
    for copy in copies:
        copy.wait()
    wave_weights(dims, *targets, phi_ref, width_out_ref)


def short_forward_kernel(
    dims,
    cells_ref,
    counts_ref,
    ids_ref,
    radial_ref,
    embed_ref,
    mix_ref,
    send_ref,
    vec_ref,
    kind_ref,
    owner_ref,
    upd_ref,
    slope_ref,
    table,
    lists,
    codes,
    pooled,
    weights,
    kinds8,
):
    own_channels, row_count, col_count = dims
    slot_count, atom_count = ids_ref.shape
    species_count, channel_count = embed_ref.shape
    radial_count = radial_ref.shape[0]
    device_count = send_ref.shape[0]
    slots, _ = direction_slots(row_count, col_count)
    own = slab_rows(cells_ref[neighbour_of((0, 0), row_count, col_count)], range(4), atom_count)
    for part in range(4):
        table[part, 0:1, :] = own[part]
    for order, step in enumerate(DIRECTIONS):
        source = neighbour_of(step, row_count, col_count)
        list_row = 4 + slots[len(DIRECTIONS) - 1 - order]
        block = slab_rows(cells_ref[source], (0, 1, 2, 3, list_row), atom_count)
        row = slice(8 + order, 9 + order)
        table[0, row, :] = block[0] + step[0] * CELL_EDGE
        table[1, row, :] = block[1] + step[1] * CELL_EDGE
        table[2, row, :] = block[2]
        table[3, row, :] = block[3]
        lists[order : order + 1, :] = block[4].astype(jnp.int32)
    picks = lists[...]
    for part in range(4):
        table[part, 8:16, :] = jnp.take_along_axis(table[part, 8:16, :], picks, axis=1)
    codes[8:16, :] = picks + atom_count * table[3, 8:16, :].astype(jnp.int32)
    codes[0:1, :] = lax.broadcasted_iota(
        jnp.int32, (1, atom_count), 1
    ) + atom_count * own[3].astype(jnp.int32)

    ids = ids_ref[...]
    lane = ids & (atom_count - 1)
    source = ids // atom_count
    here = [source == order + 1 for order in range(len(DIRECTIONS))]

    def picked(ref):
        values = jnp.take_along_axis(jnp.broadcast_to(ref[0:1, :], ids.shape), lane, axis=1)
        for order in range(len(DIRECTIONS)):
            wide = jnp.broadcast_to(ref[8 + order : 9 + order, :], ids.shape)
            values = jnp.where(here[order], jnp.take_along_axis(wide, lane, axis=1), values)
        return values

    gathered = [picked(table.at[part]) for part in range(3)]
    code = picked(codes)
    owner_ref[...] = (code & (atom_count - 1)) + source * atom_count
    gathered.append((code // atom_count).astype(F32))
    slot = lax.broadcasted_iota(jnp.int32, ids.shape, 0)
    kind = jnp.where(slot < counts_ref[...], gathered[3], -1.0)
    kind_ref[...] = kind
    squared = jnp.zeros(ids.shape, F32)
    for part in range(3):
        vector = gathered[part] - own[part]
        vec_ref[part] = vector
        squared = squared + vector * vector
    masks = [kind == float(k) for k in range(species_count)]
    for order in range(radial_count):
        basis = jnp.exp(squared * (-radial_rate(order)))
        for k in range(species_count):
            spot = k * radial_count + order
            pooled[spot : spot + 1, :] = jnp.sum(
                jnp.where(masks[k], basis, 0.0), axis=0, keepdims=True
            )
    for k in range(species_count):
        weights[k * radial_count : (k + 1) * radial_count, :] = (
            radial_ref[...] * embed_ref[k : k + 1, :] * (1.0 / slot_count)
        )
    kinds8[...] = jnp.zeros_like(kinds8)
    kinds8[0:species_count, :] = embed_ref[...]
    own_hot = (
        lax.broadcasted_iota(jnp.int32, (kinds8.shape[0], atom_count), 0).astype(F32) == own[3]
    ).astype(F32)
    initial = dot(kinds8[...], own_hot, 0, 0, EXACT)
    aggregate = dot(weights[...], pooled[...], 0, 0, GOOD)
    before = dot(mix_ref[...], aggregate, 0, 0, GOOD)
    gate = 1.0 / (1.0 + jnp.exp(-before))
    updated = initial + before * gate
    slope_ref[...] = gate + before * gate * (1.0 - gate)
    for q in range(own_channels):
        low, high = q * device_count, min(channel_count, (q + 1) * device_count)
        send_ref[0 : high - low, q, :] = updated[low:high, :]
        if high - low < device_count:
            send_ref[high - low :, q, :] = jnp.zeros(
                (device_count - (high - low), atom_count), F32
            )
    upd_ref[...] = updated


def readout_gradient(upd_ref, read_ref, out_ref, dupd_ref):
    channel_count, atom_count = upd_ref.shape
    readout = dot(read_ref[...], upd_ref[...], 0, 0, GOOD)
    gate = 1.0 / (1.0 + jnp.exp(-readout))
    scale = jnp.broadcast_to(out_ref[...], (channel_count, channel_count)).T
    dread = scale[:, 0:atom_count] * (gate + readout * gate * (1.0 - gate))
    dupd_ref[...] = dot(read_ref[...], dread, 1, 0, GOOD)


def turn_tables(turns, multiples):
    angle = turns * multiples
    halves = jnp.floor(2.0 * angle + 0.5)
    rest = angle - 0.5 * halves
    sign = 1.0 - 2.0 * (halves - 2.0 * jnp.floor(0.5 * halves))
    square = rest * rest

    def series(first, last):
        terms = [
            (-1.0) ** (p // 2) * (2.0 * math.pi) ** p / math.factorial(p)
            for p in range(first, last + 1, 2)
        ]
        total = jnp.full_like(square, terms[-1])
        for term in reversed(terms[:-1]):
            total = total * square + term
        return total

    return sign * series(0, 12), sign * rest * series(1, 13)


def table_kernel(dims, cells_ref, axes_ref):
    col_count, chunk_count, lengths = dims
    chunk = cells_ref.shape[0]
    atom_count = axes_ref.shape[2] // chunk
    first_device = pl.program_id(0) * chunk if chunk_count > 1 else 0
    multiples = lax.broadcasted_iota(jnp.int32, (HARMONICS, atom_count), 0).astype(F32)

    def one(index, _):
        device = first_device + index
        spot = pl.ds(pl.multiple_of(index * atom_count, atom_count), atom_count)
        block = slab_rows(cells_ref[index], range(3), atom_count)
        corner_row = (device // col_count).astype(F32) * CELL_EDGE
        corner_col = (device % col_count).astype(F32) * CELL_EDGE
        turns = (
            (block[0] + corner_row) * (1.0 / lengths[0]),
            (block[1] + corner_col) * (1.0 / lengths[1]),
            block[2] * (1.0 / lengths[2]),
        )
        for axis in range(3):
            numbers = multiples + 1.0 if axis == 2 else multiples
            cos, sin = turn_tables(turns[axis], numbers)
            axes_ref[2 * axis, :, spot] = cos
            axes_ref[2 * axis + 1, :, spot] = sin
        return 0

    lax.fori_loop(0, chunk, one, 0, unroll=4)


def wave_kernel(
    dims,
    recv_ref,
    axes_ref,
    phi_ref,
    width_ref,
    send_ref,
    push_ref,
    high,
    low,
    heights,
    lifted,
    sums,
    coefficients,
):
    own_channels, chunk_count, lengths = dims
    planes = (high, low, axes_ref, heights, lifted)

    def back():
        wave_back(own_channels, lengths, high, low, heights, lifted, coefficients, send_ref, push_ref)
        virial = wave_virial(own_channels, lengths, sums, phi_ref, width_ref, (1, push_ref.shape[2]))
        push_ref[:, 3, :] = jnp.broadcast_to(virial, (push_ref.shape[0], push_ref.shape[2]))

    if chunk_count == 1:
        sums[...] = wave_sums(own_channels, recv_ref, *planes)
        wave_coefficients(sums, phi_ref, coefficients)
        back()
        return
    phase, chunk_id = pl.program_id(0), pl.program_id(1)

    @pl.when((phase == 0) & (chunk_id == 0))
    def _():
        sums[...] = jnp.zeros_like(sums)

    part = wave_sums(own_channels, recv_ref, *planes)

    @pl.when(phase == 0)
    def _():
        sums[...] += part

    @pl.when((phase == 1) & (chunk_id == 0))
    def _():
        wave_coefficients(sums, phi_ref, coefficients)

    @pl.when(phase == 1)
    def _():
        back()


def wave_planes(own_channels, recv_ref, high_ref, low_ref, axes_ref, heights, lifted, devices):
    atom_count = recv_ref.shape[2]
    together, tiles = tile_layout(own_channels)
    lanes = tiles * HARMONICS
    sublane = lax.broadcasted_iota(jnp.int32, (HARMONICS, atom_count), 0)
    for index in devices:
        spot = slice(index * atom_count, (index + 1) * atom_count)
        feature = jnp.concatenate([recv_ref[index, 0:own_channels, :]] * together, axis=0)
        for part in range(2):
            for tile in range(tiles):
                first = tile * together
                height = jnp.broadcast_to(axes_ref[4 + part, first : first + 1, spot], sublane.shape)
                for n in range(1, together):
                    height = jnp.where(
                        sublane >= n * own_channels, axes_ref[4 + part, first + n : first + n + 1, spot], height
                    )
                row = part * lanes + tile * HARMONICS
                heights[row : row + HARMONICS, spot] = height
                lifted[row : row + HARMONICS, spot] = feature * height
        products = [
            axes_ref[first_axis, m : m + 1, spot] * axes_ref[second_axis, :, spot]
            for first_axis, second_axis in ((0, 2), (0, 3), (1, 2), (1, 3))
            for m in range(KMAX + 1)
        ]
        for pair in range(len(products) // 2):
            both = jnp.concatenate(products[2 * pair : 2 * pair + 2], axis=0)
            high = both.astype(BF16)
            rows = slice(2 * HARMONICS * pair, 2 * HARMONICS * (pair + 1))
            high_ref[rows, spot] = high
            low_ref[rows, spot] = (both - high.astype(F32)).astype(BF16)


def wave_sums(own_channels, recv_ref, high_ref, low_ref, axes_ref, heights, lifted):
    chunk, _, atom_count = recv_ref.shape
    lanes = lifted.shape[0] // 2
    group = math.gcd(chunk, 16)
    total = 0.0
    for first in range(0, chunk, group):
        devices = range(first, first + group)
        wave_planes(own_channels, recv_ref, high_ref, low_ref, axes_ref, heights, lifted, devices)
        spot = slice(first * atom_count, (first + group) * atom_count)
        values = lifted[:, spot]
        high = values.astype(BF16)
        low = (values - high.astype(F32)).astype(BF16)
        main = dot(high_ref[:, spot], jnp.concatenate([high, low], axis=0), 1, 1)
        total = total + main[:, : 2 * lanes] + (main[:, 2 * lanes :] + dot(low_ref[:, spot], high, 1, 1))
    return total


SIGNS = ((1.0, 1.0), (1.0, -1.0), (-1.0, 1.0), (-1.0, -1.0))


def wave_blocks(sums_ref, phi_ref):
    _, rows, lanes = phi_ref.shape
    sums = sums_ref[...]
    cos_part, sin_part = sums[:, :lanes], sums[:, lanes:]
    cc_c, cs_c, sc_c, ss_c = (cos_part[p * rows : (p + 1) * rows] for p in range(4))
    cc_s, cs_s, sc_s, ss_s = (sin_part[p * rows : (p + 1) * rows] for p in range(4))
    for sign_id, (s1, s2) in enumerate(SIGNS):
        real = cc_c - s1 * s2 * ss_c - s1 * sc_s - s2 * cs_s
        imag = cc_s - s1 * s2 * ss_s + s1 * sc_c + s2 * cs_c
        phi = phi_ref[sign_id]
        yield s1, s2, phi * real, phi * imag, real, imag


def wave_virial(own_channels, lengths, sums_ref, phi_ref, width_ref, shape):
    _, rows, lanes = phi_ref.shape
    even = first_odd = second_odd = both_odd = jnp.zeros((rows, lanes), F32)
    for s1, s2, dreal, dimag, real, imag in wave_blocks(sums_ref, phi_ref):
        power = dreal * real + dimag * imag
        even = even + power
        first_odd = first_odd + s1 * power
        second_odd = second_odd + s2 * power
        both_odd = both_odd + s1 * s2 * power
    width = width_ref[0:1, :]
    k1, k2, k3 = grid_numbers(rows, lanes, own_channels, lengths)

    def total_of(values):
        return jnp.sum(jnp.sum(values, axis=0, keepdims=True), axis=1, keepdims=True)

    energy = 0.5 * total_of(even)
    scaled = width * even
    terms = {
        (0, 0): energy - total_of(k1 * k1 * scaled),
        (1, 1): energy - total_of(k2 * k2 * scaled),
        (2, 2): energy - total_of(k3 * k3 * scaled),
        (0, 1): -total_of(k1 * k2 * width * both_odd),
        (0, 2): -total_of(k1 * k3 * width * first_odd),
        (1, 2): -total_of(k2 * k3 * width * second_odd),
    }
    return virial_row(terms, shape)


def wave_coefficients(sums_ref, phi_ref, coefficients_ref):
    _, rows, lanes = phi_ref.shape
    zero = jnp.zeros((rows, lanes), F32)
    d_cc_c = d_cc_s = d_cs_c = d_cs_s = d_sc_c = d_sc_s = d_ss_c = d_ss_s = zero
    for s1, s2, dreal, dimag, _, _ in wave_blocks(sums_ref, phi_ref):
        d_cc_c, d_ss_c = d_cc_c + dreal, d_ss_c - s1 * s2 * dreal
        d_sc_s, d_cs_s = d_sc_s - s1 * dreal, d_cs_s - s2 * dreal
        d_cc_s, d_ss_s = d_cc_s + dimag, d_ss_s - s1 * s2 * dimag
        d_sc_c, d_cs_c = d_sc_c + s1 * dimag, d_cs_c + s2 * dimag
    values = jnp.concatenate(
        [
            jnp.concatenate(pair, axis=1)
            for pair in ((d_cc_c, d_cc_s), (d_cs_c, d_cs_s), (d_sc_c, d_sc_s), (d_ss_c, d_ss_s))
        ],
        axis=0,
    )
    cc, cs, sc, ss = (values[p * rows : (p + 1) * rows] for p in range(4))
    row_id = lax.broadcasted_iota(jnp.int32, (rows, 2 * lanes), 0)
    m1 = (row_id // HARMONICS).astype(F32)
    m2 = (row_id % HARMONICS).astype(F32)
    along_x = jnp.concatenate([m1 * sc, m1 * ss, -m1 * cc, -m1 * cs], axis=0)
    along_y = jnp.concatenate([m2 * cs, -m2 * cc, m2 * ss, -m2 * sc], axis=0)
    values = jnp.concatenate([values, along_x, along_y], axis=1)
    turned = values.T
    high = turned.astype(BF16)
    count = turned.shape[0]
    coefficients_ref[0:count, :] = high
    coefficients_ref[count:, :] = (turned - high.astype(F32)).astype(BF16)


def wave_spread(high_ref, low_ref, coefficients):
    values = coefficients[...]
    count = values.shape[0] // 2
    main = dot(values, high_ref[...], 1, 0)
    return main[:count] + (main[count:] + dot(values[:count], low_ref[...], 1, 0))


def wave_back(own_channels, lengths, high_ref, low_ref, heights, lifted, coefficients, send_ref, push_ref):
    chunk, _, atom_count = push_ref.shape
    together, tiles = tile_layout(own_channels)
    lanes = tiles * HARMONICS
    sublane = lax.broadcasted_iota(jnp.int32, (HARMONICS, atom_count), 0)
    numbers = [(sublane // own_channels + 1 + tile * together).astype(F32) for tile in range(tiles)]
    result = wave_spread(high_ref, low_ref, coefficients)
    for index in range(chunk):
        spot = slice(index * atom_count, (index + 1) * atom_count)
        part = result[:, spot]
        feature = grad_x = grad_y = grad_z = jnp.zeros((HARMONICS, atom_count), F32)
        for tile in range(tiles):
            a, b = tile * HARMONICS, lanes + tile * HARMONICS
            on_cos, on_sin = part[a : a + HARMONICS], part[b : b + HARMONICS]
            feature = feature + on_cos * heights[a : a + HARMONICS, spot] + on_sin * heights[b : b + HARMONICS, spot]
            lift_cos = lifted[a : a + HARMONICS, spot]
            lift_sin = lifted[b : b + HARMONICS, spot]
            grad_z = grad_z + numbers[tile] * (on_sin * lift_cos - on_cos * lift_sin)
            a, b = a + 2 * lanes, b + 2 * lanes
            grad_x = grad_x + part[a : a + HARMONICS] * lift_cos + part[b : b + HARMONICS] * lift_sin
            a, b = a + 2 * lanes, b + 2 * lanes
            grad_y = grad_y + part[a : a + HARMONICS] * lift_cos + part[b : b + HARMONICS] * lift_sin
        total = feature[0:own_channels]
        for n in range(1, together):
            total = total + feature[n * own_channels : (n + 1) * own_channels]
        send_ref[index, 0:own_channels, :] = total
        pieces = (
            grad_x * (2.0 * math.pi / lengths[0]),
            grad_y * (2.0 * math.pi / lengths[1]),
            grad_z * (2.0 * math.pi / lengths[2]),
        )
        for row, piece in enumerate(pieces):
            push_ref[index, row : row + 1, :] = jnp.sum(piece, axis=0, keepdims=True)


def virial_row(terms, shape):
    lane = lax.broadcasted_iota(jnp.int32, shape, 1)
    row = jnp.zeros(shape, F32)
    for (i, j), value in terms.items():
        spots = (lane == 3 * i + j) | (lane == 3 * j + i)
        row = jnp.where(spots, value, row)
    return row


def short_back_kernel(
    dims,
    recv_ref,
    vec_ref,
    kind_ref,
    dupd_ref,
    slope_ref,
    owner_ref,
    back_ref,
    mix_ref,
    push_ref,
    send_ref,
    fgrad,
    dpool,
    parts,
):
    own_channels, row_count, col_count, species_count, radial_count = dims
    slot_count, atom_count = owner_ref.shape
    channel_count = mix_ref.shape[0]
    device_count = send_ref.shape[0]
    table_rows = round_up(len(DIRECTIONS) + 1, 16)
    for q in range(own_channels):
        low, high = q * device_count, min(channel_count, (q + 1) * device_count)
        fgrad[low:high, :] = recv_ref[0 : high - low, q, :]
    dbefore = (fgrad[...] + dupd_ref[...]) * slope_ref[...]
    daggregate = dot(mix_ref[...], dbefore, 1, 0, GOOD)
    dpool[...] = dot(back_ref[...], daggregate, 1, 0, GOOD)
    vectors = [vec_ref[part] for part in range(3)]
    squared = vectors[0] * vectors[0] + vectors[1] * vectors[1] + vectors[2] * vectors[2]
    kind = kind_ref[...]
    sums = [jnp.zeros(kind.shape, F32) for _ in range(species_count)]
    for order in range(radial_count):
        basis = jnp.exp(squared * (-radial_rate(order)))
        for k in range(species_count):
            spot = k * radial_count + order
            sums[k] = sums[k] + basis * dpool[spot : spot + 1, :]
    slope = jnp.zeros(kind.shape, F32)
    for k in range(species_count):
        slope = jnp.where(kind == float(k), sums[k], slope)
    grads = [slope * vector for vector in vectors]

    def total_of(values):
        return jnp.sum(jnp.sum(values, axis=0, keepdims=True), axis=1, keepdims=True)

    terms = {
        (i, j): -total_of(grads[i] * vectors[j]) for i in range(3) for j in range(i, 3)
    }
    virial = virial_row(terms, (1, atom_count))
    for part in range(3):
        parts[2 * part], parts[2 * part + 1] = split(grads[part])

    sublane = lax.broadcasted_iota(jnp.int32, (atom_count, atom_count), 0)
    table_id = lax.broadcasted_iota(jnp.int32, (table_rows, atom_count), 0)
    group = 8
    scattered = jnp.zeros((atom_count, 6 * table_rows), F32)
    for low in range(0, slot_count, group):
        hots, columns = [], []
        for s in range(low, low + group):
            ids = owner_ref[s : s + 1, :]
            hots.append(jnp.where(sublane == (ids & (atom_count - 1)), 1.0, 0.0).astype(BF16))
            mine = table_id == ids // atom_count
            columns.append(
                jnp.concatenate(
                    [
                        jnp.where(mine, parts[p, s : s + 1, :], 0.0).astype(BF16)
                        for p in range(6)
                    ],
                    axis=0,
                )
            )
        scattered = scattered + dot(
            jnp.concatenate(hots, axis=1), jnp.concatenate(columns, axis=1), 1, 1
        )
    rows = scattered.T
    send_ref[...] = push_ref[...]
    send_ref[:, 3, :] += jnp.broadcast_to(virial, (device_count, atom_count))
    me = neighbour_of((0, 0), row_count, col_count)
    for part in range(3):
        low = 2 * part * table_rows
        both = rows[low : low + table_rows] + rows[low + table_rows : low + 2 * table_rows]
        send_ref[me, part, :] += both[0, :] - jnp.sum(grads[part], axis=0)
        for order, step in enumerate(DIRECTIONS):
            target = neighbour_of(step, row_count, col_count)
            send_ref[target, part, :] += both[1 + order, :]


def final_kernel(volume, recv_ref, forces_ref, virial_ref):
    total = jnp.sum(recv_ref[...], axis=0)
    for part in range(3):
        forces_ref[part] = -total[part : part + 1, :]
    virial = total[3:4, :] * (1.0 / volume)
    for i in range(3):
        virial_ref[i : i + 1, :] = virial[:, 3 * i : 3 * i + 3]


def per_device(
    positions,
    species,
    counts,
    neighbours,
    ghost_index,
    wave_numbers,
    embedding,
    w_radial,
    w_mix,
    w_read,
    w_out,
    amplitude,
    kernel_width,
    filter_gain,
):
    row_count = lax.axis_size("row")
    col_count = lax.axis_size("col")
    device_count = row_count * col_count
    atom_count = positions.shape[3]
    slot_count = neighbours.shape[2]
    direction_count, ghost_count = ghost_index.shape[2:]
    species_count, channel_count = embedding.shape
    radial_count = w_radial.shape[0]
    own_channels = -(-channel_count // device_count)
    lengths = (CELL_EDGE * row_count, CELL_EDGE * col_count, HEIGHT)
    volume = lengths[0] * lengths[1] * lengths[2]
    rows = (KMAX + 1) * HARMONICS
    lanes = tile_layout(own_channels)[1] * HARMONICS
    _, shared = direction_slots(row_count, col_count)
    slab_first = round_up(4 + shared, 2) // 2 * atom_count
    slab_features = round_up(own_channels, 4)
    chunk = math.gcd(device_count, 32)
    chunk_count = device_count // chunk

    def exchange(slabs):
        return lax.all_to_all(slabs, AXES, 0, 0, tiled=True)

    def shape(*dims):
        return jax.ShapeDtypeStruct(dims, F32)

    def scratch(*dims):
        return pltpu.VMEM(dims, F32)

    def call(kernel, out_shape, vmem=16, **options):
        return pl.pallas_call(
            kernel,
            out_shape=out_shape,
            compiler_params=pltpu.CompilerParams(vmem_limit_bytes=vmem * 1024 * 1024),
            **options,
        )

    ids = neighbours.reshape(slot_count, atom_count)
    ghosts = ghost_index.reshape(direction_count, ghost_count)
    mesh_counts = (row_count, col_count)
    inputs = (
        counts.reshape(1, atom_count),
        ids,
        w_radial,
        embedding,
        w_mix,
        w_read,
        w_out.reshape(1, -1),
    )
    wave_inputs = (filter_gain, wave_numbers, amplitude.reshape(1, -1), kernel_width.reshape(1, -1))

    def fetched(*arrays):
        return [pltpu.with_memory_space_constraint(x, pltpu.HBM) for x in arrays]

    kept = pl.BlockSpec(memory_space=pltpu.HBM)
    near = pl.BlockSpec(memory_space=pltpu.VMEM)
    send, *inputs = call(
        functools.partial(pack_kernel, mesh_counts, len(inputs)),
        (shape(device_count, 2, slab_first),)
        + tuple(jax.ShapeDtypeStruct(x.shape, x.dtype) for x in inputs),
        in_specs=[kept] * (3 + len(inputs)),
        scratch_shapes=[
            scratch(3, 1, atom_count),
            pltpu.VMEM((1, atom_count), jnp.int32),
            pltpu.VMEM(ghosts.shape, jnp.int32),
            pltpu.SemaphoreType.DMA((3,)),
            pltpu.SemaphoreType.DMA((len(inputs),)),
        ],
        name="pack",
    )(*fetched(positions.reshape(3, 1, atom_count), species.reshape(1, atom_count), ghosts, *inputs))
    live, ids, w_radial, embedding, w_mix, w_read, w_out = inputs
    cells = exchange(send)

    pooled_rows = species_count * radial_count
    send, vectors, kinds, owners, updated, slope = call(
        functools.partial(short_forward_kernel, (own_channels,) + mesh_counts),
        (
            shape(device_count, slab_features, atom_count),
            shape(3, slot_count, atom_count),
            shape(slot_count, atom_count),
            jax.ShapeDtypeStruct((slot_count, atom_count), jnp.int32),
            shape(channel_count, atom_count),
            shape(channel_count, atom_count),
        ),
        scratch_shapes=[
            scratch(4, 16, atom_count),
            pltpu.VMEM((direction_count, atom_count), jnp.int32),
            pltpu.VMEM((16, atom_count), jnp.int32),
            scratch(pooled_rows, atom_count),
            scratch(pooled_rows, channel_count),
            scratch(round_up(species_count, 8), channel_count),
        ],
        name="short_forward",
    )(cells, live, ids, w_radial, embedding, w_mix)
    send, cells, updated = lax.optimization_barrier((send, cells, updated))
    features = exchange(send)

    axes_block = (6, HARMONICS, chunk * atom_count)
    axes_shape = shape(6, HARMONICS, device_count * atom_count)
    table_dims = (col_count, chunk_count, lengths)
    cells_inputs, axes_outputs = (), ()
    if chunk_count == 1:
        cells_inputs, axes_outputs = (cells,), (axes_shape,)
    dupd, back, phi, width, *axes = call(
        functools.partial(
            weights_kernel,
            (device_count, channel_count, own_channels, lengths, volume),
            slot_count,
            table_dims if chunk_count == 1 else None,
        ),
        (
            shape(channel_count, atom_count),
            shape(pooled_rows, channel_count),
            shape(4, rows, lanes),
            shape(8, lanes),
        )
        + axes_outputs,
        in_specs=[near] * (5 + len(cells_inputs)) + [kept] * len(wave_inputs),
        scratch_shapes=[pltpu.VMEM(x.shape, x.dtype) for x in wave_inputs]
        + [pltpu.SemaphoreType.DMA((len(wave_inputs),))],
        cost_estimate=pl.CostEstimate(
            flops=2 * 4 * rows * filter_gain.shape[0] * 3 * lanes,
            bytes_accessed=4 * filter_gain.size,
            transcendentals=0,
        ),
        name="weights",
    )(updated, w_read, w_out, w_radial, embedding, *cells_inputs, *fetched(*wave_inputs))
    if chunk_count > 1:
        axes = [
            call(
                functools.partial(table_kernel, table_dims),
                axes_shape,
                grid=(chunk_count,),
                in_specs=[pl.BlockSpec((chunk, 2, slab_first), lambda i: (i, 0, 0))],
                out_specs=pl.BlockSpec(axes_block, lambda i: (0, 0, i)),
                name="tables",
            )(cells)
        ]
    features, dupd, back = lax.optimization_barrier((features, dupd, back))

    plane = pltpu.VMEM((4 * rows, chunk * atom_count), BF16)
    wave_scratch = [plane, plane] + [scratch(2 * lanes, chunk * atom_count)] * 2
    features_block = (chunk, slab_features, atom_count)
    wave_options = {}
    if chunk_count > 1:
        wave_options = dict(
            grid=(2, chunk_count),
            in_specs=[
                pl.BlockSpec(features_block, lambda p, i: (i, 0, 0)),
                pl.BlockSpec(axes_block, lambda p, i: (0, 0, i)),
                pl.BlockSpec((4, rows, lanes), lambda p, i: (0, 0, 0)),
                pl.BlockSpec((8, lanes), lambda p, i: (0, 0)),
            ],
            out_specs=(
                pl.BlockSpec(features_block, lambda p, i: (i * p, 0, 0)),
                pl.BlockSpec((chunk, 4, atom_count), lambda p, i: (i * p, 0, 0)),
            ),
        )
    send, push = call(
        functools.partial(wave_kernel, (own_channels, chunk_count, lengths)),
        (shape(device_count, slab_features, atom_count), shape(device_count, 4, atom_count)),
        vmem=32,
        scratch_shapes=wave_scratch
        + [scratch(4 * rows, 2 * lanes), pltpu.VMEM((12 * lanes, 4 * rows), BF16)],
        name="waves",
        **wave_options,
    )(features, *axes, phi, width)
    gradients = exchange(send)

    send = call(
        functools.partial(
            short_back_kernel, (own_channels,) + mesh_counts + (species_count, radial_count)
        ),
        shape(device_count, 4, atom_count),
        scratch_shapes=[
            scratch(channel_count, atom_count),
            scratch(pooled_rows, atom_count),
            scratch(6, slot_count, atom_count),
        ],
        name="short_back",
    )(gradients, vectors, kinds, dupd, slope, owners, back, w_mix, push)
    returned = exchange(send)

    forces, virial = call(
        functools.partial(final_kernel, volume),
        (shape(3, 1, atom_count), shape(3, 3)),
        name="total",
    )(returned)
    return (forces[:, None], virial)


def solution(mesh):
    return jax.shard_map(
        per_device,
        mesh=mesh,
        in_specs=(
            P(None, "row", "col", None),
            P("row", "col", None),
            P("row", "col", None),
            P("row", "col", None, None),
            P("row", "col", None, None),
            P(),
            P(),
            P(),
            P(),
            P(),
            P(),
            P(),
            P(),
            P(),
        ),
        out_specs=(P(None, "row", "col", None), P()),
        check_vma=False,
    )
```

```python
import functools
import math

import jax
import jax.numpy as jnp
from jax import lax
from jax.experimental import pallas as pl
from jax.experimental.pallas import tpu as pltpu
from jax.sharding import PartitionSpec as P

CELL_EDGE = 12.0
HEIGHT = 36.0
KMAX = 6
HARMONICS = 8
EXACT = lax.Precision.HIGHEST
GOOD = lax.Precision.HIGH
DIRECTIONS = ((-1, -1), (-1, 0), (-1, 1), (0, -1), (0, 1), (1, -1), (1, 0), (1, 1))
F32 = jnp.float32
BF16 = jnp.bfloat16
AXES = ("row", "col")


def radial_rate(order):
    return 0.003 * 1.6**order


def round_up(value, step):
    return -(-value // step) * step


def direction_slots(row_count, col_count):
    seen = {}
    slots = []
    for row_step, col_step in DIRECTIONS:
        key = (row_step % row_count, col_step % col_count)
        slots.append(seen.get(key, 0))
        seen[key] = slots[-1] + 1
    return slots, max(seen.values())


def tile_layout(own_channels):
    shared = HARMONICS // own_channels
    return shared, -(-KMAX // shared)


def dot(lhs, rhs, lhs_dim, rhs_dim, precision=None):
    return lax.dot_general(
        lhs,
        rhs,
        (((lhs_dim,), (rhs_dim,)), ((), ())),
        precision=precision,
        preferred_element_type=F32,
    )


def split(values):
    high = values.astype(BF16).astype(F32)
    return high, values - high


def wave_weights(dims, gain_ref, waves_ref, amp_ref, width_ref, phi_ref, width_out_ref):
    device_count, channel_count, own_channels, lengths, volume = dims
    me = lax.axis_index("row") * lax.axis_size("col") + lax.axis_index("col")
    wave_count = gain_ref.shape[0]
    rows = (KMAX + 1) * HARMONICS
    together, tiles = tile_layout(own_channels)
    lanes = tiles * HARMONICS
    place = lax.broadcasted_iota(jnp.int32, (8, channel_count), 0) * device_count + me
    chosen = (lax.broadcasted_iota(jnp.int32, (8, channel_count), 1) == place).astype(F32)
    own_gain = dot(chosen, gain_ref[...], 1, 1, EXACT)
    first, second, third = waves_ref[0:1, :], waves_ref[1:2, :], waves_ref[2:3, :]
    sign = jnp.where(first < 0, 2, 0) + jnp.where(second < 0, 1, 0)
    key = sign * rows + jnp.abs(first) * HARMONICS + jnp.abs(second)
    spots = lax.broadcasted_iota(jnp.int32, (4 * rows, wave_count), 0) == key
    onehot = jnp.where(spots, 1.0, 0.0).astype(BF16)
    mine = jnp.concatenate([own_gain[:own_channels]] * together, axis=0)
    height = lax.broadcasted_iota(jnp.int32, (HARMONICS, wave_count), 0) // own_channels + 1
    blocks = [jnp.where(height + tile * together == third, mine, 0.0) for tile in range(tiles)]
    wide = jnp.concatenate(blocks, axis=0)
    high = wide.astype(BF16)
    rest = wide - high.astype(F32)
    middle = rest.astype(BF16)
    low = (rest - middle.astype(F32)).astype(BF16)
    summed = dot(onehot, high, 1, 1) + (dot(onehot, middle, 1, 1) + dot(onehot, low, 1, 1))
    lane = lax.broadcasted_iota(jnp.int32, (8, channel_count), 1)
    wanted = jnp.minimum(lane % own_channels * device_count + me, channel_count - 1)
    amp = jnp.take_along_axis(jnp.broadcast_to(amp_ref[...], (8, channel_count)), wanted, axis=1)
    width = jnp.take_along_axis(
        jnp.broadcast_to(width_ref[...], (8, channel_count)), wanted, axis=1
    )
    amp, width = amp[0:1, :lanes], width[0:1, :lanes]
    k1, k2, k3 = grid_numbers(rows, lanes, own_channels, lengths)
    squared = k1 * k1 + k2 * k2 + k3 * k3
    base = amp * jnp.exp(-width * squared) * (1.0 / volume)
    for sign_id in range(4):
        phi_ref[sign_id] = base * summed[sign_id * rows : (sign_id + 1) * rows, :]
    width_out_ref[...] = jnp.broadcast_to(width, (8, lanes))


def grid_numbers(rows, lanes, own_channels, lengths):
    row_id = lax.broadcasted_iota(jnp.int32, (rows, lanes), 0)
    lane_id = lax.broadcasted_iota(jnp.int32, (rows, lanes), 1)
    k1 = (row_id // HARMONICS).astype(F32) * (2.0 * math.pi / lengths[0])
    k2 = (row_id % HARMONICS).astype(F32) * (2.0 * math.pi / lengths[1])
    k3 = (lane_id // own_channels + 1).astype(F32) * (2.0 * math.pi / lengths[2])
    return k1, k2, k3


def neighbour_of(step, row_count, col_count):
    row = lax.rem(lax.axis_index("row") + step[0] + row_count, row_count)
    col = lax.rem(lax.axis_index("col") + step[1] + col_count, col_count)
    return row * col_count + col


def slab_rows(slab, rows, atom_count):
    width = slab.shape[-1] // atom_count
    return [
        slab[row // width : row // width + 1, row % width * atom_count : (row % width + 1) * atom_count]
        for row in rows
    ]


def pack_kernel(counts, copied, positions_ref, species_ref, ghosts_ref, *refs):
    row_count, col_count = counts
    sources, (send_ref, *targets) = refs[:copied], refs[copied : 2 * copied + 1]
    positions, species, ghosts, first_sems, sems = refs[2 * copied + 1 :]
    firsts = ((positions_ref, positions), (species_ref, species), (ghosts_ref, ghosts))
    firsts = start_copies(firsts, first_sems)
    others = start_copies(tuple(zip(sources, targets)), sems)
    device_count = send_ref.shape[0]
    atom_count = species.shape[1]
    width = send_ref.shape[2] // atom_count
    slots, _ = direction_slots(row_count, col_count)
    for copy in firsts:
        copy.wait()
    rows = [positions[0], positions[1], positions[2], species[...].astype(F32)]
    for row, values in enumerate(rows):
        low = row % width * atom_count
        send_ref[:, row // width, low : low + atom_count] = jnp.broadcast_to(
            values, (device_count, atom_count)
        )
    for order, step in enumerate(DIRECTIONS):
        target = neighbour_of(step, row_count, col_count)
        row = 4 + slots[order]
        low = row % width * atom_count
        send_ref[target, row // width, low : low + atom_count] = ghosts[order, :].astype(F32)
    for copy in others:
        copy.wait()


def start_copies(pairs, sems):
    copies = [
        pltpu.make_async_copy(source, target, sems.at[spot])
        for spot, (source, target) in enumerate(pairs)
    ]
    for copy in copies:
        copy.start()
    return copies


def weights_kernel(dims, table_dims, upd_ref, mixed_ref, *refs):
    cells, refs = refs[: len(refs) - 17 - bool(table_dims)], refs[len(refs) - 17 - bool(table_dims) :]
    sources, (dupd_ref, back_ref, phi_ref, width_out_ref), refs = refs[:6], refs[6:10], refs[10:]
    axes, targets, sems = refs[: len(refs) - 7], refs[-7:-1], refs[-1]
    copies = start_copies(tuple(zip(sources, targets)), sems)
    if table_dims:
        table_kernel(table_dims, *cells, *axes)
    pooled_rows, channel_count = mixed_ref.shape
    radial_count = dims[5]
    order_id = lax.broadcasted_iota(jnp.int32, (pooled_rows, channel_count), 0) % radial_count
    factor = jnp.zeros((pooled_rows, channel_count), F32)
    for order in range(radial_count):
        factor = jnp.where(order_id == order, -2.0 * radial_rate(order), factor)
    back_ref[...] = mixed_ref[...] * factor
    for copy in copies:
        copy.wait()
    readout_gradient(upd_ref, targets[0], targets[1], dupd_ref)
    wave_weights(dims[:5], *targets[2:], phi_ref, width_out_ref)


def short_forward_kernel(
    dims,
    cells_ref,
    counts_ref,
    ids_ref,
    radial_ref,
    embed_ref,
    mix_ref,
    send_ref,
    vec_ref,
    kind_ref,
    owner_ref,
    upd_ref,
    slope_ref,
    mixed_ref,
    table,
    lists,
    codes,
    pooled,
    weights,
    kinds8,
):
    own_channels, row_count, col_count = dims
    slot_count, atom_count = ids_ref.shape
    species_count, channel_count = embed_ref.shape
    radial_count = radial_ref.shape[0]
    device_count = send_ref.shape[0]
    slots, _ = direction_slots(row_count, col_count)
    for k in range(species_count):
        weights[k * radial_count : (k + 1) * radial_count, :] = (
            radial_ref[...] * embed_ref[k : k + 1, :] * (1.0 / slot_count)
        )
    weights[...] = dot(weights[...], mix_ref[...], 1, 0, EXACT)
    mixed_ref[...] = weights[...]
    own = slab_rows(cells_ref[neighbour_of((0, 0), row_count, col_count)], range(4), atom_count)
    for part in range(4):
        table[part, 0:1, :] = own[part]
    for order, step in enumerate(DIRECTIONS):
        source = neighbour_of(step, row_count, col_count)
        list_row = 4 + slots[len(DIRECTIONS) - 1 - order]
        block = slab_rows(cells_ref[source], (0, 1, 2, 3, list_row), atom_count)
        row = slice(8 + order, 9 + order)
        table[0, row, :] = block[0] + step[0] * CELL_EDGE
        table[1, row, :] = block[1] + step[1] * CELL_EDGE
        table[2, row, :] = block[2]
        table[3, row, :] = block[3]
        lists[order : order + 1, :] = block[4].astype(jnp.int32)
    picks = lists[...]
    for part in range(4):
        table[part, 8:16, :] = jnp.take_along_axis(table[part, 8:16, :], picks, axis=1)
    codes[8:16, :] = picks + atom_count * table[3, 8:16, :].astype(jnp.int32)
    codes[0:1, :] = lax.broadcasted_iota(
        jnp.int32, (1, atom_count), 1
    ) + atom_count * own[3].astype(jnp.int32)

    ids = ids_ref[...]
    lane = ids & (atom_count - 1)
    source = ids // atom_count
    here = [source == order + 1 for order in range(len(DIRECTIONS))]

    def picked(ref):
        values = jnp.take_along_axis(jnp.broadcast_to(ref[0:1, :], ids.shape), lane, axis=1)
        for order in range(len(DIRECTIONS)):
            wide = jnp.broadcast_to(ref[8 + order : 9 + order, :], ids.shape)
            values = jnp.where(here[order], jnp.take_along_axis(wide, lane, axis=1), values)
        return values

    gathered = [picked(table.at[part]) for part in range(3)]
    code = picked(codes)
    owner_ref[...] = (code & (atom_count - 1)) + source * atom_count
    gathered.append((code // atom_count).astype(F32))
    slot = lax.broadcasted_iota(jnp.int32, ids.shape, 0)
    kind = jnp.where(slot < counts_ref[...], gathered[3], -1.0)
    kind_ref[...] = kind
    squared = jnp.zeros(ids.shape, F32)
    for part in range(3):
        vector = gathered[part] - own[part]
        vec_ref[part] = vector
        squared = squared + vector * vector
    masks = [kind == float(k) for k in range(species_count)]
    for order in range(radial_count):
        basis = jnp.exp(squared * (-radial_rate(order)))
        for k in range(species_count):
            spot = k * radial_count + order
            pooled[spot : spot + 1, :] = jnp.sum(
                jnp.where(masks[k], basis, 0.0), axis=0, keepdims=True
            )
    kinds8[...] = jnp.zeros_like(kinds8)
    kinds8[0:species_count, :] = embed_ref[...]
    own_hot = (
        lax.broadcasted_iota(jnp.int32, (kinds8.shape[0], atom_count), 0).astype(F32) == own[3]
    ).astype(F32)
    initial = dot(kinds8[...], own_hot, 0, 0, EXACT)
    before = dot(weights[...], pooled[...], 0, 0, GOOD)
    gate = 1.0 / (1.0 + jnp.exp(-before))
    updated = initial + before * gate
    slope_ref[...] = gate + before * gate * (1.0 - gate)
    for q in range(own_channels):
        low, high = q * device_count, min(channel_count, (q + 1) * device_count)
        send_ref[0 : high - low, q, :] = updated[low:high, :]
        if high - low < device_count:
            send_ref[high - low :, q, :] = jnp.zeros(
                (device_count - (high - low), atom_count), F32
            )
    upd_ref[...] = updated


def readout_gradient(upd_ref, read_ref, out_ref, dupd_ref):
    channel_count, atom_count = upd_ref.shape
    readout = dot(read_ref[...], upd_ref[...], 0, 0, GOOD)
    gate = 1.0 / (1.0 + jnp.exp(-readout))
    scale = jnp.broadcast_to(out_ref[...], (channel_count, channel_count)).T
    dread = scale[:, 0:atom_count] * (gate + readout * gate * (1.0 - gate))
    dupd_ref[...] = dot(read_ref[...], dread, 1, 0, GOOD)


def turn_tables(turns, multiples):
    angle = turns * multiples
    halves = jnp.floor(2.0 * angle + 0.5)
    rest = angle - 0.5 * halves
    sign = 1.0 - 2.0 * (halves - 2.0 * jnp.floor(0.5 * halves))
    square = rest * rest

    def series(first, last):
        terms = [
            (-1.0) ** (p // 2) * (2.0 * math.pi) ** p / math.factorial(p)
            for p in range(first, last + 1, 2)
        ]
        total = jnp.full_like(square, terms[-1])
        for term in reversed(terms[:-1]):
            total = total * square + term
        return total

    return sign * series(0, 12), sign * rest * series(1, 13)


def table_kernel(dims, cells_ref, axes_ref):
    col_count, chunk_count, lengths = dims
    chunk = cells_ref.shape[0]
    atom_count = axes_ref.shape[2] // chunk
    first_device = pl.program_id(0) * chunk if chunk_count > 1 else 0
    multiples = lax.broadcasted_iota(jnp.int32, (HARMONICS, atom_count), 0).astype(F32)

    def one(index, _):
        device = first_device + index
        spot = pl.ds(pl.multiple_of(index * atom_count, atom_count), atom_count)
        block = slab_rows(cells_ref[index], range(3), atom_count)
        corner_row = (device // col_count).astype(F32) * CELL_EDGE
        corner_col = (device % col_count).astype(F32) * CELL_EDGE
        turns = (
            (block[0] + corner_row) * (1.0 / lengths[0]),
            (block[1] + corner_col) * (1.0 / lengths[1]),
            block[2] * (1.0 / lengths[2]),
        )
        for axis in range(3):
            numbers = multiples + 1.0 if axis == 2 else multiples
            cos, sin = turn_tables(turns[axis], numbers)
            axes_ref[2 * axis, :, spot] = cos
            axes_ref[2 * axis + 1, :, spot] = sin
        return 0

    lax.fori_loop(0, chunk, one, 0, unroll=4)


def wave_kernel(
    dims,
    recv_ref,
    axes_ref,
    phi_ref,
    width_ref,
    send_ref,
    push_ref,
    planes_ref,
    heights,
    lifted,
    sums,
    coefficients,
):
    own_channels, chunk_count, lengths = dims
    planes = (planes_ref, axes_ref, heights, lifted)

    def back():
        wave_back(own_channels, lengths, planes_ref, heights, lifted, coefficients, send_ref, push_ref)
        virial = wave_virial(own_channels, lengths, sums, phi_ref, width_ref, (1, push_ref.shape[2]))
        push_ref[:, 3, :] = jnp.broadcast_to(virial, (push_ref.shape[0], push_ref.shape[2]))

    if chunk_count == 1:
        sums[...] = wave_sums(own_channels, recv_ref, *planes)
        wave_coefficients(sums, phi_ref, coefficients)
        back()
        return
    phase, chunk_id = pl.program_id(0), pl.program_id(1)

    @pl.when((phase == 0) & (chunk_id == 0))
    def _():
        sums[...] = jnp.zeros_like(sums)

    part = wave_sums(own_channels, recv_ref, *planes)

    @pl.when(phase == 0)
    def _():
        sums[...] += part

    @pl.when((phase == 1) & (chunk_id == 0))
    def _():
        wave_coefficients(sums, phi_ref, coefficients)

    @pl.when(phase == 1)
    def _():
        back()


def wave_planes(own_channels, recv_ref, planes_ref, axes_ref, heights, lifted, devices):
    atom_count = recv_ref.shape[2]
    together, tiles = tile_layout(own_channels)
    lanes = tiles * HARMONICS
    sublane = lax.broadcasted_iota(jnp.int32, (HARMONICS, atom_count), 0)
    count = planes_ref.shape[0] // 2
    for index in devices:
        spot = slice(index * atom_count, (index + 1) * atom_count)
        feature = jnp.concatenate([recv_ref[index, 0:own_channels, :]] * together, axis=0)
        for part in range(2):
            for tile in range(tiles):
                first = tile * together
                height = jnp.broadcast_to(axes_ref[4 + part, first : first + 1, spot], sublane.shape)
                for n in range(1, together):
                    height = jnp.where(
                        sublane >= n * own_channels, axes_ref[4 + part, first + n : first + n + 1, spot], height
                    )
                row = part * lanes + tile * HARMONICS
                heights[row : row + HARMONICS, spot] = height
                lifted[row : row + HARMONICS, spot] = feature * height
        products = [
            axes_ref[first_axis, m : m + 1, spot] * axes_ref[second_axis, :, spot]
            for first_axis, second_axis in ((0, 2), (0, 3), (1, 2), (1, 3))
            for m in range(KMAX + 1)
        ]
        for pair in range(len(products) // 2):
            both = jnp.concatenate(products[2 * pair : 2 * pair + 2], axis=0)
            high = both.astype(BF16)
            rows = slice(2 * HARMONICS * pair, 2 * HARMONICS * (pair + 1))
            planes_ref[rows, spot] = high
            rows = slice(count + rows.start, count + rows.stop)
            planes_ref[rows, spot] = (both - high.astype(F32)).astype(BF16)


def wave_sums(own_channels, recv_ref, planes_ref, axes_ref, heights, lifted):
    chunk, _, atom_count = recv_ref.shape
    lanes = lifted.shape[0] // 2
    group = math.gcd(chunk, 16)
    count = planes_ref.shape[0] // 2
    total = 0.0
    for first in range(0, chunk, group):
        devices = range(first, first + group)
        wave_planes(own_channels, recv_ref, planes_ref, axes_ref, heights, lifted, devices)
        spot = slice(first * atom_count, (first + group) * atom_count)
        values = lifted[:, spot]
        high = values.astype(BF16)
        low = (values - high.astype(F32)).astype(BF16)
        main = dot(planes_ref[0:count, spot], jnp.concatenate([high, low], axis=0), 1, 1)
        total = total + main[:, : 2 * lanes] + (main[:, 2 * lanes :] + dot(planes_ref[count:, spot], high, 1, 1))
    return total


SIGNS = ((1.0, 1.0), (1.0, -1.0), (-1.0, 1.0), (-1.0, -1.0))


def wave_blocks(sums_ref, phi_ref):
    _, rows, lanes = phi_ref.shape
    sums = sums_ref[...]
    cos_part, sin_part = sums[:, :lanes], sums[:, lanes:]
    cc_c, cs_c, sc_c, ss_c = (cos_part[p * rows : (p + 1) * rows] for p in range(4))
    cc_s, cs_s, sc_s, ss_s = (sin_part[p * rows : (p + 1) * rows] for p in range(4))
    for sign_id, (s1, s2) in enumerate(SIGNS):
        real = cc_c - s1 * s2 * ss_c - s1 * sc_s - s2 * cs_s
        imag = cc_s - s1 * s2 * ss_s + s1 * sc_c + s2 * cs_c
        phi = phi_ref[sign_id]
        yield s1, s2, phi * real, phi * imag, real, imag


def wave_virial(own_channels, lengths, sums_ref, phi_ref, width_ref, shape):
    _, rows, lanes = phi_ref.shape
    even = first_odd = second_odd = both_odd = jnp.zeros((rows, lanes), F32)
    for s1, s2, dreal, dimag, real, imag in wave_blocks(sums_ref, phi_ref):
        power = dreal * real + dimag * imag
        even = even + power
        first_odd = first_odd + s1 * power
        second_odd = second_odd + s2 * power
        both_odd = both_odd + s1 * s2 * power
    width = width_ref[0:1, :]
    k1, k2, k3 = grid_numbers(rows, lanes, own_channels, lengths)

    def total_of(values):
        return jnp.sum(jnp.sum(values, axis=0, keepdims=True), axis=1, keepdims=True)

    energy = 0.5 * total_of(even)
    scaled = width * even
    terms = {
        (0, 0): energy - total_of(k1 * k1 * scaled),
        (1, 1): energy - total_of(k2 * k2 * scaled),
        (2, 2): energy - total_of(k3 * k3 * scaled),
        (0, 1): -total_of(k1 * k2 * width * both_odd),
        (0, 2): -total_of(k1 * k3 * width * first_odd),
        (1, 2): -total_of(k2 * k3 * width * second_odd),
    }
    return virial_row(terms, shape)


def wave_coefficients(sums_ref, phi_ref, coefficients_ref):
    _, rows, lanes = phi_ref.shape
    zero = jnp.zeros((rows, lanes), F32)
    d_cc_c = d_cc_s = d_cs_c = d_cs_s = d_sc_c = d_sc_s = d_ss_c = d_ss_s = zero
    for s1, s2, dreal, dimag, _, _ in wave_blocks(sums_ref, phi_ref):
        d_cc_c, d_ss_c = d_cc_c + dreal, d_ss_c - s1 * s2 * dreal
        d_sc_s, d_cs_s = d_sc_s - s1 * dreal, d_cs_s - s2 * dreal
        d_cc_s, d_ss_s = d_cc_s + dimag, d_ss_s - s1 * s2 * dimag
        d_sc_c, d_cs_c = d_sc_c + s1 * dimag, d_cs_c + s2 * dimag
    values = jnp.concatenate(
        [
            jnp.concatenate(pair, axis=1)
            for pair in ((d_cc_c, d_cc_s), (d_cs_c, d_cs_s), (d_sc_c, d_sc_s), (d_ss_c, d_ss_s))
        ],
        axis=0,
    )
    cc, cs, sc, ss = (values[p * rows : (p + 1) * rows] for p in range(4))
    row_id = lax.broadcasted_iota(jnp.int32, (rows, 2 * lanes), 0)
    m1 = (row_id // HARMONICS).astype(F32)
    m2 = (row_id % HARMONICS).astype(F32)
    along_x = jnp.concatenate([m1 * sc, m1 * ss, -m1 * cc, -m1 * cs], axis=0)
    along_y = jnp.concatenate([m2 * cs, -m2 * cc, m2 * ss, -m2 * sc], axis=0)
    values = jnp.concatenate([values, along_x, along_y], axis=1)
    turned = values.T
    high = turned.astype(BF16)
    count = turned.shape[0]
    coefficients_ref[0:count, :] = high
    coefficients_ref[count:, :] = (turned - high.astype(F32)).astype(BF16)


def wave_spread(planes_ref, coefficients):
    values = coefficients[...]
    count = values.shape[0] // 2
    both = jnp.concatenate([values[:count], values[:count]], axis=1)
    return dot(both, planes_ref[...], 1, 0) + dot(values[count:], planes_ref[0 : values.shape[1], :], 1, 0)


def wave_back(own_channels, lengths, planes_ref, heights, lifted, coefficients, send_ref, push_ref):
    chunk, _, atom_count = push_ref.shape
    together, tiles = tile_layout(own_channels)
    lanes = tiles * HARMONICS
    sublane = lax.broadcasted_iota(jnp.int32, (HARMONICS, atom_count), 0)
    numbers = [(sublane // own_channels + 1 + tile * together).astype(F32) for tile in range(tiles)]
    result = wave_spread(planes_ref, coefficients)
    for index in range(chunk):
        spot = slice(index * atom_count, (index + 1) * atom_count)
        part = result[:, spot]
        feature = grad_x = grad_y = grad_z = jnp.zeros((HARMONICS, atom_count), F32)
        for tile in range(tiles):
            a, b = tile * HARMONICS, lanes + tile * HARMONICS
            on_cos, on_sin = part[a : a + HARMONICS], part[b : b + HARMONICS]
            feature = feature + on_cos * heights[a : a + HARMONICS, spot] + on_sin * heights[b : b + HARMONICS, spot]
            lift_cos = lifted[a : a + HARMONICS, spot]
            lift_sin = lifted[b : b + HARMONICS, spot]
            grad_z = grad_z + numbers[tile] * (on_sin * lift_cos - on_cos * lift_sin)
            a, b = a + 2 * lanes, b + 2 * lanes
            grad_x = grad_x + part[a : a + HARMONICS] * lift_cos + part[b : b + HARMONICS] * lift_sin
            a, b = a + 2 * lanes, b + 2 * lanes
            grad_y = grad_y + part[a : a + HARMONICS] * lift_cos + part[b : b + HARMONICS] * lift_sin
        total = feature[0:own_channels]
        for n in range(1, together):
            total = total + feature[n * own_channels : (n + 1) * own_channels]
        send_ref[index, 0:own_channels, :] = total
        pieces = (
            grad_x * (2.0 * math.pi / lengths[0]),
            grad_y * (2.0 * math.pi / lengths[1]),
            grad_z * (2.0 * math.pi / lengths[2]),
        )
        for row, piece in enumerate(pieces):
            push_ref[index, row : row + 1, :] = jnp.sum(piece, axis=0, keepdims=True)


def virial_row(terms, shape):
    lane = lax.broadcasted_iota(jnp.int32, shape, 1)
    row = jnp.zeros(shape, F32)
    for (i, j), value in terms.items():
        spots = (lane == 3 * i + j) | (lane == 3 * j + i)
        row = jnp.where(spots, value, row)
    return row


def short_back_kernel(
    dims,
    recv_ref,
    vec_ref,
    kind_ref,
    dupd_ref,
    slope_ref,
    owner_ref,
    back_ref,
    push_ref,
    send_ref,
    fgrad,
    dpool,
    parts,
):
    own_channels, row_count, col_count, species_count, radial_count = dims
    slot_count, atom_count = owner_ref.shape
    channel_count = back_ref.shape[1]
    device_count = send_ref.shape[0]
    table_rows = round_up(len(DIRECTIONS) + 1, 16)
    for q in range(own_channels):
        low, high = q * device_count, min(channel_count, (q + 1) * device_count)
        fgrad[low:high, :] = recv_ref[0 : high - low, q, :]
    dbefore = (fgrad[...] + dupd_ref[...]) * slope_ref[...]
    dpool[...] = dot(back_ref[...], dbefore, 1, 0, GOOD)
    vectors = [vec_ref[part] for part in range(3)]
    squared = vectors[0] * vectors[0] + vectors[1] * vectors[1] + vectors[2] * vectors[2]
    kind = kind_ref[...]
    sums = [jnp.zeros(kind.shape, F32) for _ in range(species_count)]
    for order in range(radial_count):
        basis = jnp.exp(squared * (-radial_rate(order)))
        for k in range(species_count):
            spot = k * radial_count + order
            sums[k] = sums[k] + basis * dpool[spot : spot + 1, :]
    slope = jnp.zeros(kind.shape, F32)
    for k in range(species_count):
        slope = jnp.where(kind == float(k), sums[k], slope)
    grads = [slope * vector for vector in vectors]

    def total_of(values):
        return jnp.sum(jnp.sum(values, axis=0, keepdims=True), axis=1, keepdims=True)

    terms = {
        (i, j): -total_of(grads[i] * vectors[j]) for i in range(3) for j in range(i, 3)
    }
    virial = virial_row(terms, (1, atom_count))
    for part in range(3):
        parts[2 * part], parts[2 * part + 1] = split(grads[part])

    sublane = lax.broadcasted_iota(jnp.int32, (atom_count, atom_count), 0)
    table_id = lax.broadcasted_iota(jnp.int32, (table_rows, atom_count), 0)
    group = 8
    scattered = jnp.zeros((atom_count, 6 * table_rows), F32)
    for low in range(0, slot_count, group):
        hots, columns = [], []
        for s in range(low, low + group):
            ids = owner_ref[s : s + 1, :]
            hots.append(jnp.where(sublane == (ids & (atom_count - 1)), 1.0, 0.0).astype(BF16))
            mine = table_id == ids // atom_count
            columns.append(
                jnp.concatenate(
                    [
                        jnp.where(mine, parts[p, s : s + 1, :], 0.0).astype(BF16)
                        for p in range(6)
                    ],
                    axis=0,
                )
            )
        scattered = scattered + dot(
            jnp.concatenate(hots, axis=1), jnp.concatenate(columns, axis=1), 1, 1
        )
    rows = scattered.T
    send_ref[...] = push_ref[...]
    send_ref[:, 3, :] += jnp.broadcast_to(virial, (device_count, atom_count))
    me = neighbour_of((0, 0), row_count, col_count)
    for part in range(3):
        low = 2 * part * table_rows
        both = rows[low : low + table_rows] + rows[low + table_rows : low + 2 * table_rows]
        send_ref[me, part, :] += both[0, :] - jnp.sum(grads[part], axis=0)
        for order, step in enumerate(DIRECTIONS):
            target = neighbour_of(step, row_count, col_count)
            send_ref[target, part, :] += both[1 + order, :]


def final_kernel(volume, recv_ref, forces_ref, virial_ref):
    total = jnp.sum(recv_ref[...], axis=0)
    for part in range(3):
        forces_ref[part] = -total[part : part + 1, :]
    virial = total[3:4, :] * (1.0 / volume)
    for i in range(3):
        virial_ref[i : i + 1, :] = virial[:, 3 * i : 3 * i + 3]


def per_device(
    positions,
    species,
    counts,
    neighbours,
    ghost_index,
    wave_numbers,
    embedding,
    w_radial,
    w_mix,
    w_read,
    w_out,
    amplitude,
    kernel_width,
    filter_gain,
):
    row_count = lax.axis_size("row")
    col_count = lax.axis_size("col")
    device_count = row_count * col_count
    atom_count = positions.shape[3]
    slot_count = neighbours.shape[2]
    direction_count, ghost_count = ghost_index.shape[2:]
    species_count, channel_count = embedding.shape
    radial_count = w_radial.shape[0]
    own_channels = -(-channel_count // device_count)
    lengths = (CELL_EDGE * row_count, CELL_EDGE * col_count, HEIGHT)
    volume = lengths[0] * lengths[1] * lengths[2]
    rows = (KMAX + 1) * HARMONICS
    lanes = tile_layout(own_channels)[1] * HARMONICS
    _, shared = direction_slots(row_count, col_count)
    slab_first = round_up(4 + shared, 2) // 2 * atom_count
    slab_features = round_up(own_channels, 4)
    chunk = math.gcd(device_count, 32)
    chunk_count = device_count // chunk

    def exchange(slabs):
        return lax.all_to_all(slabs, AXES, 0, 0, tiled=True)

    def shape(*dims):
        return jax.ShapeDtypeStruct(dims, F32)

    def scratch(*dims):
        return pltpu.VMEM(dims, F32)

    def call(kernel, out_shape, vmem=16, **options):
        return pl.pallas_call(
            kernel,
            out_shape=out_shape,
            compiler_params=pltpu.CompilerParams(vmem_limit_bytes=vmem * 1024 * 1024),
            **options,
        )

    ids = neighbours.reshape(slot_count, atom_count)
    ghosts = ghost_index.reshape(direction_count, ghost_count)
    mesh_counts = (row_count, col_count)
    inputs = (
        counts.reshape(1, atom_count),
        ids,
        w_radial,
        embedding,
        w_mix,
    )
    wave_inputs = (
        w_read,
        w_out.reshape(1, -1),
        filter_gain,
        wave_numbers,
        amplitude.reshape(1, -1),
        kernel_width.reshape(1, -1),
    )

    def fetched(*arrays):
        return [pltpu.with_memory_space_constraint(x, pltpu.HBM) for x in arrays]

    kept = pl.BlockSpec(memory_space=pltpu.HBM)
    near = pl.BlockSpec(memory_space=pltpu.VMEM)
    send, *inputs = call(
        functools.partial(pack_kernel, mesh_counts, len(inputs)),
        (shape(device_count, 2, slab_first),)
        + tuple(jax.ShapeDtypeStruct(x.shape, x.dtype) for x in inputs),
        in_specs=[kept] * (3 + len(inputs)),
        scratch_shapes=[
            scratch(3, 1, atom_count),
            pltpu.VMEM((1, atom_count), jnp.int32),
            pltpu.VMEM(ghosts.shape, jnp.int32),
            pltpu.SemaphoreType.DMA((3,)),
            pltpu.SemaphoreType.DMA((len(inputs),)),
        ],
        name="pack",
    )(*fetched(positions.reshape(3, 1, atom_count), species.reshape(1, atom_count), ghosts, *inputs))
    live, ids, w_radial, embedding, w_mix = inputs
    cells = exchange(send)

    pooled_rows = species_count * radial_count
    send, vectors, kinds, owners, updated, slope, mixed = call(
        functools.partial(short_forward_kernel, (own_channels,) + mesh_counts),
        (
            shape(device_count, slab_features, atom_count),
            shape(3, slot_count, atom_count),
            shape(slot_count, atom_count),
            jax.ShapeDtypeStruct((slot_count, atom_count), jnp.int32),
            shape(channel_count, atom_count),
            shape(channel_count, atom_count),
            shape(pooled_rows, channel_count),
        ),
        scratch_shapes=[
            scratch(4, 16, atom_count),
            pltpu.VMEM((direction_count, atom_count), jnp.int32),
            pltpu.VMEM((16, atom_count), jnp.int32),
            scratch(pooled_rows, atom_count),
            scratch(pooled_rows, channel_count),
            scratch(round_up(species_count, 8), channel_count),
        ],
        name="short_forward",
    )(cells, live, ids, w_radial, embedding, w_mix)
    send, cells, updated, mixed = lax.optimization_barrier((send, cells, updated, mixed))
    features = exchange(send)

    axes_block = (6, HARMONICS, chunk * atom_count)
    axes_shape = shape(6, HARMONICS, device_count * atom_count)
    table_dims = (col_count, chunk_count, lengths)
    cells_inputs, axes_outputs = (), ()
    if chunk_count == 1:
        cells_inputs, axes_outputs = (cells,), (axes_shape,)
    dupd, back, phi, width, *axes = call(
        functools.partial(
            weights_kernel,
            (device_count, channel_count, own_channels, lengths, volume, radial_count),
            table_dims if chunk_count == 1 else None,
        ),
        (
            shape(channel_count, atom_count),
            shape(pooled_rows, channel_count),
            shape(4, rows, lanes),
            shape(8, lanes),
        )
        + axes_outputs,
        in_specs=[near] * (2 + len(cells_inputs)) + [kept] * len(wave_inputs),
        scratch_shapes=[pltpu.VMEM(x.shape, x.dtype) for x in wave_inputs]
        + [pltpu.SemaphoreType.DMA((len(wave_inputs),))],
        cost_estimate=pl.CostEstimate(
            flops=2 * 4 * rows * filter_gain.shape[0] * 3 * lanes,
            bytes_accessed=4 * filter_gain.size,
            transcendentals=0,
        ),
        name="weights",
    )(updated, mixed, *cells_inputs, *fetched(*wave_inputs))
    if chunk_count > 1:
        axes = [
            call(
                functools.partial(table_kernel, table_dims),
                axes_shape,
                grid=(chunk_count,),
                in_specs=[pl.BlockSpec((chunk, 2, slab_first), lambda i: (i, 0, 0))],
                out_specs=pl.BlockSpec(axes_block, lambda i: (0, 0, i)),
                name="tables",
            )(cells)
        ]
    features, dupd, back = lax.optimization_barrier((features, dupd, back))

    plane = pltpu.VMEM((8 * rows, chunk * atom_count), BF16)
    wave_scratch = [plane] + [scratch(2 * lanes, chunk * atom_count)] * 2
    features_block = (chunk, slab_features, atom_count)
    wave_options = {}
    if chunk_count > 1:
        wave_options = dict(
            grid=(2, chunk_count),
            in_specs=[
                pl.BlockSpec(features_block, lambda p, i: (i, 0, 0)),
                pl.BlockSpec(axes_block, lambda p, i: (0, 0, i)),
                pl.BlockSpec((4, rows, lanes), lambda p, i: (0, 0, 0)),
                pl.BlockSpec((8, lanes), lambda p, i: (0, 0)),
            ],
            out_specs=(
                pl.BlockSpec(features_block, lambda p, i: (i * p, 0, 0)),
                pl.BlockSpec((chunk, 4, atom_count), lambda p, i: (i * p, 0, 0)),
            ),
        )
    send, push = call(
        functools.partial(wave_kernel, (own_channels, chunk_count, lengths)),
        (shape(device_count, slab_features, atom_count), shape(device_count, 4, atom_count)),
        vmem=32,
        scratch_shapes=wave_scratch
        + [scratch(4 * rows, 2 * lanes), pltpu.VMEM((12 * lanes, 4 * rows), BF16)],
        name="waves",
        **wave_options,
    )(features, *axes, phi, width)
    gradients = exchange(send)

    send = call(
        functools.partial(
            short_back_kernel, (own_channels,) + mesh_counts + (species_count, radial_count)
        ),
        shape(device_count, 4, atom_count),
        scratch_shapes=[
            scratch(channel_count, atom_count),
            scratch(pooled_rows, atom_count),
            scratch(6, slot_count, atom_count),
        ],
        name="short_back",
    )(gradients, vectors, kinds, dupd, slope, owners, back, push)
    returned = exchange(send)

    forces, virial = call(
        functools.partial(final_kernel, volume),
        (shape(3, 1, atom_count), shape(3, 3)),
        name="total",
    )(returned)
    return (forces[:, None], virial)


def solution(mesh):
    return jax.shard_map(
        per_device,
        mesh=mesh,
        in_specs=(
            P(None, "row", "col", None),
            P("row", "col", None),
            P("row", "col", None),
            P("row", "col", None, None),
            P("row", "col", None, None),
            P(),
            P(),
            P(),
            P(),
            P(),
            P(),
            P(),
            P(),
            P(),
        ),
        out_specs=(P(None, "row", "col", None), P()),
        check_vma=False,
    )
```

```python
import functools
import math

import jax
import jax.numpy as jnp
from jax import lax
from jax.experimental import pallas as pl
from jax.experimental.pallas import tpu as pltpu
from jax.sharding import PartitionSpec as P

CELL_EDGE = 12.0
HEIGHT = 36.0
KMAX = 6
HARMONICS = 8
EXACT = lax.Precision.HIGHEST
GOOD = lax.Precision.HIGH
DIRECTIONS = ((-1, -1), (-1, 0), (-1, 1), (0, -1), (0, 1), (1, -1), (1, 0), (1, 1))
F32 = jnp.float32
BF16 = jnp.bfloat16
AXES = ("row", "col")


def radial_rate(order):
    return 0.003 * 1.6**order


def round_up(value, step):
    return -(-value // step) * step


def direction_slots(row_count, col_count):
    seen = {}
    slots = []
    for row_step, col_step in DIRECTIONS:
        key = (row_step % row_count, col_step % col_count)
        slots.append(seen.get(key, 0))
        seen[key] = slots[-1] + 1
    return slots, max(seen.values())


def tile_layout(own_channels):
    shared = HARMONICS // own_channels
    return shared, -(-KMAX // shared)


def dot(lhs, rhs, lhs_dim, rhs_dim, precision=None):
    return lax.dot_general(
        lhs,
        rhs,
        (((lhs_dim,), (rhs_dim,)), ((), ())),
        precision=precision,
        preferred_element_type=F32,
    )


def split(values):
    high = values.astype(BF16).astype(F32)
    return high, values - high


def wave_weights(dims, gain_ref, waves_ref, amp_ref, width_ref, phi_ref, width_out_ref):
    device_count, channel_count, own_channels, lengths, volume = dims
    me = lax.axis_index("row") * lax.axis_size("col") + lax.axis_index("col")
    wave_count = gain_ref.shape[0]
    rows = (KMAX + 1) * HARMONICS
    together, tiles = tile_layout(own_channels)
    lanes = tiles * HARMONICS
    place = lax.broadcasted_iota(jnp.int32, (8, channel_count), 0) * device_count + me
    chosen = (lax.broadcasted_iota(jnp.int32, (8, channel_count), 1) == place).astype(F32).astype(BF16)
    first, second, third = waves_ref[0:1, :], waves_ref[1:2, :], waves_ref[2:3, :]
    sign = jnp.where(first < 0, 2, 0) + jnp.where(second < 0, 1, 0)
    key = sign * rows + jnp.abs(first) * HARMONICS + jnp.abs(second)
    spots = lax.broadcasted_iota(jnp.int32, (4 * rows, wave_count), 0) == key
    onehot = jnp.where(spots, 1.0, 0.0).astype(BF16)
    height = lax.broadcasted_iota(jnp.int32, (HARMONICS, wave_count), 0) // own_channels + 1
    here = [height + tile * together == third for tile in range(tiles)]
    rest = gain_ref[...]
    summed = 0.0
    for _ in range(3):
        part = rest.astype(BF16)
        rest = rest - part.astype(F32)
        mine = dot(chosen, part, 1, 1)
        mine = jnp.concatenate([mine[:own_channels]] * together, axis=0)
        wide = jnp.concatenate([jnp.where(spots, mine, 0.0) for spots in here], axis=0)
        summed = summed + dot(onehot, wide.astype(BF16), 1, 1)
    lane = lax.broadcasted_iota(jnp.int32, (8, channel_count), 1)
    wanted = jnp.minimum(lane % own_channels * device_count + me, channel_count - 1)
    amp = jnp.take_along_axis(jnp.broadcast_to(amp_ref[...], (8, channel_count)), wanted, axis=1)
    width = jnp.take_along_axis(
        jnp.broadcast_to(width_ref[...], (8, channel_count)), wanted, axis=1
    )
    amp, width = amp[0:1, :lanes], width[0:1, :lanes]
    k1, k2, k3 = grid_numbers(rows, lanes, own_channels, lengths)
    squared = k1 * k1 + k2 * k2 + k3 * k3
    base = amp * jnp.exp(-width * squared) * (1.0 / volume)
    for sign_id in range(4):
        phi_ref[sign_id] = base * summed[sign_id * rows : (sign_id + 1) * rows, :]
    width_out_ref[...] = jnp.broadcast_to(width, (8, lanes))


def grid_numbers(rows, lanes, own_channels, lengths):
    row_id = lax.broadcasted_iota(jnp.int32, (rows, lanes), 0)
    lane_id = lax.broadcasted_iota(jnp.int32, (rows, lanes), 1)
    k1 = (row_id // HARMONICS).astype(F32) * (2.0 * math.pi / lengths[0])
    k2 = (row_id % HARMONICS).astype(F32) * (2.0 * math.pi / lengths[1])
    k3 = (lane_id // own_channels + 1).astype(F32) * (2.0 * math.pi / lengths[2])
    return k1, k2, k3


def neighbour_of(step, row_count, col_count):
    row = lax.rem(lax.axis_index("row") + step[0] + row_count, row_count)
    col = lax.rem(lax.axis_index("col") + step[1] + col_count, col_count)
    return row * col_count + col


def slab_rows(slab, rows, atom_count):
    width = slab.shape[-1] // atom_count
    return [
        slab[row // width : row // width + 1, row % width * atom_count : (row % width + 1) * atom_count]
        for row in rows
    ]


def pack_kernel(counts, copied, positions_ref, species_ref, ghosts_ref, *refs):
    row_count, col_count = counts
    sources, (send_ref, *targets) = refs[:copied], refs[copied : 2 * copied + 1]
    positions, species, ghosts, first_sems, sems = refs[2 * copied + 1 :]
    firsts = ((positions_ref, positions), (species_ref, species), (ghosts_ref, ghosts))
    firsts = start_copies(firsts, first_sems)
    others = start_copies(tuple(zip(sources, targets)), sems)
    device_count = send_ref.shape[0]
    atom_count = species.shape[1]
    width = send_ref.shape[2] // atom_count
    slots, _ = direction_slots(row_count, col_count)
    for copy in firsts:
        copy.wait()
    rows = [positions[0], positions[1], positions[2], species[...].astype(F32)]
    for row, values in enumerate(rows):
        low = row % width * atom_count
        send_ref[:, row // width, low : low + atom_count] = jnp.broadcast_to(
            values, (device_count, atom_count)
        )
    for order, step in enumerate(DIRECTIONS):
        target = neighbour_of(step, row_count, col_count)
        row = 4 + slots[order]
        low = row % width * atom_count
        send_ref[target, row // width, low : low + atom_count] = ghosts[order, :].astype(F32)
    for copy in others:
        copy.wait()


def start_copies(pairs, sems):
    copies = [
        pltpu.make_async_copy(source, target, sems.at[spot])
        for spot, (source, target) in enumerate(pairs)
    ]
    for copy in copies:
        copy.start()
    return copies


def weights_kernel(dims, table_dims, upd_ref, mixed_ref, *refs):
    cells, refs = refs[: len(refs) - 17 - bool(table_dims)], refs[len(refs) - 17 - bool(table_dims) :]
    sources, (dupd_ref, back_ref, phi_ref, width_out_ref), refs = refs[:6], refs[6:10], refs[10:]
    axes, targets, sems = refs[: len(refs) - 7], refs[-7:-1], refs[-1]
    copies = start_copies(tuple(zip(sources, targets)), sems)
    if table_dims:
        table_kernel(table_dims, *cells, *axes)
    pooled_rows, channel_count = mixed_ref.shape
    radial_count = dims[5]
    order_id = lax.broadcasted_iota(jnp.int32, (pooled_rows, channel_count), 0) % radial_count
    factor = jnp.zeros((pooled_rows, channel_count), F32)
    for order in range(radial_count):
        factor = jnp.where(order_id == order, -2.0 * radial_rate(order), factor)
    back_ref[...] = mixed_ref[...] * factor
    for copy in copies[:2]:
        copy.wait()
    readout_gradient(upd_ref, targets[0], targets[1], dupd_ref)
    for copy in copies[2:]:
        copy.wait()
    wave_weights(dims[:5], *targets[2:], phi_ref, width_out_ref)


def short_forward_kernel(
    dims,
    cells_ref,
    counts_ref,
    ids_ref,
    radial_ref,
    embed_ref,
    mix_ref,
    send_ref,
    vec_ref,
    kind_ref,
    owner_ref,
    upd_ref,
    slope_ref,
    mixed_ref,
    table,
    lists,
    codes,
    pooled,
    weights,
    kinds8,
):
    own_channels, row_count, col_count = dims
    slot_count, atom_count = ids_ref.shape
    species_count, channel_count = embed_ref.shape
    radial_count = radial_ref.shape[0]
    device_count = send_ref.shape[0]
    slots, _ = direction_slots(row_count, col_count)
    for k in range(species_count):
        weights[k * radial_count : (k + 1) * radial_count, :] = (
            radial_ref[...] * embed_ref[k : k + 1, :] * (1.0 / slot_count)
        )
    weights[...] = dot(weights[...], mix_ref[...], 1, 0, EXACT)
    mixed_ref[...] = weights[...]
    own = slab_rows(cells_ref[neighbour_of((0, 0), row_count, col_count)], range(4), atom_count)
    domains, places = [], []
    for step in DIRECTIONS:
        key = (step[0] % row_count, step[1] % col_count)
        if key not in domains:
            domains.append(key)
        places.append(domains.index(key))
    for part in range(3):
        table[part, 0:1, :] = own[part]
    for place, key in enumerate(domains):
        block = slab_rows(cells_ref[neighbour_of(key, row_count, col_count)], range(3), atom_count)
        for part in range(3):
            table[part, 8 + place : 9 + place, :] = block[part]
    for order, step in enumerate(DIRECTIONS):
        list_row = 4 + slots[len(DIRECTIONS) - 1 - order]
        source = neighbour_of(step, row_count, col_count)
        kinds_row, list_values = slab_rows(cells_ref[source], (3, list_row), atom_count)
        table[3, 8 + order : 9 + order, :] = kinds_row
        lists[order : order + 1, :] = list_values.astype(jnp.int32)
    picks = lists[...]
    ghost_kinds = jnp.take_along_axis(table[3, 8:16, :], picks, axis=1)
    codes[8:16, :] = picks + atom_count * ghost_kinds.astype(jnp.int32)
    codes[0:1, :] = lax.broadcasted_iota(
        jnp.int32, (1, atom_count), 1
    ) + atom_count * own[3].astype(jnp.int32)

    ids = ids_ref[...]
    lane = ids & (atom_count - 1)
    source = ids // atom_count

    def picked(ref, index, marks):
        values = jnp.take_along_axis(jnp.broadcast_to(ref[0:1, :], ids.shape), index, axis=1)
        for place, mark in enumerate(marks):
            wide = jnp.broadcast_to(ref[8 + place : 9 + place, :], ids.shape)
            values = jnp.where(mark, jnp.take_along_axis(wide, index, axis=1), values)
        return values

    marks = [source == order + 1 for order in range(len(DIRECTIONS))]
    code = picked(codes, lane, marks)
    owner = code & (atom_count - 1)
    owner_ref[...] = owner + source * atom_count
    merged = []
    for place in range(len(domains)):
        mine = [mark for mark, other in zip(marks, places) if other == place]
        merged.append(functools.reduce(jnp.logical_or, mine))
    gathered = [picked(table.at[part], owner, merged) for part in range(3)]
    for axis in range(2):
        shift = jnp.zeros(ids.shape, F32)
        for mark, step in zip(marks, DIRECTIONS):
            if step[axis]:
                shift = jnp.where(mark, step[axis] * CELL_EDGE, shift)
        gathered[axis] = gathered[axis] + shift
    gathered.append((code // atom_count).astype(F32))
    slot = lax.broadcasted_iota(jnp.int32, ids.shape, 0)
    kind = jnp.where(slot < counts_ref[...], gathered[3], -1.0)
    kind_ref[...] = kind
    squared = jnp.zeros(ids.shape, F32)
    for part in range(3):
        vector = gathered[part] - own[part]
        vec_ref[part] = vector
        squared = squared + vector * vector
    masks = [kind == float(k) for k in range(species_count)]
    for order in range(radial_count):
        basis = jnp.exp(squared * (-radial_rate(order)))
        for k in range(species_count):
            spot = k * radial_count + order
            pooled[spot : spot + 1, :] = jnp.sum(
                jnp.where(masks[k], basis, 0.0), axis=0, keepdims=True
            )
    kinds8[...] = jnp.zeros_like(kinds8)
    kinds8[0:species_count, :] = embed_ref[...]
    own_hot = (
        lax.broadcasted_iota(jnp.int32, (kinds8.shape[0], atom_count), 0).astype(F32) == own[3]
    ).astype(F32)
    initial = dot(kinds8[...], own_hot, 0, 0, EXACT)
    before = dot(weights[...], pooled[...], 0, 0, GOOD)
    gate = 1.0 / (1.0 + jnp.exp(-before))
    updated = initial + before * gate
    slope_ref[...] = gate + before * gate * (1.0 - gate)
    for q in range(own_channels):
        low, high = q * device_count, min(channel_count, (q + 1) * device_count)
        send_ref[0 : high - low, q, :] = updated[low:high, :]
        if high - low < device_count:
            send_ref[high - low :, q, :] = jnp.zeros(
                (device_count - (high - low), atom_count), F32
            )
    upd_ref[...] = updated


def readout_gradient(upd_ref, read_ref, out_ref, dupd_ref):
    channel_count, atom_count = upd_ref.shape
    readout = dot(read_ref[...], upd_ref[...], 0, 0, GOOD)
    gate = 1.0 / (1.0 + jnp.exp(-readout))
    scale = jnp.broadcast_to(out_ref[...], (channel_count, channel_count)).T
    dread = scale[:, 0:atom_count] * (gate + readout * gate * (1.0 - gate))
    dupd_ref[...] = dot(read_ref[...], dread, 1, 0, GOOD)


def turn_tables(turns, multiples):
    angle = turns * multiples
    halves = jnp.floor(2.0 * angle + 0.5)
    rest = angle - 0.5 * halves
    sign = 1.0 - 2.0 * (halves - 2.0 * jnp.floor(0.5 * halves))
    square = rest * rest

    def series(first, last):
        terms = [
            (-1.0) ** (p // 2) * (2.0 * math.pi) ** p / math.factorial(p)
            for p in range(first, last + 1, 2)
        ]
        total = jnp.full_like(square, terms[-1])
        for term in reversed(terms[:-1]):
            total = total * square + term
        return total

    return sign * series(0, 12), sign * rest * series(1, 13)


def table_kernel(dims, cells_ref, axes_ref):
    col_count, chunk_count, lengths = dims
    chunk = cells_ref.shape[0]
    atom_count = axes_ref.shape[2] // chunk
    first_device = pl.program_id(0) * chunk if chunk_count > 1 else 0
    multiples = lax.broadcasted_iota(jnp.int32, (HARMONICS, atom_count), 0).astype(F32)

    def one(index, _):
        device = first_device + index
        spot = pl.ds(pl.multiple_of(index * atom_count, atom_count), atom_count)
        block = slab_rows(cells_ref[index], range(3), atom_count)
        corner_row = (device // col_count).astype(F32) * CELL_EDGE
        corner_col = (device % col_count).astype(F32) * CELL_EDGE
        turns = (
            (block[0] + corner_row) * (1.0 / lengths[0]),
            (block[1] + corner_col) * (1.0 / lengths[1]),
            block[2] * (1.0 / lengths[2]),
        )
        for axis in range(3):
            numbers = multiples + 1.0 if axis == 2 else multiples
            cos, sin = turn_tables(turns[axis], numbers)
            axes_ref[2 * axis, :, spot] = cos
            axes_ref[2 * axis + 1, :, spot] = sin
        return 0

    lax.fori_loop(0, chunk, one, 0, unroll=4)


def wave_kernel(
    dims,
    recv_ref,
    axes_ref,
    phi_ref,
    width_ref,
    send_ref,
    push_ref,
    planes_ref,
    heights,
    lifted,
    sums,
    coefficients,
):
    own_channels, chunk_count, lengths = dims
    planes = (planes_ref, axes_ref, heights, lifted)

    def back():
        wave_back(own_channels, lengths, planes_ref, heights, lifted, coefficients, send_ref, push_ref)
        virial = wave_virial(own_channels, lengths, sums, phi_ref, width_ref, (1, push_ref.shape[2]))
        push_ref[:, 3, :] = jnp.broadcast_to(virial, (push_ref.shape[0], push_ref.shape[2]))

    if chunk_count == 1:
        sums[...] = wave_sums(own_channels, recv_ref, *planes)
        wave_coefficients(sums, phi_ref, coefficients)
        back()
        return
    phase, chunk_id = pl.program_id(0), pl.program_id(1)

    @pl.when((phase == 0) & (chunk_id == 0))
    def _():
        sums[...] = jnp.zeros_like(sums)

    part = wave_sums(own_channels, recv_ref, *planes)

    @pl.when(phase == 0)
    def _():
        sums[...] += part

    @pl.when((phase == 1) & (chunk_id == 0))
    def _():
        wave_coefficients(sums, phi_ref, coefficients)

    @pl.when(phase == 1)
    def _():
        back()


def wave_planes(own_channels, recv_ref, planes_ref, axes_ref, heights, lifted, devices):
    atom_count = recv_ref.shape[2]
    together, tiles = tile_layout(own_channels)
    lanes = tiles * HARMONICS
    sublane = lax.broadcasted_iota(jnp.int32, (HARMONICS, atom_count), 0)
    count = planes_ref.shape[0] // 2
    for index in devices:
        spot = slice(index * atom_count, (index + 1) * atom_count)
        feature = jnp.concatenate([recv_ref[index, 0:own_channels, :]] * together, axis=0)
        for part in range(2):
            for tile in range(tiles):
                first = tile * together
                height = jnp.broadcast_to(axes_ref[4 + part, first : first + 1, spot], sublane.shape)
                for n in range(1, together):
                    height = jnp.where(
                        sublane >= n * own_channels, axes_ref[4 + part, first + n : first + n + 1, spot], height
                    )
                row = part * lanes + tile * HARMONICS
                heights[row : row + HARMONICS, spot] = height
                lifted[row : row + HARMONICS, spot] = feature * height
        products = [
            axes_ref[first_axis, m : m + 1, spot] * axes_ref[second_axis, :, spot]
            for first_axis, second_axis in ((0, 2), (0, 3), (1, 2), (1, 3))
            for m in range(KMAX + 1)
        ]
        for pair in range(len(products) // 2):
            both = jnp.concatenate(products[2 * pair : 2 * pair + 2], axis=0)
            high = both.astype(BF16)
            rows = slice(2 * HARMONICS * pair, 2 * HARMONICS * (pair + 1))
            planes_ref[rows, spot] = high
            rows = slice(count + rows.start, count + rows.stop)
            planes_ref[rows, spot] = (both - high.astype(F32)).astype(BF16)


def wave_sums(own_channels, recv_ref, planes_ref, axes_ref, heights, lifted):
    chunk, _, atom_count = recv_ref.shape
    lanes = lifted.shape[0] // 2
    group = math.gcd(chunk, 16)
    count = planes_ref.shape[0] // 2
    total = 0.0
    for first in range(0, chunk, group):
        devices = range(first, first + group)
        wave_planes(own_channels, recv_ref, planes_ref, axes_ref, heights, lifted, devices)
        spot = slice(first * atom_count, (first + group) * atom_count)
        values = lifted[:, spot]
        high = values.astype(BF16)
        low = (values - high.astype(F32)).astype(BF16)
        main = dot(planes_ref[0:count, spot], jnp.concatenate([high, low], axis=0), 1, 1)
        total = total + main[:, : 2 * lanes] + (main[:, 2 * lanes :] + dot(planes_ref[count:, spot], high, 1, 1))
    return total


SIGNS = ((1.0, 1.0), (1.0, -1.0), (-1.0, 1.0), (-1.0, -1.0))


def wave_blocks(sums_ref, phi_ref):
    _, rows, lanes = phi_ref.shape
    sums = sums_ref[...]
    cos_part, sin_part = sums[:, :lanes], sums[:, lanes:]
    cc_c, cs_c, sc_c, ss_c = (cos_part[p * rows : (p + 1) * rows] for p in range(4))
    cc_s, cs_s, sc_s, ss_s = (sin_part[p * rows : (p + 1) * rows] for p in range(4))
    for sign_id, (s1, s2) in enumerate(SIGNS):
        real = cc_c - s1 * s2 * ss_c - s1 * sc_s - s2 * cs_s
        imag = cc_s - s1 * s2 * ss_s + s1 * sc_c + s2 * cs_c
        phi = phi_ref[sign_id]
        yield s1, s2, phi * real, phi * imag, real, imag


def wave_virial(own_channels, lengths, sums_ref, phi_ref, width_ref, shape):
    _, rows, lanes = phi_ref.shape
    even = first_odd = second_odd = both_odd = jnp.zeros((rows, lanes), F32)
    for s1, s2, dreal, dimag, real, imag in wave_blocks(sums_ref, phi_ref):
        power = dreal * real + dimag * imag
        even = even + power
        first_odd = first_odd + s1 * power
        second_odd = second_odd + s2 * power
        both_odd = both_odd + s1 * s2 * power
    width = width_ref[0:1, :]
    k1, k2, k3 = grid_numbers(rows, lanes, own_channels, lengths)

    def total_of(values):
        return jnp.sum(jnp.sum(values, axis=0, keepdims=True), axis=1, keepdims=True)

    energy = 0.5 * total_of(even)
    scaled = width * even
    terms = {
        (0, 0): energy - total_of(k1 * k1 * scaled),
        (1, 1): energy - total_of(k2 * k2 * scaled),
        (2, 2): energy - total_of(k3 * k3 * scaled),
        (0, 1): -total_of(k1 * k2 * width * both_odd),
        (0, 2): -total_of(k1 * k3 * width * first_odd),
        (1, 2): -total_of(k2 * k3 * width * second_odd),
    }
    return virial_row(terms, shape)


def wave_coefficients(sums_ref, phi_ref, coefficients_ref):
    _, rows, lanes = phi_ref.shape
    zero = jnp.zeros((rows, lanes), F32)
    d_cc_c = d_cc_s = d_cs_c = d_cs_s = d_sc_c = d_sc_s = d_ss_c = d_ss_s = zero
    for s1, s2, dreal, dimag, _, _ in wave_blocks(sums_ref, phi_ref):
        d_cc_c, d_ss_c = d_cc_c + dreal, d_ss_c - s1 * s2 * dreal
        d_sc_s, d_cs_s = d_sc_s - s1 * dreal, d_cs_s - s2 * dreal
        d_cc_s, d_ss_s = d_cc_s + dimag, d_ss_s - s1 * s2 * dimag
        d_sc_c, d_cs_c = d_sc_c + s1 * dimag, d_cs_c + s2 * dimag
    values = jnp.concatenate(
        [
            jnp.concatenate(pair, axis=1)
            for pair in ((d_cc_c, d_cc_s), (d_cs_c, d_cs_s), (d_sc_c, d_sc_s), (d_ss_c, d_ss_s))
        ],
        axis=0,
    )
    cc, cs, sc, ss = (values[p * rows : (p + 1) * rows] for p in range(4))
    row_id = lax.broadcasted_iota(jnp.int32, (rows, 2 * lanes), 0)
    m1 = (row_id // HARMONICS).astype(F32)
    m2 = (row_id % HARMONICS).astype(F32)
    along_x = jnp.concatenate([m1 * sc, m1 * ss, -m1 * cc, -m1 * cs], axis=0)
    along_y = jnp.concatenate([m2 * cs, -m2 * cc, m2 * ss, -m2 * sc], axis=0)
    values = jnp.concatenate([values, along_x, along_y], axis=1)
    turned = values.T
    high = turned.astype(BF16)
    count = turned.shape[0]
    coefficients_ref[0:count, :] = high
    coefficients_ref[count:, :] = (turned - high.astype(F32)).astype(BF16)


def wave_spread(planes_ref, coefficients):
    values = coefficients[...]
    count = values.shape[0] // 2
    both = jnp.concatenate([values[:count], values[:count]], axis=1)
    return dot(both, planes_ref[...], 1, 0) + dot(values[count:], planes_ref[0 : values.shape[1], :], 1, 0)


def wave_back(own_channels, lengths, planes_ref, heights, lifted, coefficients, send_ref, push_ref):
    chunk, _, atom_count = push_ref.shape
    together, tiles = tile_layout(own_channels)
    lanes = tiles * HARMONICS
    sublane = lax.broadcasted_iota(jnp.int32, (HARMONICS, atom_count), 0)
    numbers = [(sublane // own_channels + 1 + tile * together).astype(F32) for tile in range(tiles)]
    result = wave_spread(planes_ref, coefficients)
    for index in range(chunk):
        spot = slice(index * atom_count, (index + 1) * atom_count)
        part = result[:, spot]
        feature = grad_x = grad_y = grad_z = jnp.zeros((HARMONICS, atom_count), F32)
        for tile in range(tiles):
            a, b = tile * HARMONICS, lanes + tile * HARMONICS
            on_cos, on_sin = part[a : a + HARMONICS], part[b : b + HARMONICS]
            feature = feature + on_cos * heights[a : a + HARMONICS, spot] + on_sin * heights[b : b + HARMONICS, spot]
            lift_cos = lifted[a : a + HARMONICS, spot]
            lift_sin = lifted[b : b + HARMONICS, spot]
            grad_z = grad_z + numbers[tile] * (on_sin * lift_cos - on_cos * lift_sin)
            a, b = a + 2 * lanes, b + 2 * lanes
            grad_x = grad_x + part[a : a + HARMONICS] * lift_cos + part[b : b + HARMONICS] * lift_sin
            a, b = a + 2 * lanes, b + 2 * lanes
            grad_y = grad_y + part[a : a + HARMONICS] * lift_cos + part[b : b + HARMONICS] * lift_sin
        total = feature[0:own_channels]
        for n in range(1, together):
            total = total + feature[n * own_channels : (n + 1) * own_channels]
        send_ref[index, 0:own_channels, :] = total
        pieces = (
            grad_x * (2.0 * math.pi / lengths[0]),
            grad_y * (2.0 * math.pi / lengths[1]),
            grad_z * (2.0 * math.pi / lengths[2]),
        )
        for row, piece in enumerate(pieces):
            push_ref[index, row : row + 1, :] = jnp.sum(piece, axis=0, keepdims=True)


def virial_row(terms, shape):
    lane = lax.broadcasted_iota(jnp.int32, shape, 1)
    row = jnp.zeros(shape, F32)
    for (i, j), value in terms.items():
        spots = (lane == 3 * i + j) | (lane == 3 * j + i)
        row = jnp.where(spots, value, row)
    return row


def short_back_kernel(
    dims,
    recv_ref,
    vec_ref,
    kind_ref,
    dupd_ref,
    slope_ref,
    owner_ref,
    back_ref,
    push_ref,
    send_ref,
    fgrad,
    dpool,
    parts,
):
    own_channels, row_count, col_count, species_count, radial_count = dims
    slot_count, atom_count = owner_ref.shape
    channel_count = back_ref.shape[1]
    device_count = send_ref.shape[0]
    table_rows = round_up(len(DIRECTIONS) + 1, 16)
    for q in range(own_channels):
        low, high = q * device_count, min(channel_count, (q + 1) * device_count)
        fgrad[low:high, :] = recv_ref[0 : high - low, q, :]
    dbefore = (fgrad[...] + dupd_ref[...]) * slope_ref[...]
    dpool[...] = dot(back_ref[...], dbefore, 1, 0, GOOD)
    vectors = [vec_ref[part] for part in range(3)]
    squared = vectors[0] * vectors[0] + vectors[1] * vectors[1] + vectors[2] * vectors[2]
    kind = kind_ref[...]
    sums = [jnp.zeros(kind.shape, F32) for _ in range(species_count)]
    for order in range(radial_count):
        basis = jnp.exp(squared * (-radial_rate(order)))
        for k in range(species_count):
            spot = k * radial_count + order
            sums[k] = sums[k] + basis * dpool[spot : spot + 1, :]
    slope = jnp.zeros(kind.shape, F32)
    for k in range(species_count):
        slope = jnp.where(kind == float(k), sums[k], slope)
    grads = [slope * vector for vector in vectors]

    def total_of(values):
        return jnp.sum(jnp.sum(values, axis=0, keepdims=True), axis=1, keepdims=True)

    terms = {
        (i, j): -total_of(grads[i] * vectors[j]) for i in range(3) for j in range(i, 3)
    }
    virial = virial_row(terms, (1, atom_count))
    for part in range(3):
        parts[2 * part], parts[2 * part + 1] = split(grads[part])

    sublane = lax.broadcasted_iota(jnp.int32, (atom_count, atom_count), 0)
    table_id = lax.broadcasted_iota(jnp.int32, (table_rows, atom_count), 0)
    group = 8
    scattered = jnp.zeros((atom_count, 6 * table_rows), F32)
    for low in range(0, slot_count, group):
        hots, columns = [], []
        for s in range(low, low + group):
            ids = owner_ref[s : s + 1, :]
            hots.append(jnp.where(sublane == (ids & (atom_count - 1)), 1.0, 0.0).astype(BF16))
            mine = table_id == ids // atom_count
            columns.append(
                jnp.concatenate(
                    [
                        jnp.where(mine, parts[p, s : s + 1, :], 0.0).astype(BF16)
                        for p in range(6)
                    ],
                    axis=0,
                )
            )
        scattered = scattered + dot(
            jnp.concatenate(hots, axis=1), jnp.concatenate(columns, axis=1), 1, 1
        )
    rows = scattered.T
    send_ref[...] = push_ref[...]
    send_ref[:, 3, :] += jnp.broadcast_to(virial, (device_count, atom_count))
    me = neighbour_of((0, 0), row_count, col_count)
    for part in range(3):
        low = 2 * part * table_rows
        both = rows[low : low + table_rows] + rows[low + table_rows : low + 2 * table_rows]
        send_ref[me, part, :] += both[0, :] - jnp.sum(grads[part], axis=0)
        for order, step in enumerate(DIRECTIONS):
            target = neighbour_of(step, row_count, col_count)
            send_ref[target, part, :] += both[1 + order, :]


def final_kernel(volume, recv_ref, forces_ref, virial_ref):
    total = jnp.sum(recv_ref[...], axis=0)
    for part in range(3):
        forces_ref[part] = -total[part : part + 1, :]
    virial = total[3:4, :] * (1.0 / volume)
    for i in range(3):
        virial_ref[i : i + 1, :] = virial[:, 3 * i : 3 * i + 3]


def per_device(
    positions,
    species,
    counts,
    neighbours,
    ghost_index,
    wave_numbers,
    embedding,
    w_radial,
    w_mix,
    w_read,
    w_out,
    amplitude,
    kernel_width,
    filter_gain,
):
    row_count = lax.axis_size("row")
    col_count = lax.axis_size("col")
    device_count = row_count * col_count
    atom_count = positions.shape[3]
    slot_count = neighbours.shape[2]
    direction_count, ghost_count = ghost_index.shape[2:]
    species_count, channel_count = embedding.shape
    radial_count = w_radial.shape[0]
    own_channels = -(-channel_count // device_count)
    lengths = (CELL_EDGE * row_count, CELL_EDGE * col_count, HEIGHT)
    volume = lengths[0] * lengths[1] * lengths[2]
    rows = (KMAX + 1) * HARMONICS
    lanes = tile_layout(own_channels)[1] * HARMONICS
    _, shared = direction_slots(row_count, col_count)
    slab_first = round_up(4 + shared, 2) // 2 * atom_count
    slab_features = round_up(own_channels, 4)
    chunk = math.gcd(device_count, 32)
    chunk_count = device_count // chunk

    def exchange(slabs):
        return lax.all_to_all(slabs, AXES, 0, 0, tiled=True)

    def shape(*dims):
        return jax.ShapeDtypeStruct(dims, F32)

    def scratch(*dims):
        return pltpu.VMEM(dims, F32)

    def call(kernel, out_shape, vmem=16, **options):
        return pl.pallas_call(
            kernel,
            out_shape=out_shape,
            compiler_params=pltpu.CompilerParams(vmem_limit_bytes=vmem * 1024 * 1024),
            **options,
        )

    ids = neighbours.reshape(slot_count, atom_count)
    ghosts = ghost_index.reshape(direction_count, ghost_count)
    mesh_counts = (row_count, col_count)
    inputs = (
        counts.reshape(1, atom_count),
        ids,
        w_radial,
        embedding,
        w_mix,
    )
    wave_inputs = (
        w_read,
        w_out.reshape(1, -1),
        filter_gain,
        wave_numbers,
        amplitude.reshape(1, -1),
        kernel_width.reshape(1, -1),
    )

    def fetched(*arrays):
        return [pltpu.with_memory_space_constraint(x, pltpu.HBM) for x in arrays]

    kept = pl.BlockSpec(memory_space=pltpu.HBM)
    near = pl.BlockSpec(memory_space=pltpu.VMEM)
    send, *inputs = call(
        functools.partial(pack_kernel, mesh_counts, len(inputs)),
        (shape(device_count, 2, slab_first),)
        + tuple(jax.ShapeDtypeStruct(x.shape, x.dtype) for x in inputs),
        in_specs=[kept] * (3 + len(inputs)),
        scratch_shapes=[
            scratch(3, 1, atom_count),
            pltpu.VMEM((1, atom_count), jnp.int32),
            pltpu.VMEM(ghosts.shape, jnp.int32),
            pltpu.SemaphoreType.DMA((3,)),
            pltpu.SemaphoreType.DMA((len(inputs),)),
        ],
        name="pack",
    )(*fetched(positions.reshape(3, 1, atom_count), species.reshape(1, atom_count), ghosts, *inputs))
    live, ids, w_radial, embedding, w_mix = inputs
    cells = exchange(send)

    pooled_rows = species_count * radial_count
    send, vectors, kinds, owners, updated, slope, mixed = call(
        functools.partial(short_forward_kernel, (own_channels,) + mesh_counts),
        (
            shape(device_count, slab_features, atom_count),
            shape(3, slot_count, atom_count),
            shape(slot_count, atom_count),
            jax.ShapeDtypeStruct((slot_count, atom_count), jnp.int32),
            shape(channel_count, atom_count),
            shape(channel_count, atom_count),
            shape(pooled_rows, channel_count),
        ),
        scratch_shapes=[
            scratch(4, 16, atom_count),
            pltpu.VMEM((direction_count, atom_count), jnp.int32),
            pltpu.VMEM((16, atom_count), jnp.int32),
            scratch(pooled_rows, atom_count),
            scratch(pooled_rows, channel_count),
            scratch(round_up(species_count, 8), channel_count),
        ],
        name="short_forward",
    )(cells, live, ids, w_radial, embedding, w_mix)
    send, cells, updated, mixed = lax.optimization_barrier((send, cells, updated, mixed))
    features = exchange(send)

    axes_block = (6, HARMONICS, chunk * atom_count)
    axes_shape = shape(6, HARMONICS, device_count * atom_count)
    table_dims = (col_count, chunk_count, lengths)
    cells_inputs, axes_outputs = (), ()
    if chunk_count == 1:
        cells_inputs, axes_outputs = (cells,), (axes_shape,)
    dupd, back, phi, width, *axes = call(
        functools.partial(
            weights_kernel,
            (device_count, channel_count, own_channels, lengths, volume, radial_count),
            table_dims if chunk_count == 1 else None,
        ),
        (
            shape(channel_count, atom_count),
            shape(pooled_rows, channel_count),
            shape(4, rows, lanes),
            shape(8, lanes),
        )
        + axes_outputs,
        in_specs=[near] * (2 + len(cells_inputs)) + [kept] * len(wave_inputs),
        scratch_shapes=[pltpu.VMEM(x.shape, x.dtype) for x in wave_inputs]
        + [pltpu.SemaphoreType.DMA((len(wave_inputs),))],
        cost_estimate=pl.CostEstimate(
            flops=2 * 4 * rows * filter_gain.shape[0] * 3 * lanes,
            bytes_accessed=4 * filter_gain.size,
            transcendentals=0,
        ),
        name="weights",
    )(updated, mixed, *cells_inputs, *fetched(*wave_inputs))
    if chunk_count > 1:
        axes = [
            call(
                functools.partial(table_kernel, table_dims),
                axes_shape,
                grid=(chunk_count,),
                in_specs=[pl.BlockSpec((chunk, 2, slab_first), lambda i: (i, 0, 0))],
                out_specs=pl.BlockSpec(axes_block, lambda i: (0, 0, i)),
                name="tables",
            )(cells)
        ]
    features, dupd, back = lax.optimization_barrier((features, dupd, back))

    plane = pltpu.VMEM((8 * rows, chunk * atom_count), BF16)
    wave_scratch = [plane] + [scratch(2 * lanes, chunk * atom_count)] * 2
    features_block = (chunk, slab_features, atom_count)
    wave_options = {}
    if chunk_count > 1:
        wave_options = dict(
            grid=(2, chunk_count),
            in_specs=[
                pl.BlockSpec(features_block, lambda p, i: (i, 0, 0)),
                pl.BlockSpec(axes_block, lambda p, i: (0, 0, i)),
                pl.BlockSpec((4, rows, lanes), lambda p, i: (0, 0, 0)),
                pl.BlockSpec((8, lanes), lambda p, i: (0, 0)),
            ],
            out_specs=(
                pl.BlockSpec(features_block, lambda p, i: (i * p, 0, 0)),
                pl.BlockSpec((chunk, 4, atom_count), lambda p, i: (i * p, 0, 0)),
            ),
        )
    send, push = call(
        functools.partial(wave_kernel, (own_channels, chunk_count, lengths)),
        (shape(device_count, slab_features, atom_count), shape(device_count, 4, atom_count)),
        vmem=32,
        scratch_shapes=wave_scratch
        + [scratch(4 * rows, 2 * lanes), pltpu.VMEM((12 * lanes, 4 * rows), BF16)],
        name="waves",
        **wave_options,
    )(features, *axes, phi, width)
    gradients = exchange(send)

    send = call(
        functools.partial(
            short_back_kernel, (own_channels,) + mesh_counts + (species_count, radial_count)
        ),
        shape(device_count, 4, atom_count),
        scratch_shapes=[
            scratch(channel_count, atom_count),
            scratch(pooled_rows, atom_count),
            scratch(6, slot_count, atom_count),
        ],
        name="short_back",
    )(gradients, vectors, kinds, dupd, slope, owners, back, push)
    returned = exchange(send)

    forces, virial = call(
        functools.partial(final_kernel, volume),
        (shape(3, 1, atom_count), shape(3, 3)),
        name="total",
    )(returned)
    return (forces[:, None], virial)


def solution(mesh):
    return jax.shard_map(
        per_device,
        mesh=mesh,
        in_specs=(
            P(None, "row", "col", None),
            P("row", "col", None),
            P("row", "col", None),
            P("row", "col", None, None),
            P("row", "col", None, None),
            P(),
            P(),
            P(),
            P(),
            P(),
            P(),
            P(),
            P(),
            P(),
        ),
        out_specs=(P(None, "row", "col", None), P()),
        check_vma=False,
    )
```

```python
import functools
import math

import jax
import jax.numpy as jnp
from jax import lax
from jax.experimental import pallas as pl
from jax.experimental.pallas import tpu as pltpu
from jax.sharding import PartitionSpec as P

CELL_EDGE = 12.0
HEIGHT = 36.0
KMAX = 6
HARMONICS = 8
EXACT = lax.Precision.HIGHEST
GOOD = lax.Precision.HIGH
DIRECTIONS = ((-1, -1), (-1, 0), (-1, 1), (0, -1), (0, 1), (1, -1), (1, 0), (1, 1))
F32 = jnp.float32
BF16 = jnp.bfloat16
AXES = ("row", "col")


def radial_rate(order):
    return 0.003 * 1.6**order


def round_up(value, step):
    return -(-value // step) * step


def direction_slots(row_count, col_count):
    seen = {}
    slots = []
    for row_step, col_step in DIRECTIONS:
        key = (row_step % row_count, col_step % col_count)
        slots.append(seen.get(key, 0))
        seen[key] = slots[-1] + 1
    return slots, max(seen.values())


def tile_layout(own_channels):
    shared = HARMONICS // own_channels
    return shared, -(-KMAX // shared)


def dot(lhs, rhs, lhs_dim, rhs_dim, precision=None):
    return lax.dot_general(
        lhs,
        rhs,
        (((lhs_dim,), (rhs_dim,)), ((), ())),
        precision=precision,
        preferred_element_type=F32,
    )


def split(values):
    high = values.astype(BF16).astype(F32)
    return high, values - high


def wave_weights(dims, gain_ref, waves_ref, amp_ref, width_ref, phi_ref, width_out_ref):
    device_count, channel_count, own_channels, lengths, volume = dims
    me = lax.axis_index("row") * lax.axis_size("col") + lax.axis_index("col")
    wave_count = gain_ref.shape[0]
    rows = (KMAX + 1) * HARMONICS
    together, tiles = tile_layout(own_channels)
    lanes = tiles * HARMONICS
    place = lax.broadcasted_iota(jnp.int32, (8, channel_count), 0) * device_count + me
    chosen = (lax.broadcasted_iota(jnp.int32, (8, channel_count), 1) == place).astype(F32).astype(BF16)
    first, second, third = waves_ref[0:1, :], waves_ref[1:2, :], waves_ref[2:3, :]
    sign = jnp.where(first < 0, 2, 0) + jnp.where(second < 0, 1, 0)
    key = sign * rows + jnp.abs(first) * HARMONICS + jnp.abs(second)
    spots = lax.broadcasted_iota(jnp.int32, (4 * rows, wave_count), 0) == key
    onehot = jnp.where(spots, 1.0, 0.0).astype(BF16)
    height = lax.broadcasted_iota(jnp.int32, (HARMONICS, wave_count), 0) // own_channels + 1
    here = [height + tile * together == third for tile in range(tiles)]
    rest = gain_ref[...]
    summed = 0.0
    for _ in range(3):
        part = rest.astype(BF16)
        rest = rest - part.astype(F32)
        mine = dot(chosen, part, 1, 1)
        mine = jnp.concatenate([mine[:own_channels]] * together, axis=0)
        wide = jnp.concatenate([jnp.where(spots, mine, 0.0) for spots in here], axis=0)
        summed = summed + dot(onehot, wide.astype(BF16), 1, 1)
    lane = lax.broadcasted_iota(jnp.int32, (8, channel_count), 1)
    wanted = jnp.minimum(lane % own_channels * device_count + me, channel_count - 1)
    amp = jnp.take_along_axis(jnp.broadcast_to(amp_ref[...], (8, channel_count)), wanted, axis=1)
    width = jnp.take_along_axis(
        jnp.broadcast_to(width_ref[...], (8, channel_count)), wanted, axis=1
    )
    amp, width = amp[0:1, :lanes], width[0:1, :lanes]
    k1, k2, k3 = grid_numbers(rows, lanes, own_channels, lengths)
    squared = k1 * k1 + k2 * k2 + k3 * k3
    base = amp * jnp.exp(-width * squared) * (1.0 / volume)
    for sign_id in range(4):
        phi_ref[sign_id] = base * summed[sign_id * rows : (sign_id + 1) * rows, :]
    width_out_ref[...] = jnp.broadcast_to(width, (8, lanes))


def grid_numbers(rows, lanes, own_channels, lengths):
    row_id = lax.broadcasted_iota(jnp.int32, (rows, lanes), 0)
    lane_id = lax.broadcasted_iota(jnp.int32, (rows, lanes), 1)
    k1 = (row_id // HARMONICS).astype(F32) * (2.0 * math.pi / lengths[0])
    k2 = (row_id % HARMONICS).astype(F32) * (2.0 * math.pi / lengths[1])
    k3 = (lane_id // own_channels + 1).astype(F32) * (2.0 * math.pi / lengths[2])
    return k1, k2, k3


def neighbour_of(step, row_count, col_count):
    row = lax.rem(lax.axis_index("row") + step[0] + row_count, row_count)
    col = lax.rem(lax.axis_index("col") + step[1] + col_count, col_count)
    return row * col_count + col


def slab_rows(slab, rows, atom_count):
    width = slab.shape[-1] // atom_count
    return [
        slab[row // width : row // width + 1, row % width * atom_count : (row % width + 1) * atom_count]
        for row in rows
    ]


def pack_kernel(counts, copied, positions_ref, species_ref, ghosts_ref, *refs):
    row_count, col_count = counts
    sources, (send_ref, *targets) = refs[:copied], refs[copied : 2 * copied + 1]
    positions, species, ghosts, first_sems, sems = refs[2 * copied + 1 :]
    firsts = ((positions_ref, positions), (species_ref, species), (ghosts_ref, ghosts))
    firsts = start_copies(firsts, first_sems)
    others = start_copies(tuple(zip(sources, targets)), sems)
    device_count = send_ref.shape[0]
    atom_count = species.shape[1]
    width = send_ref.shape[2] // atom_count
    slots, _ = direction_slots(row_count, col_count)
    for copy in firsts:
        copy.wait()
    rows = [positions[0], positions[1], positions[2], species[...].astype(F32)]
    for row, values in enumerate(rows):
        low = row % width * atom_count
        send_ref[:, row // width, low : low + atom_count] = jnp.broadcast_to(
            values, (device_count, atom_count)
        )
    for order, step in enumerate(DIRECTIONS):
        target = neighbour_of(step, row_count, col_count)
        row = 4 + slots[order]
        low = row % width * atom_count
        send_ref[target, row // width, low : low + atom_count] = ghosts[order, :].astype(F32)
    for copy in others:
        copy.wait()


def start_copies(pairs, sems):
    copies = [
        pltpu.make_async_copy(source, target, sems.at[spot])
        for spot, (source, target) in enumerate(pairs)
    ]
    for copy in copies:
        copy.start()
    return copies


def weights_kernel(dims, table_dims, upd_ref, mixed_ref, *refs):
    cells, refs = refs[: bool(table_dims)], refs[bool(table_dims) :]
    sources, (dupd_ref, back_ref, phi_ref, width_out_ref), refs = refs[:6], refs[6:10], refs[10:]
    axes, targets, sems = refs[: len(refs) - 7], refs[-7:-1], refs[-1]
    copies = start_copies(tuple(zip(sources, targets)), sems)
    if table_dims:
        table_kernel(table_dims, *cells, axes[0])
        if len(axes) > 1:
            wave_planes(axes[1], axes[0], range(axes[1].shape[1] // upd_ref.shape[1]))
    pooled_rows, channel_count = mixed_ref.shape
    radial_count = dims[5]
    order_id = lax.broadcasted_iota(jnp.int32, (pooled_rows, channel_count), 0) % radial_count
    factor = jnp.zeros((pooled_rows, channel_count), F32)
    for order in range(radial_count):
        factor = jnp.where(order_id == order, -2.0 * radial_rate(order), factor)
    back_ref[...] = mixed_ref[...] * factor
    for copy in copies[:2]:
        copy.wait()
    readout_gradient(upd_ref, targets[0], targets[1], dupd_ref)
    for copy in copies[2:]:
        copy.wait()
    wave_weights(dims[:5], *targets[2:], phi_ref, width_out_ref)


def short_forward_kernel(
    dims,
    cells_ref,
    counts_ref,
    ids_ref,
    radial_ref,
    embed_ref,
    mix_ref,
    send_ref,
    vec_ref,
    kind_ref,
    owner_ref,
    upd_ref,
    slope_ref,
    mixed_ref,
    table,
    lists,
    codes,
    pooled,
    weights,
    kinds8,
):
    own_channels, row_count, col_count = dims
    slot_count, atom_count = ids_ref.shape
    species_count, channel_count = embed_ref.shape
    radial_count = radial_ref.shape[0]
    device_count = send_ref.shape[0]
    slots, _ = direction_slots(row_count, col_count)
    for k in range(species_count):
        weights[k * radial_count : (k + 1) * radial_count, :] = (
            radial_ref[...] * embed_ref[k : k + 1, :] * (1.0 / slot_count)
        )
    weights[...] = dot(weights[...], mix_ref[...], 1, 0, EXACT)
    mixed_ref[...] = weights[...]
    own = slab_rows(cells_ref[neighbour_of((0, 0), row_count, col_count)], range(4), atom_count)
    domains, places = [], []
    for step in DIRECTIONS:
        key = (step[0] % row_count, step[1] % col_count)
        if key not in domains:
            domains.append(key)
        places.append(domains.index(key))
    for part in range(3):
        table[part, 0:1, :] = own[part]
    for place, key in enumerate(domains):
        block = slab_rows(cells_ref[neighbour_of(key, row_count, col_count)], range(3), atom_count)
        for part in range(3):
            table[part, 8 + place : 9 + place, :] = block[part]
    for order, step in enumerate(DIRECTIONS):
        list_row = 4 + slots[len(DIRECTIONS) - 1 - order]
        source = neighbour_of(step, row_count, col_count)
        kinds_row, list_values = slab_rows(cells_ref[source], (3, list_row), atom_count)
        table[3, 8 + order : 9 + order, :] = kinds_row
        lists[order : order + 1, :] = list_values.astype(jnp.int32)
    picks = lists[...]
    ghost_kinds = jnp.take_along_axis(table[3, 8:16, :], picks, axis=1)
    codes[8:16, :] = picks + atom_count * ghost_kinds.astype(jnp.int32)
    codes[0:1, :] = lax.broadcasted_iota(
        jnp.int32, (1, atom_count), 1
    ) + atom_count * own[3].astype(jnp.int32)

    ids = ids_ref[...]
    lane = ids & (atom_count - 1)
    source = ids // atom_count

    def picked(ref, index, marks):
        values = jnp.take_along_axis(jnp.broadcast_to(ref[0:1, :], ids.shape), index, axis=1)
        for place, mark in enumerate(marks):
            wide = jnp.broadcast_to(ref[8 + place : 9 + place, :], ids.shape)
            values = jnp.where(mark, jnp.take_along_axis(wide, index, axis=1), values)
        return values

    marks = [source == order + 1 for order in range(len(DIRECTIONS))]
    code = picked(codes, lane, marks)
    owner = code & (atom_count - 1)
    owner_ref[...] = owner + source * atom_count
    merged = []
    for place in range(len(domains)):
        mine = [mark for mark, other in zip(marks, places) if other == place]
        merged.append(functools.reduce(jnp.logical_or, mine))
    gathered = [picked(table.at[part], owner, merged) for part in range(3)]
    for axis in range(2):
        shift = jnp.zeros(ids.shape, F32)
        for mark, step in zip(marks, DIRECTIONS):
            if step[axis]:
                shift = jnp.where(mark, step[axis] * CELL_EDGE, shift)
        gathered[axis] = gathered[axis] + shift
    gathered.append((code // atom_count).astype(F32))
    slot = lax.broadcasted_iota(jnp.int32, ids.shape, 0)
    kind = jnp.where(slot < counts_ref[...], gathered[3], -1.0)
    kind_ref[...] = kind
    squared = jnp.zeros(ids.shape, F32)
    for part in range(3):
        vector = gathered[part] - own[part]
        vec_ref[part] = vector
        squared = squared + vector * vector
    masks = [kind == float(k) for k in range(species_count)]
    for order in range(radial_count):
        basis = jnp.exp(squared * (-radial_rate(order)))
        for k in range(species_count):
            spot = k * radial_count + order
            pooled[spot : spot + 1, :] = jnp.sum(
                jnp.where(masks[k], basis, 0.0), axis=0, keepdims=True
            )
    kinds8[...] = jnp.zeros_like(kinds8)
    kinds8[0:species_count, :] = embed_ref[...]
    own_hot = (
        lax.broadcasted_iota(jnp.int32, (kinds8.shape[0], atom_count), 0).astype(F32) == own[3]
    ).astype(F32)
    initial = dot(kinds8[...], own_hot, 0, 0, EXACT)
    before = dot(weights[...], pooled[...], 0, 0, GOOD)
    gate = 1.0 / (1.0 + jnp.exp(-before))
    updated = initial + before * gate
    slope_ref[...] = gate + before * gate * (1.0 - gate)
    for q in range(own_channels):
        low, high = q * device_count, min(channel_count, (q + 1) * device_count)
        send_ref[0 : high - low, q, :] = updated[low:high, :]
        if high - low < device_count:
            send_ref[high - low :, q, :] = jnp.zeros(
                (device_count - (high - low), atom_count), F32
            )
    upd_ref[...] = updated


def readout_gradient(upd_ref, read_ref, out_ref, dupd_ref):
    channel_count, atom_count = upd_ref.shape
    readout = dot(read_ref[...], upd_ref[...], 0, 0, GOOD)
    gate = 1.0 / (1.0 + jnp.exp(-readout))
    scale = jnp.broadcast_to(out_ref[...], (channel_count, channel_count)).T
    dread = scale[:, 0:atom_count] * (gate + readout * gate * (1.0 - gate))
    dupd_ref[...] = dot(read_ref[...], dread, 1, 0, GOOD)


def turn_tables(turns, multiples):
    angle = turns * multiples
    halves = jnp.floor(2.0 * angle + 0.5)
    rest = angle - 0.5 * halves
    sign = 1.0 - 2.0 * (halves - 2.0 * jnp.floor(0.5 * halves))
    square = rest * rest

    def series(first, last):
        terms = [
            (-1.0) ** (p // 2) * (2.0 * math.pi) ** p / math.factorial(p)
            for p in range(first, last + 1, 2)
        ]
        total = jnp.full_like(square, terms[-1])
        for term in reversed(terms[:-1]):
            total = total * square + term
        return total

    return sign * series(0, 12), sign * rest * series(1, 13)


def table_kernel(dims, cells_ref, axes_ref):
    col_count, chunk_count, lengths = dims
    chunk = cells_ref.shape[0]
    atom_count = axes_ref.shape[2] // chunk
    first_device = pl.program_id(0) * chunk if chunk_count > 1 else 0
    multiples = lax.broadcasted_iota(jnp.int32, (HARMONICS, atom_count), 0).astype(F32)

    def one(index, _):
        device = first_device + index
        spot = pl.ds(pl.multiple_of(index * atom_count, atom_count), atom_count)
        block = slab_rows(cells_ref[index], range(3), atom_count)
        corner_row = (device // col_count).astype(F32) * CELL_EDGE
        corner_col = (device % col_count).astype(F32) * CELL_EDGE
        turns = (
            (block[0] + corner_row) * (1.0 / lengths[0]),
            (block[1] + corner_col) * (1.0 / lengths[1]),
            block[2] * (1.0 / lengths[2]),
        )
        for axis in range(3):
            numbers = multiples + 1.0 if axis == 2 else multiples
            cos, sin = turn_tables(turns[axis], numbers)
            axes_ref[2 * axis, :, spot] = cos
            axes_ref[2 * axis + 1, :, spot] = sin
        return 0

    lax.fori_loop(0, chunk, one, 0, unroll=4)


def wave_kernel(dims, recv_ref, axes_ref, phi_ref, width_ref, *refs):
    own_channels, chunk_count, lengths, ready = dims
    made, (send_ref, push_ref, *planes), (heights, lifted, sums, coefficients) = refs[:ready], refs[ready:-4], refs[-4:]
    planes = (*made, *planes)
    parts = (planes, ready, axes_ref, heights, lifted)

    def back():
        wave_back(own_channels, lengths, planes, heights, lifted, coefficients, send_ref, push_ref)
        virial = wave_virial(own_channels, lengths, sums, phi_ref, width_ref, (1, push_ref.shape[2]))
        push_ref[:, 3, :] = jnp.broadcast_to(virial, (push_ref.shape[0], push_ref.shape[2]))

    if chunk_count == 1:
        sums[...] = wave_sums(own_channels, recv_ref, *parts)
        wave_coefficients(sums, phi_ref, coefficients)
        back()
        return
    phase, chunk_id = pl.program_id(0), pl.program_id(1)

    @pl.when((phase == 0) & (chunk_id == 0))
    def _():
        sums[...] = jnp.zeros_like(sums)

    part = wave_sums(own_channels, recv_ref, *parts)

    @pl.when(phase == 0)
    def _():
        sums[...] += part

    @pl.when((phase == 1) & (chunk_id == 0))
    def _():
        wave_coefficients(sums, phi_ref, coefficients)

    @pl.when(phase == 1)
    def _():
        back()


def wave_planes(planes_ref, axes_ref, devices):
    atom_count = planes_ref.shape[1] // len(devices)
    count = planes_ref.shape[0] // 2
    for place, index in enumerate(devices):
        spot = slice(index * atom_count, (index + 1) * atom_count)
        target = slice(place * atom_count, (place + 1) * atom_count)
        products = [
            axes_ref[first_axis, m : m + 1, spot] * axes_ref[second_axis, :, spot]
            for first_axis, second_axis in ((0, 2), (0, 3), (1, 2), (1, 3))
            for m in range(KMAX + 1)
        ]
        for pair in range(len(products) // 2):
            both = jnp.concatenate(products[2 * pair : 2 * pair + 2], axis=0)
            high = both.astype(BF16)
            rows = slice(2 * HARMONICS * pair, 2 * HARMONICS * (pair + 1))
            planes_ref[rows, target] = high
            rows = slice(count + rows.start, count + rows.stop)
            planes_ref[rows, target] = (both - high.astype(F32)).astype(BF16)


def wave_lift(own_channels, recv_ref, axes_ref, heights, lifted, devices):
    atom_count = recv_ref.shape[2]
    together, tiles = tile_layout(own_channels)
    lanes = tiles * HARMONICS
    sublane = lax.broadcasted_iota(jnp.int32, (HARMONICS, atom_count), 0)
    for index in devices:
        spot = slice(index * atom_count, (index + 1) * atom_count)
        feature = jnp.concatenate([recv_ref[index, 0:own_channels, :]] * together, axis=0)
        for part in range(2):
            for tile in range(tiles):
                first = tile * together
                height = jnp.broadcast_to(axes_ref[4 + part, first : first + 1, spot], sublane.shape)
                for n in range(1, together):
                    height = jnp.where(
                        sublane >= n * own_channels, axes_ref[4 + part, first + n : first + n + 1, spot], height
                    )
                row = part * lanes + tile * HARMONICS
                heights[row : row + HARMONICS, spot] = height
                lifted[row : row + HARMONICS, spot] = feature * height


def plane_groups(chunk, planes):
    each = chunk // len(planes)
    return [(ref, range(place * each, (place + 1) * each)) for place, ref in enumerate(planes)]


def wave_sums(own_channels, recv_ref, planes, ready, axes_ref, heights, lifted):
    chunk, _, atom_count = recv_ref.shape
    lanes = lifted.shape[0] // 2
    total = 0.0
    for place, (ref, devices) in enumerate(plane_groups(chunk, planes)):
        wave_lift(own_channels, recv_ref, axes_ref, heights, lifted, devices)
        if place >= ready:
            wave_planes(ref, axes_ref, devices)
        count = ref.shape[0] // 2
        values = lifted[:, devices[0] * atom_count : (devices[-1] + 1) * atom_count]
        high = values.astype(BF16)
        low = (values - high.astype(F32)).astype(BF16)
        main = dot(ref[0:count, :], jnp.concatenate([high, low], axis=0), 1, 1)
        total = total + main[:, : 2 * lanes] + (main[:, 2 * lanes :] + dot(ref[count:, :], high, 1, 1))
    return total


SIGNS = ((1.0, 1.0), (1.0, -1.0), (-1.0, 1.0), (-1.0, -1.0))


def wave_blocks(sums_ref, phi_ref):
    _, rows, lanes = phi_ref.shape
    sums = sums_ref[...]
    cos_part, sin_part = sums[:, :lanes], sums[:, lanes:]
    cc_c, cs_c, sc_c, ss_c = (cos_part[p * rows : (p + 1) * rows] for p in range(4))
    cc_s, cs_s, sc_s, ss_s = (sin_part[p * rows : (p + 1) * rows] for p in range(4))
    for sign_id, (s1, s2) in enumerate(SIGNS):
        real = cc_c - s1 * s2 * ss_c - s1 * sc_s - s2 * cs_s
        imag = cc_s - s1 * s2 * ss_s + s1 * sc_c + s2 * cs_c
        phi = phi_ref[sign_id]
        yield s1, s2, phi * real, phi * imag, real, imag


def wave_virial(own_channels, lengths, sums_ref, phi_ref, width_ref, shape):
    _, rows, lanes = phi_ref.shape
    even = first_odd = second_odd = both_odd = jnp.zeros((rows, lanes), F32)
    for s1, s2, dreal, dimag, real, imag in wave_blocks(sums_ref, phi_ref):
        power = dreal * real + dimag * imag
        even = even + power
        first_odd = first_odd + s1 * power
        second_odd = second_odd + s2 * power
        both_odd = both_odd + s1 * s2 * power
    width = width_ref[0:1, :]
    k1, k2, k3 = grid_numbers(rows, lanes, own_channels, lengths)

    def total_of(values):
        return jnp.sum(jnp.sum(values, axis=0, keepdims=True), axis=1, keepdims=True)

    energy = 0.5 * total_of(even)
    scaled = width * even
    terms = {
        (0, 0): energy - total_of(k1 * k1 * scaled),
        (1, 1): energy - total_of(k2 * k2 * scaled),
        (2, 2): energy - total_of(k3 * k3 * scaled),
        (0, 1): -total_of(k1 * k2 * width * both_odd),
        (0, 2): -total_of(k1 * k3 * width * first_odd),
        (1, 2): -total_of(k2 * k3 * width * second_odd),
    }
    return virial_row(terms, shape)


def wave_coefficients(sums_ref, phi_ref, coefficients_ref):
    _, rows, lanes = phi_ref.shape
    zero = jnp.zeros((rows, lanes), F32)
    d_cc_c = d_cc_s = d_cs_c = d_cs_s = d_sc_c = d_sc_s = d_ss_c = d_ss_s = zero
    for s1, s2, dreal, dimag, _, _ in wave_blocks(sums_ref, phi_ref):
        d_cc_c, d_ss_c = d_cc_c + dreal, d_ss_c - s1 * s2 * dreal
        d_sc_s, d_cs_s = d_sc_s - s1 * dreal, d_cs_s - s2 * dreal
        d_cc_s, d_ss_s = d_cc_s + dimag, d_ss_s - s1 * s2 * dimag
        d_sc_c, d_cs_c = d_sc_c + s1 * dimag, d_cs_c + s2 * dimag
    values = jnp.concatenate(
        [
            jnp.concatenate(pair, axis=1)
            for pair in ((d_cc_c, d_cc_s), (d_cs_c, d_cs_s), (d_sc_c, d_sc_s), (d_ss_c, d_ss_s))
        ],
        axis=0,
    )
    cc, cs, sc, ss = (values[p * rows : (p + 1) * rows] for p in range(4))
    row_id = lax.broadcasted_iota(jnp.int32, (rows, 2 * lanes), 0)
    m1 = (row_id // HARMONICS).astype(F32)
    m2 = (row_id % HARMONICS).astype(F32)
    along_x = jnp.concatenate([m1 * sc, m1 * ss, -m1 * cc, -m1 * cs], axis=0)
    along_y = jnp.concatenate([m2 * cs, -m2 * cc, m2 * ss, -m2 * sc], axis=0)
    values = jnp.concatenate([values, along_x, along_y], axis=1)
    turned = values.T
    high = turned.astype(BF16)
    count = turned.shape[0]
    coefficients_ref[0:count, :] = high
    coefficients_ref[count:, :] = (turned - high.astype(F32)).astype(BF16)


def wave_spread(planes_ref, coefficients):
    values = coefficients[...]
    count = values.shape[0] // 2
    both = jnp.concatenate([values[:count], values[:count]], axis=1)
    return dot(both, planes_ref[...], 1, 0) + dot(values[count:], planes_ref[0 : values.shape[1], :], 1, 0)


def wave_back(own_channels, lengths, planes, heights, lifted, coefficients, send_ref, push_ref):
    chunk, _, atom_count = push_ref.shape
    together, tiles = tile_layout(own_channels)
    lanes = tiles * HARMONICS
    sublane = lax.broadcasted_iota(jnp.int32, (HARMONICS, atom_count), 0)
    numbers = [(sublane // own_channels + 1 + tile * together).astype(F32) for tile in range(tiles)]
    spread = []
    for ref, devices in plane_groups(chunk, planes):
        result = wave_spread(ref, coefficients)
        spread += [(result, place, index) for place, index in enumerate(devices)]
    for result, place, index in spread:
        spot = slice(index * atom_count, (index + 1) * atom_count)
        part = result[:, place * atom_count : (place + 1) * atom_count]
        feature = grad_x = grad_y = grad_z = jnp.zeros((HARMONICS, atom_count), F32)
        for tile in range(tiles):
            a, b = tile * HARMONICS, lanes + tile * HARMONICS
            on_cos, on_sin = part[a : a + HARMONICS], part[b : b + HARMONICS]
            feature = feature + on_cos * heights[a : a + HARMONICS, spot] + on_sin * heights[b : b + HARMONICS, spot]
            lift_cos = lifted[a : a + HARMONICS, spot]
            lift_sin = lifted[b : b + HARMONICS, spot]
            grad_z = grad_z + numbers[tile] * (on_sin * lift_cos - on_cos * lift_sin)
            a, b = a + 2 * lanes, b + 2 * lanes
            grad_x = grad_x + part[a : a + HARMONICS] * lift_cos + part[b : b + HARMONICS] * lift_sin
            a, b = a + 2 * lanes, b + 2 * lanes
            grad_y = grad_y + part[a : a + HARMONICS] * lift_cos + part[b : b + HARMONICS] * lift_sin
        total = feature[0:own_channels]
        for n in range(1, together):
            total = total + feature[n * own_channels : (n + 1) * own_channels]
        send_ref[index, 0:own_channels, :] = total
        pieces = (
            grad_x * (2.0 * math.pi / lengths[0]),
            grad_y * (2.0 * math.pi / lengths[1]),
            grad_z * (2.0 * math.pi / lengths[2]),
        )
        for row, piece in enumerate(pieces):
            push_ref[index, row : row + 1, :] = jnp.sum(piece, axis=0, keepdims=True)


def virial_row(terms, shape):
    lane = lax.broadcasted_iota(jnp.int32, shape, 1)
    row = jnp.zeros(shape, F32)
    for (i, j), value in terms.items():
        spots = (lane == 3 * i + j) | (lane == 3 * j + i)
        row = jnp.where(spots, value, row)
    return row


def short_back_kernel(
    dims,
    recv_ref,
    vec_ref,
    kind_ref,
    dupd_ref,
    slope_ref,
    owner_ref,
    back_ref,
    push_ref,
    send_ref,
    fgrad,
    dpool,
    parts,
):
    own_channels, row_count, col_count, species_count, radial_count = dims
    slot_count, atom_count = owner_ref.shape
    channel_count = back_ref.shape[1]
    device_count = send_ref.shape[0]
    table_rows = round_up(len(DIRECTIONS) + 1, 16)
    for q in range(own_channels):
        low, high = q * device_count, min(channel_count, (q + 1) * device_count)
        fgrad[low:high, :] = recv_ref[0 : high - low, q, :]
    dbefore = (fgrad[...] + dupd_ref[...]) * slope_ref[...]
    dpool[...] = dot(back_ref[...], dbefore, 1, 0, GOOD)
    vectors = [vec_ref[part] for part in range(3)]
    squared = vectors[0] * vectors[0] + vectors[1] * vectors[1] + vectors[2] * vectors[2]
    kind = kind_ref[...]
    sums = [jnp.zeros(kind.shape, F32) for _ in range(species_count)]
    for order in range(radial_count):
        basis = jnp.exp(squared * (-radial_rate(order)))
        for k in range(species_count):
            spot = k * radial_count + order
            sums[k] = sums[k] + basis * dpool[spot : spot + 1, :]
    slope = jnp.zeros(kind.shape, F32)
    for k in range(species_count):
        slope = jnp.where(kind == float(k), sums[k], slope)
    grads = [slope * vector for vector in vectors]

    def total_of(values):
        return jnp.sum(jnp.sum(values, axis=0, keepdims=True), axis=1, keepdims=True)

    terms = {
        (i, j): -total_of(grads[i] * vectors[j]) for i in range(3) for j in range(i, 3)
    }
    virial = virial_row(terms, (1, atom_count))
    for part in range(3):
        parts[2 * part], parts[2 * part + 1] = split(grads[part])

    sublane = lax.broadcasted_iota(jnp.int32, (atom_count, atom_count), 0)
    table_id = lax.broadcasted_iota(jnp.int32, (table_rows, atom_count), 0)
    group = 8
    scattered = jnp.zeros((atom_count, 6 * table_rows), F32)
    for low in range(0, slot_count, group):
        hots, columns = [], []
        for s in range(low, low + group):
            ids = owner_ref[s : s + 1, :]
            hots.append(jnp.where(sublane == (ids & (atom_count - 1)), 1.0, 0.0).astype(BF16))
            mine = table_id == ids // atom_count
            columns.append(
                jnp.concatenate(
                    [
                        jnp.where(mine, parts[p, s : s + 1, :], 0.0).astype(BF16)
                        for p in range(6)
                    ],
                    axis=0,
                )
            )
        scattered = scattered + dot(
            jnp.concatenate(hots, axis=1), jnp.concatenate(columns, axis=1), 1, 1
        )
    rows = scattered.T
    send_ref[...] = push_ref[...]
    send_ref[:, 3, :] += jnp.broadcast_to(virial, (device_count, atom_count))
    me = neighbour_of((0, 0), row_count, col_count)
    for part in range(3):
        low = 2 * part * table_rows
        both = rows[low : low + table_rows] + rows[low + table_rows : low + 2 * table_rows]
        send_ref[me, part, :] += both[0, :] - jnp.sum(grads[part], axis=0)
        for order, step in enumerate(DIRECTIONS):
            target = neighbour_of(step, row_count, col_count)
            send_ref[target, part, :] += both[1 + order, :]


def final_kernel(volume, recv_ref, forces_ref, virial_ref):
    total = jnp.sum(recv_ref[...], axis=0)
    for part in range(3):
        forces_ref[part] = -total[part : part + 1, :]
    virial = total[3:4, :] * (1.0 / volume)
    for i in range(3):
        virial_ref[i : i + 1, :] = virial[:, 3 * i : 3 * i + 3]


def per_device(
    positions,
    species,
    counts,
    neighbours,
    ghost_index,
    wave_numbers,
    embedding,
    w_radial,
    w_mix,
    w_read,
    w_out,
    amplitude,
    kernel_width,
    filter_gain,
):
    row_count = lax.axis_size("row")
    col_count = lax.axis_size("col")
    device_count = row_count * col_count
    atom_count = positions.shape[3]
    slot_count = neighbours.shape[2]
    direction_count, ghost_count = ghost_index.shape[2:]
    species_count, channel_count = embedding.shape
    radial_count = w_radial.shape[0]
    own_channels = -(-channel_count // device_count)
    lengths = (CELL_EDGE * row_count, CELL_EDGE * col_count, HEIGHT)
    volume = lengths[0] * lengths[1] * lengths[2]
    rows = (KMAX + 1) * HARMONICS
    lanes = tile_layout(own_channels)[1] * HARMONICS
    _, shared = direction_slots(row_count, col_count)
    slab_first = round_up(4 + shared, 2) // 2 * atom_count
    slab_features = round_up(own_channels, 4)
    chunk = math.gcd(device_count, 32)
    chunk_count = device_count // chunk

    def exchange(slabs):
        return lax.all_to_all(slabs, AXES, 0, 0, tiled=True)

    def shape(*dims):
        return jax.ShapeDtypeStruct(dims, F32)

    def scratch(*dims):
        return pltpu.VMEM(dims, F32)

    def call(kernel, out_shape, vmem=16, **options):
        return pl.pallas_call(
            kernel,
            out_shape=out_shape,
            compiler_params=pltpu.CompilerParams(vmem_limit_bytes=vmem * 1024 * 1024),
            **options,
        )

    ids = neighbours.reshape(slot_count, atom_count)
    ghosts = ghost_index.reshape(direction_count, ghost_count)
    mesh_counts = (row_count, col_count)
    inputs = (
        counts.reshape(1, atom_count),
        ids,
        w_radial,
        embedding,
        w_mix,
    )
    wave_inputs = (
        w_read,
        w_out.reshape(1, -1),
        filter_gain,
        wave_numbers,
        amplitude.reshape(1, -1),
        kernel_width.reshape(1, -1),
    )

    def fetched(*arrays):
        return [pltpu.with_memory_space_constraint(x, pltpu.HBM) for x in arrays]

    kept = pl.BlockSpec(memory_space=pltpu.HBM)
    near = pl.BlockSpec(memory_space=pltpu.VMEM)
    send, *inputs = call(
        functools.partial(pack_kernel, mesh_counts, len(inputs)),
        (shape(device_count, 2, slab_first),)
        + tuple(jax.ShapeDtypeStruct(x.shape, x.dtype) for x in inputs),
        in_specs=[kept] * (3 + len(inputs)),
        scratch_shapes=[
            scratch(3, 1, atom_count),
            pltpu.VMEM((1, atom_count), jnp.int32),
            pltpu.VMEM(ghosts.shape, jnp.int32),
            pltpu.SemaphoreType.DMA((3,)),
            pltpu.SemaphoreType.DMA((len(inputs),)),
        ],
        name="pack",
    )(*fetched(positions.reshape(3, 1, atom_count), species.reshape(1, atom_count), ghosts, *inputs))
    live, ids, w_radial, embedding, w_mix = inputs
    cells = exchange(send)

    pooled_rows = species_count * radial_count
    send, vectors, kinds, owners, updated, slope, mixed = call(
        functools.partial(short_forward_kernel, (own_channels,) + mesh_counts),
        (
            shape(device_count, slab_features, atom_count),
            shape(3, slot_count, atom_count),
            shape(slot_count, atom_count),
            jax.ShapeDtypeStruct((slot_count, atom_count), jnp.int32),
            shape(channel_count, atom_count),
            shape(channel_count, atom_count),
            shape(pooled_rows, channel_count),
        ),
        scratch_shapes=[
            scratch(4, 16, atom_count),
            pltpu.VMEM((direction_count, atom_count), jnp.int32),
            pltpu.VMEM((16, atom_count), jnp.int32),
            scratch(pooled_rows, atom_count),
            scratch(pooled_rows, channel_count),
            scratch(round_up(species_count, 8), channel_count),
        ],
        name="short_forward",
    )(cells, live, ids, w_radial, embedding, w_mix)
    send, cells, updated, mixed = lax.optimization_barrier((send, cells, updated, mixed))
    features = exchange(send)

    axes_block = (6, HARMONICS, chunk * atom_count)
    ready = int(chunk_count == 1 and chunk % 2 == 0)
    axes_shape = shape(6, HARMONICS, device_count * atom_count)
    table_dims = (col_count, chunk_count, lengths)
    cells_inputs, axes_outputs = (), ()
    if chunk_count == 1:
        cells_inputs, axes_outputs = (cells,), (axes_shape,)
        if ready:
            axes_outputs += (jax.ShapeDtypeStruct((8 * rows, chunk // 2 * atom_count), BF16),)
    dupd, back, phi, width, *axes = call(
        functools.partial(
            weights_kernel,
            (device_count, channel_count, own_channels, lengths, volume, radial_count),
            table_dims if chunk_count == 1 else None,
        ),
        (
            shape(channel_count, atom_count),
            shape(pooled_rows, channel_count),
            shape(4, rows, lanes),
            shape(8, lanes),
        )
        + axes_outputs,
        in_specs=[near] * (2 + len(cells_inputs)) + [kept] * len(wave_inputs),
        scratch_shapes=[pltpu.VMEM(x.shape, x.dtype) for x in wave_inputs]
        + [pltpu.SemaphoreType.DMA((len(wave_inputs),))],
        cost_estimate=pl.CostEstimate(
            flops=2 * 4 * rows * filter_gain.shape[0] * 3 * lanes,
            bytes_accessed=4 * filter_gain.size,
            transcendentals=0,
        ),
        name="weights",
    )(updated, mixed, *cells_inputs, *fetched(*wave_inputs))
    if chunk_count > 1:
        axes = [
            call(
                functools.partial(table_kernel, table_dims),
                axes_shape,
                grid=(chunk_count,),
                in_specs=[pl.BlockSpec((chunk, 2, slab_first), lambda i: (i, 0, 0))],
                out_specs=pl.BlockSpec(axes_block, lambda i: (0, 0, i)),
                name="tables",
            )(cells)
        ]
    features, dupd, back = lax.optimization_barrier((features, dupd, back))

    plane = pltpu.VMEM((8 * rows, chunk // (1 + ready) * atom_count), BF16)
    wave_scratch = [plane] + [scratch(2 * lanes, chunk * atom_count)] * 2
    features_block = (chunk, slab_features, atom_count)
    wave_options = {}
    if chunk_count > 1:
        wave_options = dict(
            grid=(2, chunk_count),
            in_specs=[
                pl.BlockSpec(features_block, lambda p, i: (i, 0, 0)),
                pl.BlockSpec(axes_block, lambda p, i: (0, 0, i)),
                pl.BlockSpec((4, rows, lanes), lambda p, i: (0, 0, 0)),
                pl.BlockSpec((8, lanes), lambda p, i: (0, 0)),
            ],
            out_specs=(
                pl.BlockSpec(features_block, lambda p, i: (i * p, 0, 0)),
                pl.BlockSpec((chunk, 4, atom_count), lambda p, i: (i * p, 0, 0)),
            ),
        )
    send, push = call(
        functools.partial(wave_kernel, (own_channels, chunk_count, lengths, ready)),
        (shape(device_count, slab_features, atom_count), shape(device_count, 4, atom_count)),
        vmem=32,
        scratch_shapes=wave_scratch
        + [scratch(4 * rows, 2 * lanes), pltpu.VMEM((12 * lanes, 4 * rows), BF16)],
        name="waves",
        **wave_options,
    )(features, axes[0], phi, width, *axes[1:])
    gradients = exchange(send)

    send = call(
        functools.partial(
            short_back_kernel, (own_channels,) + mesh_counts + (species_count, radial_count)
        ),
        shape(device_count, 4, atom_count),
        scratch_shapes=[
            scratch(channel_count, atom_count),
            scratch(pooled_rows, atom_count),
            scratch(6, slot_count, atom_count),
        ],
        name="short_back",
    )(gradients, vectors, kinds, dupd, slope, owners, back, push)
    returned = exchange(send)

    forces, virial = call(
        functools.partial(final_kernel, volume),
        (shape(3, 1, atom_count), shape(3, 3)),
        name="total",
    )(returned)
    return (forces[:, None], virial)


def solution(mesh):
    return jax.shard_map(
        per_device,
        mesh=mesh,
        in_specs=(
            P(None, "row", "col", None),
            P("row", "col", None),
            P("row", "col", None),
            P("row", "col", None, None),
            P("row", "col", None, None),
            P(),
            P(),
            P(),
            P(),
            P(),
            P(),
            P(),
            P(),
            P(),
        ),
        out_specs=(P(None, "row", "col", None), P()),
        check_vma=False,
    )
```

```python
import functools
import math

import jax
import jax.numpy as jnp
from jax import lax
from jax.experimental import pallas as pl
from jax.experimental.pallas import tpu as pltpu
from jax.sharding import PartitionSpec as P

CELL_EDGE = 12.0
HEIGHT = 36.0
KMAX = 6
HARMONICS = 8
EXACT = lax.Precision.HIGHEST
GOOD = lax.Precision.HIGH
DIRECTIONS = ((-1, -1), (-1, 0), (-1, 1), (0, -1), (0, 1), (1, -1), (1, 0), (1, 1))
F32 = jnp.float32
BF16 = jnp.bfloat16
AXES = ("row", "col")


def radial_rate(order):
    return 0.003 * 1.6**order


def round_up(value, step):
    return -(-value // step) * step


def direction_slots(row_count, col_count):
    seen = {}
    slots = []
    for row_step, col_step in DIRECTIONS:
        key = (row_step % row_count, col_step % col_count)
        slots.append(seen.get(key, 0))
        seen[key] = slots[-1] + 1
    return slots, max(seen.values())


def tile_layout(own_channels):
    shared = HARMONICS // own_channels
    return shared, -(-KMAX // shared)


def dot(lhs, rhs, lhs_dim, rhs_dim, precision=None):
    return lax.dot_general(
        lhs,
        rhs,
        (((lhs_dim,), (rhs_dim,)), ((), ())),
        precision=precision,
        preferred_element_type=F32,
    )


def split(values):
    high = values.astype(BF16).astype(F32)
    return high, values - high


def wave_weights(dims, gain_ref, waves_ref, amp_ref, width_ref, phi_ref, width_out_ref):
    device_count, channel_count, own_channels, lengths, volume = dims
    me = lax.axis_index("row") * lax.axis_size("col") + lax.axis_index("col")
    wave_count = gain_ref.shape[0]
    rows = (KMAX + 1) * HARMONICS
    together, tiles = tile_layout(own_channels)
    lanes = tiles * HARMONICS
    place = lax.broadcasted_iota(jnp.int32, (8, channel_count), 0) * device_count + me
    chosen = (lax.broadcasted_iota(jnp.int32, (8, channel_count), 1) == place).astype(F32).astype(BF16)
    first, second, third = waves_ref[0:1, :], waves_ref[1:2, :], waves_ref[2:3, :]
    sign = jnp.where(first < 0, 2, 0) + jnp.where(second < 0, 1, 0)
    key = sign * rows + jnp.abs(first) * HARMONICS + jnp.abs(second)
    spots = lax.broadcasted_iota(jnp.int32, (4 * rows, wave_count), 0) == key
    onehot = jnp.where(spots, 1.0, 0.0).astype(BF16)
    height = lax.broadcasted_iota(jnp.int32, (HARMONICS, wave_count), 0) // own_channels + 1
    here = [height + tile * together == third for tile in range(tiles)]
    rest = gain_ref[...]
    summed = 0.0
    for _ in range(3):
        part = rest.astype(BF16)
        rest = rest - part.astype(F32)
        mine = dot(chosen, part, 1, 1)
        mine = jnp.concatenate([mine[:own_channels]] * together, axis=0)
        wide = jnp.concatenate([jnp.where(spots, mine, 0.0) for spots in here], axis=0)
        summed = summed + dot(onehot, wide.astype(BF16), 1, 1)
    lane = lax.broadcasted_iota(jnp.int32, (8, channel_count), 1)
    wanted = jnp.minimum(lane % own_channels * device_count + me, channel_count - 1)
    amp = jnp.take_along_axis(jnp.broadcast_to(amp_ref[...], (8, channel_count)), wanted, axis=1)
    width = jnp.take_along_axis(
        jnp.broadcast_to(width_ref[...], (8, channel_count)), wanted, axis=1
    )
    amp, width = amp[0:1, :lanes], width[0:1, :lanes]
    k1, k2, k3 = grid_numbers(rows, lanes, own_channels, lengths)
    squared = k1 * k1 + k2 * k2 + k3 * k3
    base = amp * jnp.exp(-width * squared) * (1.0 / volume)
    for sign_id in range(4):
        phi_ref[sign_id] = base * summed[sign_id * rows : (sign_id + 1) * rows, :]
    width_out_ref[...] = jnp.broadcast_to(width, (8, lanes))


def grid_numbers(rows, lanes, own_channels, lengths):
    row_id = lax.broadcasted_iota(jnp.int32, (rows, lanes), 0)
    lane_id = lax.broadcasted_iota(jnp.int32, (rows, lanes), 1)
    k1 = (row_id // HARMONICS).astype(F32) * (2.0 * math.pi / lengths[0])
    k2 = (row_id % HARMONICS).astype(F32) * (2.0 * math.pi / lengths[1])
    k3 = (lane_id // own_channels + 1).astype(F32) * (2.0 * math.pi / lengths[2])
    return k1, k2, k3


def neighbour_of(step, row_count, col_count):
    row = lax.rem(lax.axis_index("row") + step[0] + row_count, row_count)
    col = lax.rem(lax.axis_index("col") + step[1] + col_count, col_count)
    return row * col_count + col


def slab_rows(slab, rows, atom_count):
    width = slab.shape[-1] // atom_count
    return [
        slab[row // width : row // width + 1, row % width * atom_count : (row % width + 1) * atom_count]
        for row in rows
    ]


def pack_kernel(counts, copied, positions_ref, species_ref, ghosts_ref, *refs):
    row_count, col_count = counts
    sources, (send_ref, *targets) = refs[:copied], refs[copied : 2 * copied + 1]
    positions, species, ghosts, first_sems, sems = refs[2 * copied + 1 :]
    firsts = ((positions_ref, positions), (species_ref, species), (ghosts_ref, ghosts))
    firsts = start_copies(firsts, first_sems)
    others = start_copies(tuple(zip(sources, targets)), sems)
    device_count = send_ref.shape[0]
    atom_count = species.shape[1]
    width = send_ref.shape[2] // atom_count
    slots, _ = direction_slots(row_count, col_count)
    for copy in firsts:
        copy.wait()
    rows = [positions[0], positions[1], positions[2], species[...].astype(F32)]
    for row, values in enumerate(rows):
        low = row % width * atom_count
        send_ref[:, row // width, low : low + atom_count] = jnp.broadcast_to(
            values, (device_count, atom_count)
        )
    for order, step in enumerate(DIRECTIONS):
        target = neighbour_of(step, row_count, col_count)
        row = 4 + slots[order]
        low = row % width * atom_count
        send_ref[target, row // width, low : low + atom_count] = ghosts[order, :].astype(F32)
    for copy in others:
        copy.wait()


def start_copies(pairs, sems):
    copies = [
        pltpu.make_async_copy(source, target, sems.at[spot])
        for spot, (source, target) in enumerate(pairs)
    ]
    for copy in copies:
        copy.start()
    return copies


def weights_kernel(dims, table_dims, upd_ref, mixed_ref, *refs):
    cells, refs = refs[: bool(table_dims)], refs[bool(table_dims) :]
    sources, (dupd_ref, back_ref, phi_ref, width_out_ref), refs = refs[:6], refs[6:10], refs[10:]
    axes, targets, sems = refs[: len(refs) - 7], refs[-7:-1], refs[-1]
    copies = start_copies(tuple(zip(sources, targets)), sems)
    if table_dims:
        table_kernel(table_dims, *cells, axes[0])
        if len(axes) > 1:
            wave_planes(axes[1], axes[0], range(axes[1].shape[1] // upd_ref.shape[1]))
    pooled_rows, channel_count = mixed_ref.shape
    radial_count = dims[5]
    order_id = lax.broadcasted_iota(jnp.int32, (pooled_rows, channel_count), 0) % radial_count
    factor = jnp.zeros((pooled_rows, channel_count), F32)
    for order in range(radial_count):
        factor = jnp.where(order_id == order, -2.0 * radial_rate(order), factor)
    back_ref[...] = mixed_ref[...] * factor
    for copy in copies[:2]:
        copy.wait()
    readout_gradient(upd_ref, targets[0], targets[1], dupd_ref)
    for copy in copies[2:]:
        copy.wait()
    wave_weights(dims[:5], *targets[2:], phi_ref, width_out_ref)


def short_forward_kernel(
    dims,
    cells_ref,
    counts_ref,
    ids_ref,
    radial_ref,
    embed_ref,
    mix_ref,
    send_ref,
    vec_ref,
    kind_ref,
    owner_ref,
    upd_ref,
    slope_ref,
    mixed_ref,
    table,
    lists,
    codes,
    pooled,
    weights,
    kinds8,
):
    own_channels, row_count, col_count = dims
    slot_count, atom_count = ids_ref.shape
    species_count, channel_count = embed_ref.shape
    radial_count = radial_ref.shape[0]
    device_count = send_ref.shape[0]
    slots, _ = direction_slots(row_count, col_count)
    for k in range(species_count):
        weights[k * radial_count : (k + 1) * radial_count, :] = (
            radial_ref[...] * embed_ref[k : k + 1, :] * (1.0 / slot_count)
        )
    weights[...] = dot(weights[...], mix_ref[...], 1, 0, EXACT)
    mixed_ref[...] = weights[...]
    own = slab_rows(cells_ref[neighbour_of((0, 0), row_count, col_count)], range(4), atom_count)
    domains, places = [], []
    for step in DIRECTIONS:
        key = (step[0] % row_count, step[1] % col_count)
        if key not in domains:
            domains.append(key)
        places.append(domains.index(key))
    for part in range(3):
        table[part, 0:1, :] = own[part]
    for place, key in enumerate(domains):
        block = slab_rows(cells_ref[neighbour_of(key, row_count, col_count)], range(3), atom_count)
        for part in range(3):
            table[part, 8 + place : 9 + place, :] = block[part]
    for order, step in enumerate(DIRECTIONS):
        list_row = 4 + slots[len(DIRECTIONS) - 1 - order]
        source = neighbour_of(step, row_count, col_count)
        kinds_row, list_values = slab_rows(cells_ref[source], (3, list_row), atom_count)
        table[3, 8 + order : 9 + order, :] = kinds_row
        lists[order : order + 1, :] = list_values.astype(jnp.int32)
    picks = lists[...]
    ghost_kinds = jnp.take_along_axis(table[3, 8:16, :], picks, axis=1)
    codes[8:16, :] = picks + atom_count * ghost_kinds.astype(jnp.int32)
    codes[0:1, :] = lax.broadcasted_iota(
        jnp.int32, (1, atom_count), 1
    ) + atom_count * own[3].astype(jnp.int32)

    ids = ids_ref[...]
    lane = ids & (atom_count - 1)
    source = ids // atom_count

    def picked(ref, index, marks):
        values = jnp.take_along_axis(jnp.broadcast_to(ref[0:1, :], ids.shape), index, axis=1)
        for place, mark in enumerate(marks):
            wide = jnp.broadcast_to(ref[8 + place : 9 + place, :], ids.shape)
            values = jnp.where(mark, jnp.take_along_axis(wide, index, axis=1), values)
        return values

    marks = [source == order + 1 for order in range(len(DIRECTIONS))]
    code = picked(codes, lane, marks)
    owner = code & (atom_count - 1)
    owner_ref[...] = owner + source * atom_count
    merged = []
    for place in range(len(domains)):
        mine = [mark for mark, other in zip(marks, places) if other == place]
        merged.append(functools.reduce(jnp.logical_or, mine))
    gathered = [picked(table.at[part], owner, merged) for part in range(3)]
    for axis in range(2):
        shift = jnp.zeros(ids.shape, F32)
        for mark, step in zip(marks, DIRECTIONS):
            if step[axis]:
                shift = jnp.where(mark, step[axis] * CELL_EDGE, shift)
        gathered[axis] = gathered[axis] + shift
    gathered.append((code // atom_count).astype(F32))
    slot = lax.broadcasted_iota(jnp.int32, ids.shape, 0)
    kind = jnp.where(slot < counts_ref[...], gathered[3], -1.0)
    kind_ref[...] = kind
    squared = jnp.zeros(ids.shape, F32)
    for part in range(3):
        vector = gathered[part] - own[part]
        vec_ref[part] = vector
        squared = squared + vector * vector
    masks = [kind == float(k) for k in range(species_count)]
    for order in range(radial_count):
        basis = jnp.exp(squared * (-radial_rate(order)))
        for k in range(species_count):
            spot = k * radial_count + order
            pooled[spot : spot + 1, :] = jnp.sum(
                jnp.where(masks[k], basis, 0.0), axis=0, keepdims=True
            )
    kinds8[...] = jnp.zeros_like(kinds8)
    kinds8[0:species_count, :] = embed_ref[...]
    own_hot = (
        lax.broadcasted_iota(jnp.int32, (kinds8.shape[0], atom_count), 0).astype(F32) == own[3]
    ).astype(F32)
    initial = dot(kinds8[...], own_hot, 0, 0, EXACT)
    before = dot(weights[...], pooled[...], 0, 0, GOOD)
    gate = 1.0 / (1.0 + jnp.exp(-before))
    updated = initial + before * gate
    slope_ref[...] = gate + before * gate * (1.0 - gate)
    for q in range(own_channels):
        low, high = q * device_count, min(channel_count, (q + 1) * device_count)
        send_ref[0 : high - low, q, :] = updated[low:high, :]
        if high - low < device_count:
            send_ref[high - low :, q, :] = jnp.zeros(
                (device_count - (high - low), atom_count), F32
            )
    upd_ref[...] = updated


def readout_gradient(upd_ref, read_ref, out_ref, dupd_ref):
    channel_count, atom_count = upd_ref.shape
    readout = dot(read_ref[...], upd_ref[...], 0, 0, GOOD)
    gate = 1.0 / (1.0 + jnp.exp(-readout))
    scale = jnp.broadcast_to(out_ref[...], (channel_count, channel_count)).T
    dread = scale[:, 0:atom_count] * (gate + readout * gate * (1.0 - gate))
    dupd_ref[...] = dot(read_ref[...], dread, 1, 0, GOOD)


def turn_tables(turns, multiples):
    angle = turns * multiples
    halves = jnp.floor(2.0 * angle + 0.5)
    rest = angle - 0.5 * halves
    sign = 1.0 - 2.0 * (halves - 2.0 * jnp.floor(0.5 * halves))
    square = rest * rest

    def series(first, last):
        terms = [
            (-1.0) ** (p // 2) * (2.0 * math.pi) ** p / math.factorial(p)
            for p in range(first, last + 1, 2)
        ]
        total = jnp.full_like(square, terms[-1])
        for term in reversed(terms[:-1]):
            total = total * square + term
        return total

    return sign * series(0, 12), sign * rest * series(1, 13)


def table_kernel(dims, cells_ref, axes_ref):
    col_count, chunk_count, lengths = dims
    chunk = cells_ref.shape[0]
    atom_count = axes_ref.shape[2] // chunk
    first_device = pl.program_id(0) * chunk if chunk_count > 1 else 0
    multiples = lax.broadcasted_iota(jnp.int32, (HARMONICS, atom_count), 0).astype(F32)

    def one(index, _):
        device = first_device + index
        spot = pl.ds(pl.multiple_of(index * atom_count, atom_count), atom_count)
        block = slab_rows(cells_ref[index], range(3), atom_count)
        corner_row = (device // col_count).astype(F32) * CELL_EDGE
        corner_col = (device % col_count).astype(F32) * CELL_EDGE
        turns = (
            (block[0] + corner_row) * (1.0 / lengths[0]),
            (block[1] + corner_col) * (1.0 / lengths[1]),
            block[2] * (1.0 / lengths[2]),
        )
        for axis in range(3):
            numbers = multiples + 1.0 if axis == 2 else multiples
            cos, sin = turn_tables(turns[axis], numbers)
            axes_ref[2 * axis, :, spot] = cos
            axes_ref[2 * axis + 1, :, spot] = sin
        return 0

    lax.fori_loop(0, chunk, one, 0, unroll=4)


def wave_kernel(dims, recv_ref, axes_ref, phi_ref, width_ref, *refs):
    own_channels, chunk_count, lengths, ready = dims
    made, (send_ref, push_ref, *planes), (heights, lifted, sums, coefficients) = refs[:ready], refs[ready:-4], refs[-4:]
    planes = (*made, *planes)
    parts = (planes, ready, axes_ref, heights, lifted)

    def back():
        wave_back(own_channels, lengths, planes, heights, lifted, coefficients, send_ref, push_ref)
        virial = wave_virial(own_channels, lengths, sums, phi_ref, width_ref, (1, push_ref.shape[2]))
        push_ref[:, 3, :] = jnp.broadcast_to(virial, (push_ref.shape[0], push_ref.shape[2]))

    if chunk_count == 1:
        sums[...] = wave_sums(own_channels, recv_ref, *parts)
        wave_coefficients(sums, phi_ref, coefficients)
        back()
        return
    phase, chunk_id = pl.program_id(0), pl.program_id(1)

    @pl.when((phase == 0) & (chunk_id == 0))
    def _():
        sums[...] = jnp.zeros_like(sums)

    part = wave_sums(own_channels, recv_ref, *parts)

    @pl.when(phase == 0)
    def _():
        sums[...] += part

    @pl.when((phase == 1) & (chunk_id == 0))
    def _():
        wave_coefficients(sums, phi_ref, coefficients)

    @pl.when(phase == 1)
    def _():
        back()


def wave_planes(planes_ref, axes_ref, devices):
    atom_count = planes_ref.shape[1] // len(devices)
    count = planes_ref.shape[0] // 2
    for place, index in enumerate(devices):
        spot = slice(index * atom_count, (index + 1) * atom_count)
        target = slice(place * atom_count, (place + 1) * atom_count)
        products = [
            axes_ref[first_axis, m : m + 1, spot] * axes_ref[second_axis, :, spot]
            for first_axis, second_axis in ((0, 2), (0, 3), (1, 2), (1, 3))
            for m in range(KMAX + 1)
        ]
        for pair in range(len(products) // 2):
            both = jnp.concatenate(products[2 * pair : 2 * pair + 2], axis=0)
            high = both.astype(BF16)
            rows = slice(2 * HARMONICS * pair, 2 * HARMONICS * (pair + 1))
            planes_ref[rows, target] = high
            rows = slice(count + rows.start, count + rows.stop)
            planes_ref[rows, target] = (both - high.astype(F32)).astype(BF16)


def wave_lift(own_channels, recv_ref, axes_ref, heights, lifted, devices):
    atom_count = recv_ref.shape[2]
    together, tiles = tile_layout(own_channels)
    lanes = tiles * HARMONICS
    sublane = lax.broadcasted_iota(jnp.int32, (HARMONICS, atom_count), 0)
    for index in devices:
        spot = slice(index * atom_count, (index + 1) * atom_count)
        feature = jnp.concatenate([recv_ref[index, 0:own_channels, :]] * together, axis=0)
        for part in range(2):
            for tile in range(tiles):
                first = tile * together
                height = jnp.broadcast_to(axes_ref[4 + part, first : first + 1, spot], sublane.shape)
                for n in range(1, together):
                    height = jnp.where(
                        sublane >= n * own_channels, axes_ref[4 + part, first + n : first + n + 1, spot], height
                    )
                row = part * lanes + tile * HARMONICS
                heights[row : row + HARMONICS, spot] = height
                lifted[row : row + HARMONICS, spot] = feature * height


def plane_groups(chunk, planes):
    each = chunk // len(planes)
    return [(ref, range(place * each, (place + 1) * each)) for place, ref in enumerate(planes)]


def wave_sums(own_channels, recv_ref, planes, ready, axes_ref, heights, lifted):
    chunk, _, atom_count = recv_ref.shape
    lanes = lifted.shape[0] // 2
    total = 0.0
    for place, (ref, devices) in enumerate(plane_groups(chunk, planes)):
        wave_lift(own_channels, recv_ref, axes_ref, heights, lifted, devices)
        if place >= ready:
            wave_planes(ref, axes_ref, devices)
        count = ref.shape[0] // 2
        values = lifted[:, devices[0] * atom_count : (devices[-1] + 1) * atom_count]
        high = values.astype(BF16)
        low = (values - high.astype(F32)).astype(BF16)
        main = dot(ref[0:count, :], jnp.concatenate([high, low], axis=0), 1, 1)
        total = total + main[:, : 2 * lanes] + (main[:, 2 * lanes :] + dot(ref[count:, :], high, 1, 1))
    return total


SIGNS = ((1.0, 1.0), (1.0, -1.0), (-1.0, 1.0), (-1.0, -1.0))


def wave_blocks(sums_ref, phi_ref):
    _, rows, lanes = phi_ref.shape
    sums = sums_ref[...]
    cos_part, sin_part = sums[:, :lanes], sums[:, lanes:]
    cc_c, cs_c, sc_c, ss_c = (cos_part[p * rows : (p + 1) * rows] for p in range(4))
    cc_s, cs_s, sc_s, ss_s = (sin_part[p * rows : (p + 1) * rows] for p in range(4))
    for sign_id, (s1, s2) in enumerate(SIGNS):
        real = cc_c - s1 * s2 * ss_c - s1 * sc_s - s2 * cs_s
        imag = cc_s - s1 * s2 * ss_s + s1 * sc_c + s2 * cs_c
        phi = phi_ref[sign_id]
        yield s1, s2, phi * real, phi * imag, real, imag


def wave_virial(own_channels, lengths, sums_ref, phi_ref, width_ref, shape):
    _, rows, lanes = phi_ref.shape
    even = first_odd = second_odd = both_odd = jnp.zeros((rows, lanes), F32)
    for s1, s2, dreal, dimag, real, imag in wave_blocks(sums_ref, phi_ref):
        power = dreal * real + dimag * imag
        even = even + power
        first_odd = first_odd + s1 * power
        second_odd = second_odd + s2 * power
        both_odd = both_odd + s1 * s2 * power
    width = width_ref[0:1, :]
    k1, k2, k3 = grid_numbers(rows, lanes, own_channels, lengths)

    def total_of(values):
        return jnp.sum(jnp.sum(values, axis=0, keepdims=True), axis=1, keepdims=True)

    energy = 0.5 * total_of(even)
    scaled = width * even
    terms = {
        (0, 0): energy - total_of(k1 * k1 * scaled),
        (1, 1): energy - total_of(k2 * k2 * scaled),
        (2, 2): energy - total_of(k3 * k3 * scaled),
        (0, 1): -total_of(k1 * k2 * width * both_odd),
        (0, 2): -total_of(k1 * k3 * width * first_odd),
        (1, 2): -total_of(k2 * k3 * width * second_odd),
    }
    return virial_row(terms, shape)


def wave_coefficients(sums_ref, phi_ref, coefficients_ref):
    _, rows, lanes = phi_ref.shape
    zero = jnp.zeros((rows, lanes), F32)
    d_cc_c = d_cc_s = d_cs_c = d_cs_s = d_sc_c = d_sc_s = d_ss_c = d_ss_s = zero
    for s1, s2, dreal, dimag, _, _ in wave_blocks(sums_ref, phi_ref):
        d_cc_c, d_ss_c = d_cc_c + dreal, d_ss_c - s1 * s2 * dreal
        d_sc_s, d_cs_s = d_sc_s - s1 * dreal, d_cs_s - s2 * dreal
        d_cc_s, d_ss_s = d_cc_s + dimag, d_ss_s - s1 * s2 * dimag
        d_sc_c, d_cs_c = d_sc_c + s1 * dimag, d_cs_c + s2 * dimag
    values = jnp.concatenate(
        [
            jnp.concatenate(pair, axis=1)
            for pair in ((d_cc_c, d_cc_s), (d_cs_c, d_cs_s), (d_sc_c, d_sc_s), (d_ss_c, d_ss_s))
        ],
        axis=0,
    )
    cc, cs, sc, ss = (values[p * rows : (p + 1) * rows] for p in range(4))
    row_id = lax.broadcasted_iota(jnp.int32, (rows, 2 * lanes), 0)
    m1 = (row_id // HARMONICS).astype(F32)
    m2 = (row_id % HARMONICS).astype(F32)
    along_x = jnp.concatenate([m1 * sc, m1 * ss, -m1 * cc, -m1 * cs], axis=0)
    along_y = jnp.concatenate([m2 * cs, -m2 * cc, m2 * ss, -m2 * sc], axis=0)
    values = jnp.concatenate([values, along_x, along_y], axis=1)
    turned = values.T
    high = turned.astype(BF16)
    count = turned.shape[0]
    coefficients_ref[0:count, :] = high
    coefficients_ref[count:, :] = (turned - high.astype(F32)).astype(BF16)


def wave_spread(planes_ref, coefficients):
    values = coefficients[...]
    count = values.shape[0] // 2
    both = jnp.concatenate([values[:count], values[:count]], axis=1)
    return dot(both, planes_ref[...], 1, 0) + dot(values[count:], planes_ref[0 : values.shape[1], :], 1, 0)


def wave_back(own_channels, lengths, planes, heights, lifted, coefficients, send_ref, push_ref):
    chunk, _, atom_count = push_ref.shape
    together, tiles = tile_layout(own_channels)
    lanes = tiles * HARMONICS
    sublane = lax.broadcasted_iota(jnp.int32, (HARMONICS, atom_count), 0)
    numbers = [(sublane // own_channels + 1 + tile * together).astype(F32) for tile in range(tiles)]
    spread = []
    for ref, devices in plane_groups(chunk, planes):
        result = wave_spread(ref, coefficients)
        spread += [(result, place, index) for place, index in enumerate(devices)]
    for result, place, index in spread:
        spot = slice(index * atom_count, (index + 1) * atom_count)
        part = result[:, place * atom_count : (place + 1) * atom_count]
        feature = grad_x = grad_y = grad_z = jnp.zeros((HARMONICS, atom_count), F32)
        for tile in range(tiles):
            a, b = tile * HARMONICS, lanes + tile * HARMONICS
            on_cos, on_sin = part[a : a + HARMONICS], part[b : b + HARMONICS]
            feature = feature + on_cos * heights[a : a + HARMONICS, spot] + on_sin * heights[b : b + HARMONICS, spot]
            lift_cos = lifted[a : a + HARMONICS, spot]
            lift_sin = lifted[b : b + HARMONICS, spot]
            grad_z = grad_z + numbers[tile] * (on_sin * lift_cos - on_cos * lift_sin)
            a, b = a + 2 * lanes, b + 2 * lanes
            grad_x = grad_x + part[a : a + HARMONICS] * lift_cos + part[b : b + HARMONICS] * lift_sin
            a, b = a + 2 * lanes, b + 2 * lanes
            grad_y = grad_y + part[a : a + HARMONICS] * lift_cos + part[b : b + HARMONICS] * lift_sin
        total = feature[0:own_channels]
        for n in range(1, together):
            total = total + feature[n * own_channels : (n + 1) * own_channels]
        send_ref[index, 0:own_channels, :] = total
        pieces = (
            grad_x * (2.0 * math.pi / lengths[0]),
            grad_y * (2.0 * math.pi / lengths[1]),
            grad_z * (2.0 * math.pi / lengths[2]),
        )
        first, second, third = (piece + pltpu.roll(piece, HARMONICS // 2, 0) for piece in pieces)
        first = jnp.where(sublane < HARMONICS // 2, first, second)
        first = first + pltpu.roll(first, 2, 0)
        third = third + pltpu.roll(third, 2, 0)
        first = jnp.where(sublane % 4 >= 2, first, third)
        first = first + pltpu.roll(first, 1, 0)
        for row, place in enumerate((3, 7, 1)):
            push_ref[index, row : row + 1, :] = first[place : place + 1]


def virial_row(terms, shape):
    lane = lax.broadcasted_iota(jnp.int32, shape, 1)
    row = jnp.zeros(shape, F32)
    for (i, j), value in terms.items():
        spots = (lane == 3 * i + j) | (lane == 3 * j + i)
        row = jnp.where(spots, value, row)
    return row


def short_back_kernel(
    dims,
    recv_ref,
    vec_ref,
    kind_ref,
    dupd_ref,
    slope_ref,
    owner_ref,
    back_ref,
    push_ref,
    send_ref,
    fgrad,
    dpool,
    parts,
):
    own_channels, row_count, col_count, species_count, radial_count = dims
    slot_count, atom_count = owner_ref.shape
    channel_count = back_ref.shape[1]
    device_count = send_ref.shape[0]
    table_rows = round_up(len(DIRECTIONS) + 1, 16)
    for q in range(own_channels):
        low, high = q * device_count, min(channel_count, (q + 1) * device_count)
        fgrad[low:high, :] = recv_ref[0 : high - low, q, :]
    dbefore = (fgrad[...] + dupd_ref[...]) * slope_ref[...]
    dpool[...] = dot(back_ref[...], dbefore, 1, 0, GOOD)
    vectors = [vec_ref[part] for part in range(3)]
    squared = vectors[0] * vectors[0] + vectors[1] * vectors[1] + vectors[2] * vectors[2]
    kind = kind_ref[...]
    sums = [jnp.zeros(kind.shape, F32) for _ in range(species_count)]
    for order in range(radial_count):
        basis = jnp.exp(squared * (-radial_rate(order)))
        for k in range(species_count):
            spot = k * radial_count + order
            sums[k] = sums[k] + basis * dpool[spot : spot + 1, :]
    slope = jnp.zeros(kind.shape, F32)
    for k in range(species_count):
        slope = jnp.where(kind == float(k), sums[k], slope)
    grads = [slope * vector for vector in vectors]

    def total_of(values):
        return jnp.sum(jnp.sum(values, axis=0, keepdims=True), axis=1, keepdims=True)

    terms = {
        (i, j): -total_of(grads[i] * vectors[j]) for i in range(3) for j in range(i, 3)
    }
    virial = virial_row(terms, (1, atom_count))
    for part in range(3):
        parts[2 * part], parts[2 * part + 1] = split(grads[part])

    sublane = lax.broadcasted_iota(jnp.int32, (atom_count, atom_count), 0)
    table_id = lax.broadcasted_iota(jnp.int32, (table_rows, atom_count), 0)
    group = 8
    scattered = jnp.zeros((atom_count, 6 * table_rows), F32)
    for low in range(0, slot_count, group):
        hots, columns = [], []
        for s in range(low, low + group):
            ids = owner_ref[s : s + 1, :]
            hots.append(jnp.where(sublane == (ids & (atom_count - 1)), 1.0, 0.0).astype(BF16))
            mine = table_id == ids // atom_count
            columns.append(
                jnp.concatenate(
                    [
                        jnp.where(mine, parts[p, s : s + 1, :], 0.0).astype(BF16)
                        for p in range(6)
                    ],
                    axis=0,
                )
            )
        scattered = scattered + dot(
            jnp.concatenate(hots, axis=1), jnp.concatenate(columns, axis=1), 1, 1
        )
    rows = scattered.T
    send_ref[...] = push_ref[...]
    send_ref[:, 3, :] += jnp.broadcast_to(virial, (device_count, atom_count))
    me = neighbour_of((0, 0), row_count, col_count)
    for part in range(3):
        low = 2 * part * table_rows
        both = rows[low : low + table_rows] + rows[low + table_rows : low + 2 * table_rows]
        send_ref[me, part, :] += both[0, :] - jnp.sum(grads[part], axis=0)
        for order, step in enumerate(DIRECTIONS):
            target = neighbour_of(step, row_count, col_count)
            send_ref[target, part, :] += both[1 + order, :]


def final_kernel(volume, recv_ref, forces_ref, virial_ref):
    total = jnp.sum(recv_ref[...], axis=0)
    for part in range(3):
        forces_ref[part] = -total[part : part + 1, :]
    virial = total[3:4, :] * (1.0 / volume)
    for i in range(3):
        virial_ref[i : i + 1, :] = virial[:, 3 * i : 3 * i + 3]


def per_device(
    positions,
    species,
    counts,
    neighbours,
    ghost_index,
    wave_numbers,
    embedding,
    w_radial,
    w_mix,
    w_read,
    w_out,
    amplitude,
    kernel_width,
    filter_gain,
):
    row_count = lax.axis_size("row")
    col_count = lax.axis_size("col")
    device_count = row_count * col_count
    atom_count = positions.shape[3]
    slot_count = neighbours.shape[2]
    direction_count, ghost_count = ghost_index.shape[2:]
    species_count, channel_count = embedding.shape
    radial_count = w_radial.shape[0]
    own_channels = -(-channel_count // device_count)
    lengths = (CELL_EDGE * row_count, CELL_EDGE * col_count, HEIGHT)
    volume = lengths[0] * lengths[1] * lengths[2]
    rows = (KMAX + 1) * HARMONICS
    lanes = tile_layout(own_channels)[1] * HARMONICS
    _, shared = direction_slots(row_count, col_count)
    slab_first = round_up(4 + shared, 2) // 2 * atom_count
    slab_features = round_up(own_channels, 4)
    chunk = math.gcd(device_count, 32)
    chunk_count = device_count // chunk

    def exchange(slabs):
        return lax.all_to_all(slabs, AXES, 0, 0, tiled=True)

    def shape(*dims):
        return jax.ShapeDtypeStruct(dims, F32)

    def scratch(*dims):
        return pltpu.VMEM(dims, F32)

    def call(kernel, out_shape, vmem=16, **options):
        return pl.pallas_call(
            kernel,
            out_shape=out_shape,
            compiler_params=pltpu.CompilerParams(vmem_limit_bytes=vmem * 1024 * 1024),
            **options,
        )

    ids = neighbours.reshape(slot_count, atom_count)
    ghosts = ghost_index.reshape(direction_count, ghost_count)
    mesh_counts = (row_count, col_count)
    inputs = (
        counts.reshape(1, atom_count),
        ids,
        w_radial,
        embedding,
        w_mix,
    )
    wave_inputs = (
        w_read,
        w_out.reshape(1, -1),
        filter_gain,
        wave_numbers,
        amplitude.reshape(1, -1),
        kernel_width.reshape(1, -1),
    )

    def fetched(*arrays):
        return [pltpu.with_memory_space_constraint(x, pltpu.HBM) for x in arrays]

    kept = pl.BlockSpec(memory_space=pltpu.HBM)
    near = pl.BlockSpec(memory_space=pltpu.VMEM)
    send, *inputs = call(
        functools.partial(pack_kernel, mesh_counts, len(inputs)),
        (shape(device_count, 2, slab_first),)
        + tuple(jax.ShapeDtypeStruct(x.shape, x.dtype) for x in inputs),
        in_specs=[kept] * (3 + len(inputs)),
        scratch_shapes=[
            scratch(3, 1, atom_count),
            pltpu.VMEM((1, atom_count), jnp.int32),
            pltpu.VMEM(ghosts.shape, jnp.int32),
            pltpu.SemaphoreType.DMA((3,)),
            pltpu.SemaphoreType.DMA((len(inputs),)),
        ],
        name="pack",
    )(*fetched(positions.reshape(3, 1, atom_count), species.reshape(1, atom_count), ghosts, *inputs))
    live, ids, w_radial, embedding, w_mix = inputs
    cells = exchange(send)

    pooled_rows = species_count * radial_count
    send, vectors, kinds, owners, updated, slope, mixed = call(
        functools.partial(short_forward_kernel, (own_channels,) + mesh_counts),
        (
            shape(device_count, slab_features, atom_count),
            shape(3, slot_count, atom_count),
            shape(slot_count, atom_count),
            jax.ShapeDtypeStruct((slot_count, atom_count), jnp.int32),
            shape(channel_count, atom_count),
            shape(channel_count, atom_count),
            shape(pooled_rows, channel_count),
        ),
        scratch_shapes=[
            scratch(4, 16, atom_count),
            pltpu.VMEM((direction_count, atom_count), jnp.int32),
            pltpu.VMEM((16, atom_count), jnp.int32),
            scratch(pooled_rows, atom_count),
            scratch(pooled_rows, channel_count),
            scratch(round_up(species_count, 8), channel_count),
        ],
        name="short_forward",
    )(cells, live, ids, w_radial, embedding, w_mix)
    send, cells, updated, mixed = lax.optimization_barrier((send, cells, updated, mixed))
    features = exchange(send)

    axes_block = (6, HARMONICS, chunk * atom_count)
    ready = int(chunk_count == 1 and chunk % 2 == 0)
    axes_shape = shape(6, HARMONICS, device_count * atom_count)
    table_dims = (col_count, chunk_count, lengths)
    cells_inputs, axes_outputs = (), ()
    if chunk_count == 1:
        cells_inputs, axes_outputs = (cells,), (axes_shape,)
        if ready:
            axes_outputs += (jax.ShapeDtypeStruct((8 * rows, chunk // 2 * atom_count), BF16),)
    dupd, back, phi, width, *axes = call(
        functools.partial(
            weights_kernel,
            (device_count, channel_count, own_channels, lengths, volume, radial_count),
            table_dims if chunk_count == 1 else None,
        ),
        (
            shape(channel_count, atom_count),
            shape(pooled_rows, channel_count),
            shape(4, rows, lanes),
            shape(8, lanes),
        )
        + axes_outputs,
        in_specs=[near] * (2 + len(cells_inputs)) + [kept] * len(wave_inputs),
        scratch_shapes=[pltpu.VMEM(x.shape, x.dtype) for x in wave_inputs]
        + [pltpu.SemaphoreType.DMA((len(wave_inputs),))],
        cost_estimate=pl.CostEstimate(
            flops=2 * 4 * rows * filter_gain.shape[0] * 3 * lanes,
            bytes_accessed=4 * filter_gain.size,
            transcendentals=0,
        ),
        name="weights",
    )(updated, mixed, *cells_inputs, *fetched(*wave_inputs))
    if chunk_count > 1:
        axes = [
            call(
                functools.partial(table_kernel, table_dims),
                axes_shape,
                grid=(chunk_count,),
                in_specs=[pl.BlockSpec((chunk, 2, slab_first), lambda i: (i, 0, 0))],
                out_specs=pl.BlockSpec(axes_block, lambda i: (0, 0, i)),
                name="tables",
            )(cells)
        ]
    features, dupd, back = lax.optimization_barrier((features, dupd, back))

    plane = pltpu.VMEM((8 * rows, chunk // (1 + ready) * atom_count), BF16)
    wave_scratch = [plane] + [scratch(2 * lanes, chunk * atom_count)] * 2
    features_block = (chunk, slab_features, atom_count)
    wave_options = {}
    if chunk_count > 1:
        wave_options = dict(
            grid=(2, chunk_count),
            in_specs=[
                pl.BlockSpec(features_block, lambda p, i: (i, 0, 0)),
                pl.BlockSpec(axes_block, lambda p, i: (0, 0, i)),
                pl.BlockSpec((4, rows, lanes), lambda p, i: (0, 0, 0)),
                pl.BlockSpec((8, lanes), lambda p, i: (0, 0)),
            ],
            out_specs=(
                pl.BlockSpec(features_block, lambda p, i: (i * p, 0, 0)),
                pl.BlockSpec((chunk, 4, atom_count), lambda p, i: (i * p, 0, 0)),
            ),
        )
    send, push = call(
        functools.partial(wave_kernel, (own_channels, chunk_count, lengths, ready)),
        (shape(device_count, slab_features, atom_count), shape(device_count, 4, atom_count)),
        vmem=32,
        scratch_shapes=wave_scratch
        + [scratch(4 * rows, 2 * lanes), pltpu.VMEM((12 * lanes, 4 * rows), BF16)],
        name="waves",
        **wave_options,
    )(features, axes[0], phi, width, *axes[1:])
    gradients = exchange(send)

    send = call(
        functools.partial(
            short_back_kernel, (own_channels,) + mesh_counts + (species_count, radial_count)
        ),
        shape(device_count, 4, atom_count),
        scratch_shapes=[
            scratch(channel_count, atom_count),
            scratch(pooled_rows, atom_count),
            scratch(6, slot_count, atom_count),
        ],
        name="short_back",
    )(gradients, vectors, kinds, dupd, slope, owners, back, push)
    returned = exchange(send)

    forces, virial = call(
        functools.partial(final_kernel, volume),
        (shape(3, 1, atom_count), shape(3, 3)),
        name="total",
    )(returned)
    return (forces[:, None], virial)


def solution(mesh):
    return jax.shard_map(
        per_device,
        mesh=mesh,
        in_specs=(
            P(None, "row", "col", None),
            P("row", "col", None),
            P("row", "col", None),
            P("row", "col", None, None),
            P("row", "col", None, None),
            P(),
            P(),
            P(),
            P(),
            P(),
            P(),
            P(),
            P(),
            P(),
        ),
        out_specs=(P(None, "row", "col", None), P()),
        check_vma=False,
    )
```

```python
import functools
import math

import jax
import jax.numpy as jnp
from jax import lax
from jax.experimental import pallas as pl
from jax.experimental.pallas import tpu as pltpu
from jax.sharding import PartitionSpec as P

CELL_EDGE = 12.0
HEIGHT = 36.0
KMAX = 6
HARMONICS = 8
EXACT = lax.Precision.HIGHEST
GOOD = lax.Precision.HIGH
DIRECTIONS = ((-1, -1), (-1, 0), (-1, 1), (0, -1), (0, 1), (1, -1), (1, 0), (1, 1))
F32 = jnp.float32
BF16 = jnp.bfloat16
AXES = ("row", "col")


def radial_rate(order):
    return 0.003 * 1.6**order


def round_up(value, step):
    return -(-value // step) * step


def direction_slots(row_count, col_count):
    seen = {}
    slots = []
    for row_step, col_step in DIRECTIONS:
        key = (row_step % row_count, col_step % col_count)
        slots.append(seen.get(key, 0))
        seen[key] = slots[-1] + 1
    return slots, max(seen.values())


def tile_layout(own_channels):
    shared = HARMONICS // own_channels
    return shared, -(-KMAX // shared)


def dot(lhs, rhs, lhs_dim, rhs_dim, precision=None):
    return lax.dot_general(
        lhs,
        rhs,
        (((lhs_dim,), (rhs_dim,)), ((), ())),
        precision=precision,
        preferred_element_type=F32,
    )


def split(values):
    high = values.astype(BF16).astype(F32)
    return high, values - high


def wave_weights(dims, gain_ref, waves_ref, amp_ref, width_ref, phi_ref, width_out_ref):
    device_count, channel_count, own_channels, lengths, volume = dims
    me = lax.axis_index("row") * lax.axis_size("col") + lax.axis_index("col")
    wave_count = gain_ref.shape[0]
    rows = (KMAX + 1) * HARMONICS
    together, tiles = tile_layout(own_channels)
    lanes = tiles * HARMONICS
    place = lax.broadcasted_iota(jnp.int32, (8, channel_count), 0) * device_count + me
    chosen = (lax.broadcasted_iota(jnp.int32, (8, channel_count), 1) == place).astype(F32).astype(BF16)
    first, second, third = waves_ref[0:1, :], waves_ref[1:2, :], waves_ref[2:3, :]
    sign = jnp.where(first < 0, 2, 0) + jnp.where(second < 0, 1, 0)
    key = sign * rows + jnp.abs(first) * HARMONICS + jnp.abs(second)
    spots = lax.broadcasted_iota(jnp.int32, (4 * rows, wave_count), 0) == key
    onehot = jnp.where(spots, 1.0, 0.0).astype(BF16)
    height = lax.broadcasted_iota(jnp.int32, (HARMONICS, wave_count), 0) // own_channels + 1
    here = [height + tile * together == third for tile in range(tiles)]
    rest = gain_ref[...]
    summed = 0.0
    for _ in range(3):
        part = rest.astype(BF16)
        rest = rest - part.astype(F32)
        mine = dot(chosen, part, 1, 1)
        mine = jnp.concatenate([mine[:own_channels]] * together, axis=0)
        wide = jnp.concatenate([jnp.where(spots, mine, 0.0) for spots in here], axis=0)
        summed = summed + dot(onehot, wide.astype(BF16), 1, 1)
    lane = lax.broadcasted_iota(jnp.int32, (8, channel_count), 1)
    wanted = jnp.minimum(lane % own_channels * device_count + me, channel_count - 1)
    amp = jnp.take_along_axis(jnp.broadcast_to(amp_ref[...], (8, channel_count)), wanted, axis=1)
    width = jnp.take_along_axis(
        jnp.broadcast_to(width_ref[...], (8, channel_count)), wanted, axis=1
    )
    amp, width = amp[0:1, :lanes], width[0:1, :lanes]
    k1, k2, k3 = grid_numbers(rows, lanes, own_channels, lengths)
    squared = k1 * k1 + k2 * k2 + k3 * k3
    base = amp * jnp.exp(-width * squared) * (1.0 / volume)
    for sign_id in range(4):
        phi_ref[sign_id] = base * summed[sign_id * rows : (sign_id + 1) * rows, :]
    width_out_ref[...] = jnp.broadcast_to(width, (8, lanes))


def grid_numbers(rows, lanes, own_channels, lengths):
    row_id = lax.broadcasted_iota(jnp.int32, (rows, lanes), 0)
    lane_id = lax.broadcasted_iota(jnp.int32, (rows, lanes), 1)
    k1 = (row_id // HARMONICS).astype(F32) * (2.0 * math.pi / lengths[0])
    k2 = (row_id % HARMONICS).astype(F32) * (2.0 * math.pi / lengths[1])
    k3 = (lane_id // own_channels + 1).astype(F32) * (2.0 * math.pi / lengths[2])
    return k1, k2, k3


def neighbour_of(step, row_count, col_count):
    row = lax.rem(lax.axis_index("row") + step[0] + row_count, row_count)
    col = lax.rem(lax.axis_index("col") + step[1] + col_count, col_count)
    return row * col_count + col


def slab_rows(slab, rows, atom_count):
    width = slab.shape[-1] // atom_count
    return [
        slab[row // width : row // width + 1, row % width * atom_count : (row % width + 1) * atom_count]
        for row in rows
    ]


def pack_kernel(counts, copied, positions_ref, species_ref, ghosts_ref, *refs):
    row_count, col_count = counts
    sources, (send_ref, *targets) = refs[:copied], refs[copied : 2 * copied + 1]
    positions, species, ghosts, first_sems, sems = refs[2 * copied + 1 :]
    firsts = ((positions_ref, positions), (species_ref, species), (ghosts_ref, ghosts))
    firsts = start_copies(firsts, first_sems)
    others = start_copies(tuple(zip(sources, targets)), sems)
    device_count = send_ref.shape[0]
    atom_count = species.shape[1]
    width = send_ref.shape[2] // atom_count
    slots, _ = direction_slots(row_count, col_count)
    for copy in firsts:
        copy.wait()
    rows = [positions[0], positions[1], positions[2], species[...].astype(F32)]
    for row, values in enumerate(rows):
        low = row % width * atom_count
        send_ref[:, row // width, low : low + atom_count] = jnp.broadcast_to(
            values, (device_count, atom_count)
        )
    for order, step in enumerate(DIRECTIONS):
        target = neighbour_of(step, row_count, col_count)
        row = 4 + slots[order]
        low = row % width * atom_count
        send_ref[target, row // width, low : low + atom_count] = ghosts[order, :].astype(F32)
    for copy in others:
        copy.wait()


def start_copies(pairs, sems):
    copies = [
        pltpu.make_async_copy(source, target, sems.at[spot])
        for spot, (source, target) in enumerate(pairs)
    ]
    for copy in copies:
        copy.start()
    return copies


def weights_kernel(dims, table_dims, upd_ref, mixed_ref, *refs):
    cells, refs = refs[: bool(table_dims)], refs[bool(table_dims) :]
    sources, (dupd_ref, back_ref, phi_ref, width_out_ref), refs = refs[:6], refs[6:10], refs[10:]
    axes, targets, sems = refs[: len(refs) - 7], refs[-7:-1], refs[-1]
    copies = start_copies(tuple(zip(sources, targets)), sems)
    if table_dims:
        table_kernel(table_dims, *cells, axes[0])
        if len(axes) > 1:
            wave_planes(axes[1], axes[0], range(axes[1].shape[1] // upd_ref.shape[1]))
    pooled_rows, channel_count = mixed_ref.shape
    radial_count = dims[5]
    order_id = lax.broadcasted_iota(jnp.int32, (pooled_rows, channel_count), 0) % radial_count
    factor = jnp.zeros((pooled_rows, channel_count), F32)
    for order in range(radial_count):
        factor = jnp.where(order_id == order, -2.0 * radial_rate(order), factor)
    back_ref[...] = mixed_ref[...] * factor
    for copy in copies[:2]:
        copy.wait()
    readout_gradient(upd_ref, targets[0], targets[1], dupd_ref)
    for copy in copies[2:]:
        copy.wait()
    wave_weights(dims[:5], *targets[2:], phi_ref, width_out_ref)


def short_forward_kernel(
    dims,
    cells_ref,
    counts_ref,
    ids_ref,
    radial_ref,
    embed_ref,
    mix_ref,
    send_ref,
    vec_ref,
    kind_ref,
    owner_ref,
    upd_ref,
    slope_ref,
    mixed_ref,
    table,
    lists,
    codes,
    pooled,
    weights,
    kinds8,
):
    own_channels, row_count, col_count = dims
    slot_count, atom_count = ids_ref.shape
    species_count, channel_count = embed_ref.shape
    radial_count = radial_ref.shape[0]
    device_count = send_ref.shape[0]
    slots, _ = direction_slots(row_count, col_count)
    for k in range(species_count):
        weights[k * radial_count : (k + 1) * radial_count, :] = (
            radial_ref[...] * embed_ref[k : k + 1, :] * (1.0 / slot_count)
        )
    weights[...] = dot(weights[...], mix_ref[...], 1, 0, GOOD)
    mixed_ref[...] = weights[...]
    own = slab_rows(cells_ref[neighbour_of((0, 0), row_count, col_count)], range(4), atom_count)
    domains, places = [], []
    for step in DIRECTIONS:
        key = (step[0] % row_count, step[1] % col_count)
        if key not in domains:
            domains.append(key)
        places.append(domains.index(key))
    for part in range(3):
        table[part, 0:1, :] = own[part]
    for place, key in enumerate(domains):
        block = slab_rows(cells_ref[neighbour_of(key, row_count, col_count)], range(3), atom_count)
        for part in range(3):
            table[part, 8 + place : 9 + place, :] = block[part]
    for order, step in enumerate(DIRECTIONS):
        list_row = 4 + slots[len(DIRECTIONS) - 1 - order]
        source = neighbour_of(step, row_count, col_count)
        kinds_row, list_values = slab_rows(cells_ref[source], (3, list_row), atom_count)
        table[3, 8 + order : 9 + order, :] = kinds_row
        lists[order : order + 1, :] = list_values.astype(jnp.int32)
    picks = lists[...]
    ghost_kinds = jnp.take_along_axis(table[3, 8:16, :], picks, axis=1)
    codes[8:16, :] = picks + atom_count * ghost_kinds.astype(jnp.int32)
    codes[0:1, :] = lax.broadcasted_iota(
        jnp.int32, (1, atom_count), 1
    ) + atom_count * own[3].astype(jnp.int32)

    ids = ids_ref[...]
    lane = ids & (atom_count - 1)
    source = ids // atom_count

    def picked(ref, index, marks):
        values = jnp.take_along_axis(jnp.broadcast_to(ref[0:1, :], ids.shape), index, axis=1)
        for place, mark in enumerate(marks):
            wide = jnp.broadcast_to(ref[8 + place : 9 + place, :], ids.shape)
            values = jnp.where(mark, jnp.take_along_axis(wide, index, axis=1), values)
        return values

    marks = [source == order + 1 for order in range(len(DIRECTIONS))]
    code = picked(codes, lane, marks)
    owner = code & (atom_count - 1)
    owner_ref[...] = owner + source * atom_count
    merged = []
    for place in range(len(domains)):
        mine = [mark for mark, other in zip(marks, places) if other == place]
        merged.append(functools.reduce(jnp.logical_or, mine))
    gathered = [picked(table.at[part], owner, merged) for part in range(3)]
    for axis in range(2):
        shift = jnp.zeros(ids.shape, F32)
        for mark, step in zip(marks, DIRECTIONS):
            if step[axis]:
                shift = jnp.where(mark, step[axis] * CELL_EDGE, shift)
        gathered[axis] = gathered[axis] + shift
    gathered.append((code // atom_count).astype(F32))
    slot = lax.broadcasted_iota(jnp.int32, ids.shape, 0)
    kind = jnp.where(slot < counts_ref[...], gathered[3], -1.0)
    kind_ref[...] = kind
    squared = jnp.zeros(ids.shape, F32)
    for part in range(3):
        vector = gathered[part] - own[part]
        vec_ref[part] = vector
        squared = squared + vector * vector
    masks = [kind == float(k) for k in range(species_count)]
    for order in range(radial_count):
        basis = jnp.exp(squared * (-radial_rate(order)))
        for k in range(species_count):
            spot = k * radial_count + order
            pooled[spot : spot + 1, :] = jnp.sum(
                jnp.where(masks[k], basis, 0.0), axis=0, keepdims=True
            )
    kinds8[...] = jnp.zeros_like(kinds8)
    kinds8[0:species_count, :] = embed_ref[...]
    own_hot = (
        lax.broadcasted_iota(jnp.int32, (kinds8.shape[0], atom_count), 0).astype(F32) == own[3]
    ).astype(F32)
    initial = dot(kinds8[...], own_hot, 0, 0, EXACT)
    before = dot(weights[...], pooled[...], 0, 0, GOOD)
    gate = 1.0 / (1.0 + jnp.exp(-before))
    updated = initial + before * gate
    slope_ref[...] = gate + before * gate * (1.0 - gate)
    for q in range(own_channels):
        low, high = q * device_count, min(channel_count, (q + 1) * device_count)
        send_ref[0 : high - low, q, :] = updated[low:high, :]
        if high - low < device_count:
            send_ref[high - low :, q, :] = jnp.zeros(
                (device_count - (high - low), atom_count), F32
            )
    upd_ref[...] = updated


def readout_gradient(upd_ref, read_ref, out_ref, dupd_ref):
    channel_count, atom_count = upd_ref.shape
    readout = dot(read_ref[...], upd_ref[...], 0, 0, GOOD)
    gate = 1.0 / (1.0 + jnp.exp(-readout))
    scale = jnp.broadcast_to(out_ref[...], (channel_count, channel_count)).T
    dread = scale[:, 0:atom_count] * (gate + readout * gate * (1.0 - gate))
    dupd_ref[...] = dot(read_ref[...], dread, 1, 0, GOOD)


def turn_tables(turns, multiples):
    angle = turns * multiples
    halves = jnp.floor(2.0 * angle + 0.5)
    rest = angle - 0.5 * halves
    sign = 1.0 - 2.0 * (halves - 2.0 * jnp.floor(0.5 * halves))
    square = rest * rest

    def series(first, last):
        terms = [
            (-1.0) ** (p // 2) * (2.0 * math.pi) ** p / math.factorial(p)
            for p in range(first, last + 1, 2)
        ]
        total = jnp.full_like(square, terms[-1])
        for term in reversed(terms[:-1]):
            total = total * square + term
        return total

    return sign * series(0, 12), sign * rest * series(1, 13)


def table_kernel(dims, cells_ref, axes_ref):
    col_count, chunk_count, lengths = dims
    chunk = cells_ref.shape[0]
    atom_count = axes_ref.shape[2] // chunk
    first_device = pl.program_id(0) * chunk if chunk_count > 1 else 0
    multiples = lax.broadcasted_iota(jnp.int32, (HARMONICS, atom_count), 0).astype(F32)

    def one(index, _):
        device = first_device + index
        spot = pl.ds(pl.multiple_of(index * atom_count, atom_count), atom_count)
        block = slab_rows(cells_ref[index], range(3), atom_count)
        corner_row = (device // col_count).astype(F32) * CELL_EDGE
        corner_col = (device % col_count).astype(F32) * CELL_EDGE
        turns = (
            (block[0] + corner_row) * (1.0 / lengths[0]),
            (block[1] + corner_col) * (1.0 / lengths[1]),
            block[2] * (1.0 / lengths[2]),
        )
        for axis in range(3):
            numbers = multiples + 1.0 if axis == 2 else multiples
            cos, sin = turn_tables(turns[axis], numbers)
            axes_ref[2 * axis, :, spot] = cos
            axes_ref[2 * axis + 1, :, spot] = sin
        return 0

    lax.fori_loop(0, chunk, one, 0, unroll=4)


def wave_kernel(dims, recv_ref, axes_ref, phi_ref, width_ref, *refs):
    own_channels, chunk_count, lengths, ready = dims
    made, (send_ref, push_ref, *planes), (heights, lifted, sums, coefficients) = refs[:ready], refs[ready:-4], refs[-4:]
    planes = (*made, *planes)
    parts = (planes, ready, axes_ref, heights, lifted)

    def back():
        wave_back(own_channels, lengths, planes, heights, lifted, coefficients, send_ref, push_ref)
        virial = wave_virial(own_channels, lengths, sums, phi_ref, width_ref, (1, push_ref.shape[2]))
        push_ref[:, 3, :] = jnp.broadcast_to(virial, (push_ref.shape[0], push_ref.shape[2]))

    if chunk_count == 1:
        sums[...] = wave_sums(own_channels, recv_ref, *parts)
        wave_coefficients(sums, phi_ref, coefficients)
        back()
        return
    phase, chunk_id = pl.program_id(0), pl.program_id(1)

    @pl.when((phase == 0) & (chunk_id == 0))
    def _():
        sums[...] = jnp.zeros_like(sums)

    part = wave_sums(own_channels, recv_ref, *parts)

    @pl.when(phase == 0)
    def _():
        sums[...] += part

    @pl.when((phase == 1) & (chunk_id == 0))
    def _():
        wave_coefficients(sums, phi_ref, coefficients)

    @pl.when(phase == 1)
    def _():
        back()


def wave_planes(planes_ref, axes_ref, devices):
    atom_count = planes_ref.shape[1] // len(devices)
    count = planes_ref.shape[0] // 2
    for place, index in enumerate(devices):
        spot = slice(index * atom_count, (index + 1) * atom_count)
        target = slice(place * atom_count, (place + 1) * atom_count)
        products = [
            axes_ref[first_axis, m : m + 1, spot] * axes_ref[second_axis, :, spot]
            for first_axis, second_axis in ((0, 2), (0, 3), (1, 2), (1, 3))
            for m in range(KMAX + 1)
        ]
        for pair in range(len(products) // 2):
            both = jnp.concatenate(products[2 * pair : 2 * pair + 2], axis=0)
            high = both.astype(BF16)
            rows = slice(2 * HARMONICS * pair, 2 * HARMONICS * (pair + 1))
            planes_ref[rows, target] = high
            rows = slice(count + rows.start, count + rows.stop)
            planes_ref[rows, target] = (both - high.astype(F32)).astype(BF16)


def wave_lift(own_channels, recv_ref, axes_ref, heights, lifted, devices):
    atom_count = recv_ref.shape[2]
    together, tiles = tile_layout(own_channels)
    lanes = tiles * HARMONICS
    sublane = lax.broadcasted_iota(jnp.int32, (HARMONICS, atom_count), 0)
    for index in devices:
        spot = slice(index * atom_count, (index + 1) * atom_count)
        feature = jnp.concatenate([recv_ref[index, 0:own_channels, :]] * together, axis=0)
        for part in range(2):
            for tile in range(tiles):
                first = tile * together
                height = jnp.broadcast_to(axes_ref[4 + part, first : first + 1, spot], sublane.shape)
                for n in range(1, together):
                    height = jnp.where(
                        sublane >= n * own_channels, axes_ref[4 + part, first + n : first + n + 1, spot], height
                    )
                row = part * lanes + tile * HARMONICS
                heights[row : row + HARMONICS, spot] = height
                lifted[row : row + HARMONICS, spot] = feature * height


def plane_groups(chunk, planes):
    each = chunk // len(planes)
    return [(ref, range(place * each, (place + 1) * each)) for place, ref in enumerate(planes)]


def wave_sums(own_channels, recv_ref, planes, ready, axes_ref, heights, lifted):
    chunk, _, atom_count = recv_ref.shape
    lanes = lifted.shape[0] // 2
    total = 0.0
    for place, (ref, devices) in enumerate(plane_groups(chunk, planes)):
        wave_lift(own_channels, recv_ref, axes_ref, heights, lifted, devices)
        if place >= ready:
            wave_planes(ref, axes_ref, devices)
        count = ref.shape[0] // 2
        values = lifted[:, devices[0] * atom_count : (devices[-1] + 1) * atom_count]
        high = values.astype(BF16)
        low = (values - high.astype(F32)).astype(BF16)
        main = dot(ref[0:count, :], jnp.concatenate([high, low], axis=0), 1, 1)
        total = total + main[:, : 2 * lanes] + (main[:, 2 * lanes :] + dot(ref[count:, :], high, 1, 1))
    return total


SIGNS = ((1.0, 1.0), (1.0, -1.0), (-1.0, 1.0), (-1.0, -1.0))


def wave_blocks(sums_ref, phi_ref):
    _, rows, lanes = phi_ref.shape
    sums = sums_ref[...]
    cos_part, sin_part = sums[:, :lanes], sums[:, lanes:]
    cc_c, cs_c, sc_c, ss_c = (cos_part[p * rows : (p + 1) * rows] for p in range(4))
    cc_s, cs_s, sc_s, ss_s = (sin_part[p * rows : (p + 1) * rows] for p in range(4))
    for sign_id, (s1, s2) in enumerate(SIGNS):
        real = cc_c - s1 * s2 * ss_c - s1 * sc_s - s2 * cs_s
        imag = cc_s - s1 * s2 * ss_s + s1 * sc_c + s2 * cs_c
        phi = phi_ref[sign_id]
        yield s1, s2, phi * real, phi * imag, real, imag


def wave_virial(own_channels, lengths, sums_ref, phi_ref, width_ref, shape):
    _, rows, lanes = phi_ref.shape
    even = first_odd = second_odd = both_odd = jnp.zeros((rows, lanes), F32)
    for s1, s2, dreal, dimag, real, imag in wave_blocks(sums_ref, phi_ref):
        power = dreal * real + dimag * imag
        even = even + power
        first_odd = first_odd + s1 * power
        second_odd = second_odd + s2 * power
        both_odd = both_odd + s1 * s2 * power
    width = width_ref[0:1, :]
    k1, k2, k3 = grid_numbers(rows, lanes, own_channels, lengths)

    def total_of(values):
        return jnp.sum(jnp.sum(values, axis=0, keepdims=True), axis=1, keepdims=True)

    energy = 0.5 * total_of(even)
    scaled = width * even
    terms = {
        (0, 0): energy - total_of(k1 * k1 * scaled),
        (1, 1): energy - total_of(k2 * k2 * scaled),
        (2, 2): energy - total_of(k3 * k3 * scaled),
        (0, 1): -total_of(k1 * k2 * width * both_odd),
        (0, 2): -total_of(k1 * k3 * width * first_odd),
        (1, 2): -total_of(k2 * k3 * width * second_odd),
    }
    return virial_row(terms, shape)


def wave_coefficients(sums_ref, phi_ref, coefficients_ref):
    _, rows, lanes = phi_ref.shape
    zero = jnp.zeros((rows, lanes), F32)
    d_cc_c = d_cc_s = d_cs_c = d_cs_s = d_sc_c = d_sc_s = d_ss_c = d_ss_s = zero
    for s1, s2, dreal, dimag, _, _ in wave_blocks(sums_ref, phi_ref):
        d_cc_c, d_ss_c = d_cc_c + dreal, d_ss_c - s1 * s2 * dreal
        d_sc_s, d_cs_s = d_sc_s - s1 * dreal, d_cs_s - s2 * dreal
        d_cc_s, d_ss_s = d_cc_s + dimag, d_ss_s - s1 * s2 * dimag
        d_sc_c, d_cs_c = d_sc_c + s1 * dimag, d_cs_c + s2 * dimag
    values = jnp.concatenate(
        [
            jnp.concatenate(pair, axis=1)
            for pair in ((d_cc_c, d_cc_s), (d_cs_c, d_cs_s), (d_sc_c, d_sc_s), (d_ss_c, d_ss_s))
        ],
        axis=0,
    )
    cc, cs, sc, ss = (values[p * rows : (p + 1) * rows] for p in range(4))
    row_id = lax.broadcasted_iota(jnp.int32, (rows, 2 * lanes), 0)
    m1 = (row_id // HARMONICS).astype(F32)
    m2 = (row_id % HARMONICS).astype(F32)
    along_x = jnp.concatenate([m1 * sc, m1 * ss, -m1 * cc, -m1 * cs], axis=0)
    along_y = jnp.concatenate([m2 * cs, -m2 * cc, m2 * ss, -m2 * sc], axis=0)
    values = jnp.concatenate([values, along_x, along_y], axis=1)
    turned = values.T
    high = turned.astype(BF16)
    count = turned.shape[0]
    coefficients_ref[0:count, :] = high
    coefficients_ref[count:, :] = (turned - high.astype(F32)).astype(BF16)


def wave_spread(planes_ref, coefficients):
    values = coefficients[...]
    count = values.shape[0] // 2
    both = jnp.concatenate([values[:count], values[:count]], axis=1)
    return dot(both, planes_ref[...], 1, 0) + dot(values[count:], planes_ref[0 : values.shape[1], :], 1, 0)


def wave_back(own_channels, lengths, planes, heights, lifted, coefficients, send_ref, push_ref):
    chunk, _, atom_count = push_ref.shape
    together, tiles = tile_layout(own_channels)
    lanes = tiles * HARMONICS
    sublane = lax.broadcasted_iota(jnp.int32, (HARMONICS, atom_count), 0)
    numbers = [(sublane // own_channels + 1 + tile * together).astype(F32) for tile in range(tiles)]
    spread = []
    for ref, devices in plane_groups(chunk, planes):
        result = wave_spread(ref, coefficients)
        spread += [(result, place, index) for place, index in enumerate(devices)]
    for result, place, index in spread:
        spot = slice(index * atom_count, (index + 1) * atom_count)
        part = result[:, place * atom_count : (place + 1) * atom_count]
        feature = grad_x = grad_y = grad_z = jnp.zeros((HARMONICS, atom_count), F32)
        for tile in range(tiles):
            a, b = tile * HARMONICS, lanes + tile * HARMONICS
            on_cos, on_sin = part[a : a + HARMONICS], part[b : b + HARMONICS]
            feature = feature + on_cos * heights[a : a + HARMONICS, spot] + on_sin * heights[b : b + HARMONICS, spot]
            lift_cos = lifted[a : a + HARMONICS, spot]
            lift_sin = lifted[b : b + HARMONICS, spot]
            grad_z = grad_z + numbers[tile] * (on_sin * lift_cos - on_cos * lift_sin)
            a, b = a + 2 * lanes, b + 2 * lanes
            grad_x = grad_x + part[a : a + HARMONICS] * lift_cos + part[b : b + HARMONICS] * lift_sin
            a, b = a + 2 * lanes, b + 2 * lanes
            grad_y = grad_y + part[a : a + HARMONICS] * lift_cos + part[b : b + HARMONICS] * lift_sin
        total = feature[0:own_channels]
        for n in range(1, together):
            total = total + feature[n * own_channels : (n + 1) * own_channels]
        send_ref[index, 0:own_channels, :] = total
        pieces = (
            grad_x * (2.0 * math.pi / lengths[0]),
            grad_y * (2.0 * math.pi / lengths[1]),
            grad_z * (2.0 * math.pi / lengths[2]),
        )
        first, second, third = (piece + pltpu.roll(piece, HARMONICS // 2, 0) for piece in pieces)
        first = jnp.where(sublane < HARMONICS // 2, first, second)
        first = first + pltpu.roll(first, 2, 0)
        third = third + pltpu.roll(third, 2, 0)
        first = jnp.where(sublane % 4 >= 2, first, third)
        first = first + pltpu.roll(first, 1, 0)
        for row, place in enumerate((3, 7, 1)):
            push_ref[index, row : row + 1, :] = first[place : place + 1]


def virial_row(terms, shape):
    lane = lax.broadcasted_iota(jnp.int32, shape, 1)
    row = jnp.zeros(shape, F32)
    for (i, j), value in terms.items():
        spots = (lane == 3 * i + j) | (lane == 3 * j + i)
        row = jnp.where(spots, value, row)
    return row


def short_back_kernel(
    dims,
    recv_ref,
    vec_ref,
    kind_ref,
    dupd_ref,
    slope_ref,
    owner_ref,
    back_ref,
    push_ref,
    send_ref,
    fgrad,
    dpool,
    parts,
):
    own_channels, row_count, col_count, species_count, radial_count = dims
    slot_count, atom_count = owner_ref.shape
    channel_count = back_ref.shape[1]
    device_count = send_ref.shape[0]
    table_rows = round_up(len(DIRECTIONS) + 1, 16)
    for q in range(own_channels):
        low, high = q * device_count, min(channel_count, (q + 1) * device_count)
        fgrad[low:high, :] = recv_ref[0 : high - low, q, :]
    dbefore = (fgrad[...] + dupd_ref[...]) * slope_ref[...]
    dpool[...] = dot(back_ref[...], dbefore, 1, 0, GOOD)
    vectors = [vec_ref[part] for part in range(3)]
    squared = vectors[0] * vectors[0] + vectors[1] * vectors[1] + vectors[2] * vectors[2]
    kind = kind_ref[...]
    sums = [jnp.zeros(kind.shape, F32) for _ in range(species_count)]
    for order in range(radial_count):
        basis = jnp.exp(squared * (-radial_rate(order)))
        for k in range(species_count):
            spot = k * radial_count + order
            sums[k] = sums[k] + basis * dpool[spot : spot + 1, :]
    slope = jnp.zeros(kind.shape, F32)
    for k in range(species_count):
        slope = jnp.where(kind == float(k), sums[k], slope)
    grads = [slope * vector for vector in vectors]

    def total_of(values):
        return jnp.sum(jnp.sum(values, axis=0, keepdims=True), axis=1, keepdims=True)

    terms = {
        (i, j): -total_of(grads[i] * vectors[j]) for i in range(3) for j in range(i, 3)
    }
    virial = virial_row(terms, (1, atom_count))
    for part in range(3):
        parts[2 * part], parts[2 * part + 1] = split(grads[part])

    sublane = lax.broadcasted_iota(jnp.int32, (atom_count, atom_count), 0)
    table_id = lax.broadcasted_iota(jnp.int32, (table_rows, atom_count), 0)
    group = 8
    scattered = jnp.zeros((atom_count, 6 * table_rows), F32)
    for low in range(0, slot_count, group):
        hots, columns = [], []
        for s in range(low, low + group):
            ids = owner_ref[s : s + 1, :]
            hots.append(jnp.where(sublane == (ids & (atom_count - 1)), 1.0, 0.0).astype(BF16))
            mine = table_id == ids // atom_count
            columns.append(
                jnp.concatenate(
                    [
                        jnp.where(mine, parts[p, s : s + 1, :], 0.0).astype(BF16)
                        for p in range(6)
                    ],
                    axis=0,
                )
            )
        scattered = scattered + dot(
            jnp.concatenate(hots, axis=1), jnp.concatenate(columns, axis=1), 1, 1
        )
    rows = scattered.T
    send_ref[...] = push_ref[...]
    send_ref[:, 3, :] += jnp.broadcast_to(virial, (device_count, atom_count))
    me = neighbour_of((0, 0), row_count, col_count)
    for part in range(3):
        low = 2 * part * table_rows
        both = rows[low : low + table_rows] + rows[low + table_rows : low + 2 * table_rows]
        send_ref[me, part, :] += both[0, :] - jnp.sum(grads[part], axis=0)
        for order, step in enumerate(DIRECTIONS):
            target = neighbour_of(step, row_count, col_count)
            send_ref[target, part, :] += both[1 + order, :]


def final_kernel(volume, recv_ref, forces_ref, virial_ref):
    total = jnp.sum(recv_ref[...], axis=0)
    for part in range(3):
        forces_ref[part] = -total[part : part + 1, :]
    virial = total[3:4, :] * (1.0 / volume)
    for i in range(3):
        virial_ref[i : i + 1, :] = virial[:, 3 * i : 3 * i + 3]


def per_device(
    positions,
    species,
    counts,
    neighbours,
    ghost_index,
    wave_numbers,
    embedding,
    w_radial,
    w_mix,
    w_read,
    w_out,
    amplitude,
    kernel_width,
    filter_gain,
):
    row_count = lax.axis_size("row")
    col_count = lax.axis_size("col")
    device_count = row_count * col_count
    atom_count = positions.shape[3]
    slot_count = neighbours.shape[2]
    direction_count, ghost_count = ghost_index.shape[2:]
    species_count, channel_count = embedding.shape
    radial_count = w_radial.shape[0]
    own_channels = -(-channel_count // device_count)
    lengths = (CELL_EDGE * row_count, CELL_EDGE * col_count, HEIGHT)
    volume = lengths[0] * lengths[1] * lengths[2]
    rows = (KMAX + 1) * HARMONICS
    lanes = tile_layout(own_channels)[1] * HARMONICS
    _, shared = direction_slots(row_count, col_count)
    slab_first = round_up(4 + shared, 2) // 2 * atom_count
    slab_features = round_up(own_channels, 4)
    chunk = math.gcd(device_count, 32)
    chunk_count = device_count // chunk

    def exchange(slabs):
        return lax.all_to_all(slabs, AXES, 0, 0, tiled=True)

    def shape(*dims):
        return jax.ShapeDtypeStruct(dims, F32)

    def scratch(*dims):
        return pltpu.VMEM(dims, F32)

    def call(kernel, out_shape, vmem=16, **options):
        return pl.pallas_call(
            kernel,
            out_shape=out_shape,
            compiler_params=pltpu.CompilerParams(vmem_limit_bytes=vmem * 1024 * 1024),
            **options,
        )

    ids = neighbours.reshape(slot_count, atom_count)
    ghosts = ghost_index.reshape(direction_count, ghost_count)
    mesh_counts = (row_count, col_count)
    inputs = (
        counts.reshape(1, atom_count),
        ids,
        w_radial,
        embedding,
        w_mix,
    )
    wave_inputs = (
        w_read,
        w_out.reshape(1, -1),
        filter_gain,
        wave_numbers,
        amplitude.reshape(1, -1),
        kernel_width.reshape(1, -1),
    )

    def fetched(*arrays):
        return [pltpu.with_memory_space_constraint(x, pltpu.HBM) for x in arrays]

    kept = pl.BlockSpec(memory_space=pltpu.HBM)
    near = pl.BlockSpec(memory_space=pltpu.VMEM)
    send, *inputs = call(
        functools.partial(pack_kernel, mesh_counts, len(inputs)),
        (shape(device_count, 2, slab_first),)
        + tuple(jax.ShapeDtypeStruct(x.shape, x.dtype) for x in inputs),
        in_specs=[kept] * (3 + len(inputs)),
        scratch_shapes=[
            scratch(3, 1, atom_count),
            pltpu.VMEM((1, atom_count), jnp.int32),
            pltpu.VMEM(ghosts.shape, jnp.int32),
            pltpu.SemaphoreType.DMA((3,)),
            pltpu.SemaphoreType.DMA((len(inputs),)),
        ],
        name="pack",
    )(*fetched(positions.reshape(3, 1, atom_count), species.reshape(1, atom_count), ghosts, *inputs))
    live, ids, w_radial, embedding, w_mix = inputs
    cells = exchange(send)

    pooled_rows = species_count * radial_count
    send, vectors, kinds, owners, updated, slope, mixed = call(
        functools.partial(short_forward_kernel, (own_channels,) + mesh_counts),
        (
            shape(device_count, slab_features, atom_count),
            shape(3, slot_count, atom_count),
            shape(slot_count, atom_count),
            jax.ShapeDtypeStruct((slot_count, atom_count), jnp.int32),
            shape(channel_count, atom_count),
            shape(channel_count, atom_count),
            shape(pooled_rows, channel_count),
        ),
        scratch_shapes=[
            scratch(4, 16, atom_count),
            pltpu.VMEM((direction_count, atom_count), jnp.int32),
            pltpu.VMEM((16, atom_count), jnp.int32),
            scratch(pooled_rows, atom_count),
            scratch(pooled_rows, channel_count),
            scratch(round_up(species_count, 8), channel_count),
        ],
        name="short_forward",
    )(cells, live, ids, w_radial, embedding, w_mix)
    send, cells, updated, mixed = lax.optimization_barrier((send, cells, updated, mixed))
    features = exchange(send)

    axes_block = (6, HARMONICS, chunk * atom_count)
    ready = int(chunk_count == 1 and chunk % 2 == 0)
    axes_shape = shape(6, HARMONICS, device_count * atom_count)
    table_dims = (col_count, chunk_count, lengths)
    cells_inputs, axes_outputs = (), ()
    if chunk_count == 1:
        cells_inputs, axes_outputs = (cells,), (axes_shape,)
        if ready:
            axes_outputs += (jax.ShapeDtypeStruct((8 * rows, chunk // 2 * atom_count), BF16),)
    dupd, back, phi, width, *axes = call(
        functools.partial(
            weights_kernel,
            (device_count, channel_count, own_channels, lengths, volume, radial_count),
            table_dims if chunk_count == 1 else None,
        ),
        (
            shape(channel_count, atom_count),
            shape(pooled_rows, channel_count),
            shape(4, rows, lanes),
            shape(8, lanes),
        )
        + axes_outputs,
        in_specs=[near] * (2 + len(cells_inputs)) + [kept] * len(wave_inputs),
        scratch_shapes=[pltpu.VMEM(x.shape, x.dtype) for x in wave_inputs]
        + [pltpu.SemaphoreType.DMA((len(wave_inputs),))],
        cost_estimate=pl.CostEstimate(
            flops=2 * 4 * rows * filter_gain.shape[0] * 3 * lanes,
            bytes_accessed=4 * filter_gain.size,
            transcendentals=0,
        ),
        name="weights",
    )(updated, mixed, *cells_inputs, *fetched(*wave_inputs))
    if chunk_count > 1:
        axes = [
            call(
                functools.partial(table_kernel, table_dims),
                axes_shape,
                grid=(chunk_count,),
                in_specs=[pl.BlockSpec((chunk, 2, slab_first), lambda i: (i, 0, 0))],
                out_specs=pl.BlockSpec(axes_block, lambda i: (0, 0, i)),
                name="tables",
            )(cells)
        ]
    features, dupd, back = lax.optimization_barrier((features, dupd, back))

    plane = pltpu.VMEM((8 * rows, chunk // (1 + ready) * atom_count), BF16)
    wave_scratch = [plane] + [scratch(2 * lanes, chunk * atom_count)] * 2
    features_block = (chunk, slab_features, atom_count)
    wave_options = {}
    if chunk_count > 1:
        wave_options = dict(
            grid=(2, chunk_count),
            in_specs=[
                pl.BlockSpec(features_block, lambda p, i: (i, 0, 0)),
                pl.BlockSpec(axes_block, lambda p, i: (0, 0, i)),
                pl.BlockSpec((4, rows, lanes), lambda p, i: (0, 0, 0)),
                pl.BlockSpec((8, lanes), lambda p, i: (0, 0)),
            ],
            out_specs=(
                pl.BlockSpec(features_block, lambda p, i: (i * p, 0, 0)),
                pl.BlockSpec((chunk, 4, atom_count), lambda p, i: (i * p, 0, 0)),
            ),
        )
    send, push = call(
        functools.partial(wave_kernel, (own_channels, chunk_count, lengths, ready)),
        (shape(device_count, slab_features, atom_count), shape(device_count, 4, atom_count)),
        vmem=32,
        scratch_shapes=wave_scratch
        + [scratch(4 * rows, 2 * lanes), pltpu.VMEM((12 * lanes, 4 * rows), BF16)],
        name="waves",
        **wave_options,
    )(features, axes[0], phi, width, *axes[1:])
    gradients = exchange(send)

    send = call(
        functools.partial(
            short_back_kernel, (own_channels,) + mesh_counts + (species_count, radial_count)
        ),
        shape(device_count, 4, atom_count),
        scratch_shapes=[
            scratch(channel_count, atom_count),
            scratch(pooled_rows, atom_count),
            scratch(6, slot_count, atom_count),
        ],
        name="short_back",
    )(gradients, vectors, kinds, dupd, slope, owners, back, push)
    returned = exchange(send)

    forces, virial = call(
        functools.partial(final_kernel, volume),
        (shape(3, 1, atom_count), shape(3, 3)),
        name="total",
    )(returned)
    return (forces[:, None], virial)


def solution(mesh):
    return jax.shard_map(
        per_device,
        mesh=mesh,
        in_specs=(
            P(None, "row", "col", None),
            P("row", "col", None),
            P("row", "col", None),
            P("row", "col", None, None),
            P("row", "col", None, None),
            P(),
            P(),
            P(),
            P(),
            P(),
            P(),
            P(),
            P(),
            P(),
        ),
        out_specs=(P(None, "row", "col", None), P()),
        check_vma=False,
    )
```
